512 devices in a mesh: lat: 8 (over z_hi, y), lon: 64 (over z_lo, x, core).
Axes of the slice: x: 4, y: 4, z: 16 (z_hi: 2, z_lo: 8; z = z_hi * 8 + z_lo), core: 2. Of those that a mesh axis runs over, the one named last changes fastest.
Arguments:
- tokens: bfloat16 [1, 4, 96, 384, 192], P(None, None, 'lat', 'lon'), may hold values from -6 to 6
- fine_gain: float32 [192], replicated, may hold values from 0.25 to 1.75
- fine_shift: float32 [192], replicated, may hold values from -3 to 3
- fine_qkv: bfloat16 [192, 576], replicated, may hold values from -0.4375 to 0.4375
- fine_qkv_bias: float32 [576], replicated, may hold values from -8 to 8
- fine_proj: bfloat16 [192, 192], replicated, may hold values from -0.4375 to 0.4375
- fine_proj_bias: float32 [192], replicated, may hold values from -3 to 3
- fine_table: bfloat16 [16, 39744], P('lat'), may hold values from -5 to 305
- merge_gain: float32 [768], replicated, may hold values from 0.25 to 1.75
- merge_shift: float32 [768], replicated, may hold values from -3 to 3
- merge_weight: bfloat16 [768, 384], replicated, may hold values from -0.21875 to 0.21875
- coarse_gain: float32 [384], replicated, may hold values from 0.25 to 1.75
- coarse_shift: float32 [384], replicated, may hold values from -3 to 3
- coarse_qkv: bfloat16 [384, 1152], replicated, may hold values from -0.3125 to 0.3125
- coarse_qkv_bias: float32 [1152], replicated, may hold values from -8 to 8
- coarse_proj: bfloat16 [384, 384], replicated, may hold values from -0.3125 to 0.3125
- coarse_proj_bias: float32 [384], replicated, may hold values from -3 to 3
- coarse_table: bfloat16 [16, 39744], P('lat'), may hold values from -5 to 305
- cotangent: bfloat16 [1, 4, 48, 192, 384], P(None, None, 'lat', 'lon'), may hold values from -6 to 6
Outputs:
- coarse_out: bfloat16 [1, 4, 48, 192, 384], P(None, None, 'lat', 'lon')
- token_grad: bfloat16 [1, 4, 96, 384, 192], P(None, None, 'lat', 'lon')
- param_grads: float32 [1037184], P('lon')
- fine_table_grad: float32 [16, 39744], P('lat')
- coarse_table_grad: float32 [16, 39744], P('lat')
The draws below stay inside these ranges and needn't reach their ends.
All inputs are finite; a program needn't handle non-finite values.
Results may differ from the reference program's by a relative error of at most 0.035.
Values may be sent and summed in bfloat16 or wider, within the bound.
A program may use at most 128 MiB of HBM per device.

```python
import math
import jax
import jax.numpy as jnp
from jax import lax

SAMPLES = 1
LEVELS = 4
WZ = 2
WLAT = 6
WLON = 12
HEAD = 32
C_F = 192
HEADS_F = 6
C_C = 384
HEADS_C = 12
NLAT = 96
NLON = 384
ZWIN = 2
POS = 3312
POSH = 1656


def draw_fine_qkv_bias(key, part):
    key = jax.random.fold_in(key, 5)
    shared_key = jax.random.fold_in(key, 1)
    return jnp.clip(0.5 * jax.random.normal(shared_key, (3 * C_F,), jnp.float32), -3.0, 3.0)


def draw_coarse_qkv_bias(key, part):
    key = jax.random.fold_in(key, 9)
    shared_key = jax.random.fold_in(key, 1)
    return jnp.clip(0.5 * jax.random.normal(shared_key, (3 * C_C,), jnp.float32), -3.0, 3.0)


def table_values(key, rows, groups, entries):
    noise_key = jax.random.fold_in(key, 0)
    base = jnp.clip(jax.random.normal(noise_key, (rows, groups * entries), jnp.float32), -5.0, 5.0)
    return base


def draw_fine_table(key, part):
    key = jax.random.fold_in(key, 13)
    return table_values(key, NLAT // WLAT, ZWIN * HEADS_F, POS).astype(jnp.bfloat16)


def draw_coarse_table(key, part):
    key = jax.random.fold_in(key, 17)
    return table_values(key, NLAT // WLAT, ZWIN * HEADS_C, POSH).astype(jnp.bfloat16)


def block_scale(own_key, extent, cuts, low, high):
    level = 1.0
    for axis_at, parts in cuts:
        heights = jax.random.uniform(jax.random.fold_in(jax.random.fold_in(own_key, 6), axis_at), (parts,), jnp.float32, low / len(cuts), high / len(cuts))
        level = level * jnp.repeat(jnp.exp(heights), extent[axis_at] // parts).reshape((-1,) + (1,) * (len(extent) - 1 - axis_at))
    return level


def scatter_about(own_key, shape, scale, reach, shards=(), held_as=jnp.bfloat16):
    values = jax.random.normal(own_key, shape, jnp.float32) * scale
    if len(shards) > 0:
        values = block_scale(own_key, shape, shards, -0.22, 0.18) * values
    return jnp.clip(values, min=-reach, max=reach).astype(held_as)


def setup_inputs(seed: int = 0) -> dict:
    seeds = jax.random.split(jax.random.key(seed), 20)
    tokens = scatter_about(seeds[0], (SAMPLES, LEVELS, NLAT, NLON, C_F), 1.0, 6.0, ((2, 8), (3, 64)))
    fine_gain = jnp.clip(1.0 + 0.15 * jax.random.normal(seeds[1], (C_F,), jnp.float32), 0.25, 1.75)
    fine_shift = scatter_about(seeds[2], (C_F,), 0.5, 3.0, (), jnp.float32)
    fine_qkv = scatter_about(seeds[3], (C_F, 3 * C_F), C_F ** -0.5, 0.4375)
    fine_qkv_bias = draw_fine_qkv_bias(jax.random.fold_in(seeds[19], 71), 0)
    fine_proj = scatter_about(seeds[5], (C_F, C_F), C_F ** -0.5, 0.4375)
    fine_proj_bias = scatter_about(seeds[6], (C_F,), 0.5, 3.0, (), jnp.float32)
    fine_table = draw_fine_table(jax.random.fold_in(seeds[19], 71), 0)
    merge_gain = jnp.clip(1.0 + 0.15 * jax.random.normal(seeds[8], (4 * C_F,), jnp.float32), 0.25, 1.75)
    merge_shift = scatter_about(seeds[9], (4 * C_F,), 0.5, 3.0, (), jnp.float32)
    merge_weight = scatter_about(seeds[10], (4 * C_F, C_C), (4 * C_F) ** -0.5, 0.21875)
    coarse_gain = jnp.clip(1.0 + 0.15 * jax.random.normal(seeds[11], (C_C,), jnp.float32), 0.25, 1.75)
    coarse_shift = scatter_about(seeds[12], (C_C,), 0.5, 3.0, (), jnp.float32)
    coarse_qkv = scatter_about(seeds[13], (C_C, 3 * C_C), C_C ** -0.5, 0.3125)
    coarse_qkv_bias = draw_coarse_qkv_bias(jax.random.fold_in(seeds[19], 71), 0)
    coarse_proj = scatter_about(seeds[15], (C_C, C_C), C_C ** -0.5, 0.3125)
    coarse_proj_bias = scatter_about(seeds[16], (C_C,), 0.5, 3.0, (), jnp.float32)
    coarse_table = draw_coarse_table(jax.random.fold_in(seeds[19], 71), 0)
    cotangent = scatter_about(seeds[18], (SAMPLES, LEVELS, NLAT // 2, NLON // 2, C_C), 1.0, 6.0, ((2, 8), (3, 64)))
    return dict(tokens=tokens, fine_gain=fine_gain, fine_shift=fine_shift, fine_qkv=fine_qkv, fine_qkv_bias=fine_qkv_bias, fine_proj=fine_proj, fine_proj_bias=fine_proj_bias, fine_table=fine_table, merge_gain=merge_gain, merge_shift=merge_shift, merge_weight=merge_weight, coarse_gain=coarse_gain, coarse_shift=coarse_shift, coarse_qkv=coarse_qkv, coarse_qkv_bias=coarse_qkv_bias, coarse_proj=coarse_proj, coarse_proj_bias=coarse_proj_bias, coarse_table=coarse_table, cotangent=cotangent)


EPS = 1e-05
NEGATIVE = -1e+30

def layer_norm(volume, scaling, offset):
    centre = volume - lax.optimization_barrier(jnp.mean(volume, -1, keepdims=True))
    spread = lax.optimization_barrier(jnp.mean(centre * centre, -1, keepdims=True))
    return centre * lax.rsqrt(spread + EPS) * scaling + offset

def coordinates(depth, height, breadth):
    flattened = jnp.arange(depth * height * breadth, dtype=jnp.int32)
    return (flattened // (height * breadth), flattened // breadth % height, flattened % breadth)

def relative_index(level_query, lat_query, lon_query, level_key, lat_key, lon_key, lat_span):
    return (((level_query * WZ + level_key) * lat_span + lat_query) * WLAT + lat_key) * (2 * WLON - 1) + lon_query - lon_key + WLON - 1

def to_windows(volume):
    samples, levels, lat_rows, lon_cols, channels = volume.shape
    shaped = volume.reshape(samples, levels // WZ, WZ, lat_rows // WLAT, WLAT, lon_cols // WLON, WLON, channels)
    shaped = shaped.transpose(3, 5, 0, 1, 2, 4, 6, 7)
    return shaped.reshape(lat_rows // WLAT * (lon_cols // WLON), samples, levels // WZ, WZ * WLAT * WLON, channels)

def from_windows(windows, lat_rows, lon_cols):
    samples = windows.shape[1]
    zones = windows.shape[2]
    channels = windows.shape[4]
    shaped = windows.reshape(lat_rows // WLAT, lon_cols // WLON, samples, zones, WZ, WLAT, WLON, channels)
    shaped = shaped.transpose(2, 3, 4, 0, 5, 1, 6, 7)
    return shaped.reshape(samples, zones * WZ, lat_rows, lon_cols, channels)

def attend(queries, key_vectors, values, bias_terms, allowed):
    factor = HEAD ** (-0.5)
    scores = jnp.einsum('...qhd,...khd->...hqk', queries.astype(jnp.float32), key_vectors.astype(jnp.float32)) * factor + bias_terms
    scores = jnp.where(allowed, scores, NEGATIVE)
    maximum = lax.optimization_barrier(jnp.max(scores, -1, keepdims=True))
    weights = jnp.exp(scores - maximum)
    probability = weights / lax.optimization_barrier(jnp.sum(weights, -1, keepdims=True))
    narrow = lax.optimization_barrier(probability.astype(jnp.bfloat16))
    mixture = jnp.einsum('...hqk,...khd->...qhd', narrow.astype(jnp.float32), values.astype(jnp.float32))
    return (probability, narrow, mixture.astype(jnp.bfloat16))

def attend_back(queries, key_vectors, values, probability, narrow, mixture_grad):
    factor = HEAD ** (-0.5)
    grad_wide = mixture_grad.astype(jnp.float32)
    value_grad = jnp.einsum('...hqk,...qhd->...khd', narrow.astype(jnp.float32), grad_wide)
    prob_grad = jnp.einsum('...qhd,...khd->...hqk', grad_wide, values.astype(jnp.float32))
    score_grad = probability * (prob_grad - lax.optimization_barrier(jnp.sum(prob_grad * probability, -1, keepdims=True)))
    score_narrow = lax.optimization_barrier(score_grad.astype(jnp.bfloat16)).astype(jnp.float32)
    query_grad = jnp.einsum('...hqk,...khd->...qhd', score_narrow, key_vectors.astype(jnp.float32)) * factor
    key_grad = jnp.einsum('...hqk,...qhd->...khd', score_narrow, queries.astype(jnp.float32)) * factor
    return (query_grad, key_grad, value_grad, score_grad)

def coarse_full(table):
    types = table.shape[0] // 2
    shaped = table.reshape(types, 2, ZWIN, HEADS_C, WZ, WZ, WLAT // 2, WLAT, 2 * WLON - 1)
    shaped = shaped.transpose(0, 2, 3, 4, 5, 1, 6, 7, 8)
    return shaped.reshape(types, ZWIN, HEADS_C, POS)

def coarse_split(table_grad):
    types = table_grad.shape[0]
    shaped = table_grad.reshape(types, ZWIN, HEADS_C, WZ, WZ, 2, WLAT // 2, WLAT, 2 * WLON - 1)
    shaped = shaped.transpose(0, 5, 1, 2, 3, 4, 6, 7, 8)
    return shaped.reshape(types * 2, ZWIN * HEADS_C * POSH)

def split_heads(qkv_out, channels, heads):
    lead = qkv_out.shape[:-1]
    queries = qkv_out[..., :channels].reshape(lead + (heads, HEAD))
    key_vectors = qkv_out[..., channels:2 * channels].reshape(lead + (heads, HEAD))
    values = qkv_out[..., 2 * channels:].reshape(lead + (heads, HEAD))
    return (queries, key_vectors, values)

def reference(tokens, fine_gain, fine_shift, fine_qkv, fine_qkv_bias, fine_proj, fine_proj_bias, fine_table, merge_gain, merge_shift, merge_weight, coarse_gain, coarse_shift, coarse_qkv, coarse_qkv_bias, coarse_proj, coarse_proj_bias, coarse_table, cotangent):
    samples = tokens.shape[0]
    channels = C_F
    coarse_width = C_C
    window = WZ * WLAT * WLON
    shift_by = (-1, -(WLAT // 2), -(WLON // 2))
    back_by = (1, WLAT // 2, WLON // 2)
    lat_windows = NLAT // WLAT
    lon_windows = NLON // WLON
    coarse_lon_windows = NLON // 2 // WLON
    coarse_types = NLAT // 2 // WLAT
    level_pos, lat_pos, lon_pos = coordinates(WZ, WLAT, WLON)
    table_index = relative_index(level_pos[:, None], lat_pos[:, None], lon_pos[:, None], level_pos[None], lat_pos[None], lon_pos[None], WLAT).reshape(-1)
    level_ok = (level_pos[:, None] == level_pos[None]) | (jnp.arange(ZWIN) < ZWIN - 1)[:, None, None]
    lat_same = (lat_pos[:, None] < WLAT // 2) == (lat_pos[None] < WLAT // 2)
    fine_terms = jnp.take(fine_table.astype(jnp.float32).reshape(lat_windows, ZWIN, HEADS_F, POS), table_index, axis=3)
    fine_terms = fine_terms.reshape(lat_windows, ZWIN, HEADS_F, window, window)
    coarse_terms = jnp.take(coarse_full(coarse_table.astype(jnp.float32)), table_index, axis=3)
    coarse_terms = coarse_terms.reshape(coarse_types, ZWIN, HEADS_C, window, window)
    norm_factor = 1.0 / math.sqrt(SAMPLES * LEVELS * NLAT * NLON / 4)
    x_wide = tokens.astype(jnp.float32)
    normed = layer_norm(x_wide, fine_gain, fine_shift).astype(jnp.bfloat16)
    fine_windows = to_windows(jnp.roll(normed, shift_by, axis=(1, 2, 3)))
    fine_kinds = jnp.arange(lat_windows * lon_windows, dtype=jnp.int32) // lon_windows

    def fine_core(window_tokens, window_kind):
        qkv_out = (jnp.dot(window_tokens, fine_qkv, preferred_element_type=jnp.float32) + fine_qkv_bias).astype(jnp.bfloat16)
        queries, key_vectors, values = split_heads(qkv_out, channels, HEADS_F)
        allowed = level_ok[:, None] & (lat_same | (window_kind != lat_windows - 1))
        probability, narrow, mixture = attend(queries, key_vectors, values, fine_terms[window_kind], allowed)
        return (queries, key_vectors, values, probability, narrow, mixture)

    def fine_step(element):
        mixture = fine_core(element[0], element[1])[5]
        return mixture.reshape(samples, ZWIN, window, channels)
    fine_mixture = lax.map(fine_step, (fine_windows, fine_kinds))
    attn_windows = (jnp.dot(fine_mixture, fine_proj, preferred_element_type=jnp.float32) + fine_proj_bias).astype(jnp.bfloat16)
    fine_attn = jnp.roll(from_windows(attn_windows, NLAT, NLON), back_by, axis=(1, 2, 3))
    fine_out = (x_wide + fine_attn.astype(jnp.float32)).astype(jnp.bfloat16)
    quartet = fine_out.reshape(samples, LEVELS, NLAT // 2, 2, NLON // 2, 2, channels).transpose(0, 1, 2, 4, 5, 3, 6)
    quartet = quartet.reshape(samples, LEVELS, NLAT // 2, NLON // 2, 4 * channels)
    quartet_wide = quartet.astype(jnp.float32)
    merged_norm = layer_norm(quartet_wide, merge_gain, merge_shift).astype(jnp.bfloat16)
    coarse = jnp.dot(merged_norm, merge_weight, preferred_element_type=jnp.float32).astype(jnp.bfloat16)
    coarse_wide = coarse.astype(jnp.float32)
    coarse_norm = layer_norm(coarse_wide, coarse_gain, coarse_shift).astype(jnp.bfloat16)
    coarse_windows = to_windows(coarse_norm)
    coarse_kinds = jnp.arange(coarse_types * coarse_lon_windows, dtype=jnp.int32) // coarse_lon_windows

    def coarse_core(window_tokens, window_kind):
        qkv_out = (jnp.dot(window_tokens, coarse_qkv, preferred_element_type=jnp.float32) + coarse_qkv_bias).astype(jnp.bfloat16)
        queries, key_vectors, values = split_heads(qkv_out, coarse_width, HEADS_C)
        probability, narrow, mixture = attend(queries, key_vectors, values, coarse_terms[window_kind], True)
        return (queries, key_vectors, values, probability, narrow, mixture)

    def coarse_step(element):
        mixture = coarse_core(element[0], element[1])[5]
        return mixture.reshape(samples, ZWIN, window, coarse_width)
    coarse_mixture = lax.map(coarse_step, (coarse_windows, coarse_kinds))
    coarse_attn_w = (jnp.dot(coarse_mixture, coarse_proj, preferred_element_type=jnp.float32) + coarse_proj_bias).astype(jnp.bfloat16)
    coarse_attn = from_windows(coarse_attn_w, NLAT // 2, NLON // 2)
    coarse_out = (coarse_wide + coarse_attn.astype(jnp.float32)).astype(jnp.bfloat16)
    grad_windows = to_windows(cotangent)

    def coarse_back(totals, element):
        window_tokens, grad_out, window_kind = element
        queries, key_vectors, values, probability, narrow, mixture = coarse_core(window_tokens, window_kind)
        mixture_grad = jnp.dot(grad_out, coarse_proj.T, preferred_element_type=jnp.float32).astype(jnp.bfloat16)
        mixture_grad = mixture_grad.reshape(samples, ZWIN, window, HEADS_C, HEAD)
        query_grad, key_grad, value_grad, score_grad = attend_back(queries, key_vectors, values, probability, narrow, mixture_grad)
        qkv_grad = jnp.concatenate([query_grad.reshape(samples, ZWIN, window, coarse_width), key_grad.reshape(samples, ZWIN, window, coarse_width), value_grad.reshape(samples, ZWIN, window, coarse_width)], -1).astype(jnp.bfloat16)
        summed = lax.optimization_barrier(jnp.sum(score_grad, 0)).reshape(ZWIN, HEADS_C, window * window)
        update = jnp.zeros((ZWIN, HEADS_C, POS), jnp.float32).at[:, :, table_index].add(summed)
        return (totals.at[window_kind].add(update), qkv_grad)
    coarse_table_total, coarse_qkv_grad = lax.scan(coarse_back, jnp.zeros((coarse_types, ZWIN, HEADS_C, POS), jnp.float32), (coarse_windows, grad_windows, coarse_kinds))
    grad_proj_c = jnp.dot(coarse_mixture.reshape(-1, coarse_width).T, grad_windows.reshape(-1, coarse_width), preferred_element_type=jnp.float32)
    grad_proj_bias_c = lax.optimization_barrier(jnp.sum(cotangent.astype(jnp.float32), (0, 1, 2, 3)))
    grad_qkv_c = jnp.dot(coarse_windows.reshape(-1, coarse_width).T, coarse_qkv_grad.reshape(-1, 3 * coarse_width), preferred_element_type=jnp.float32)
    grad_qkv_bias_c = lax.optimization_barrier(jnp.sum(coarse_qkv_grad.astype(jnp.float32), (0, 1, 2, 3)))
    grad_norm_c = from_windows(jnp.dot(coarse_qkv_grad, coarse_qkv.T, preferred_element_type=jnp.float32), NLAT // 2, NLON // 2)
    unused, back_coarse = jax.vjp(layer_norm, coarse_wide, coarse_gain, coarse_shift)
    grad_c, grad_gain_c, grad_shift_c = back_coarse(grad_norm_c)
    coarse_grad = (cotangent.astype(jnp.float32) + grad_c).astype(jnp.bfloat16)
    grad_merge = jnp.dot(merged_norm.reshape(-1, 4 * channels).T, coarse_grad.reshape(-1, coarse_width), preferred_element_type=jnp.float32)
    grad_merged = jnp.dot(coarse_grad, merge_weight.T, preferred_element_type=jnp.float32)
    unused, back_merge = jax.vjp(layer_norm, quartet_wide, merge_gain, merge_shift)
    grad_quartet, grad_gain_m, grad_shift_m = back_merge(grad_merged)
    fine_out_grad = grad_quartet.reshape(samples, LEVELS, NLAT // 2, NLON // 2, 2, 2, channels).transpose(0, 1, 2, 5, 3, 4, 6)
    fine_out_grad = fine_out_grad.reshape(samples, LEVELS, NLAT, NLON, channels)
    fine_attn_grad = fine_out_grad.astype(jnp.bfloat16)
    attn_grad_windows = to_windows(jnp.roll(fine_attn_grad, shift_by, axis=(1, 2, 3)))

    def fine_back(totals, element):
        window_tokens, grad_out, window_kind = element
        queries, key_vectors, values, probability, narrow, mixture = fine_core(window_tokens, window_kind)
        mixture_grad = jnp.dot(grad_out, fine_proj.T, preferred_element_type=jnp.float32).astype(jnp.bfloat16)
        mixture_grad = mixture_grad.reshape(samples, ZWIN, window, HEADS_F, HEAD)
        query_grad, key_grad, value_grad, score_grad = attend_back(queries, key_vectors, values, probability, narrow, mixture_grad)
        qkv_grad = jnp.concatenate([query_grad.reshape(samples, ZWIN, window, channels), key_grad.reshape(samples, ZWIN, window, channels), value_grad.reshape(samples, ZWIN, window, channels)], -1).astype(jnp.bfloat16)
        token_part = jnp.dot(qkv_grad, fine_qkv.T, preferred_element_type=jnp.float32).astype(jnp.bfloat16)
        summed = lax.optimization_barrier(jnp.sum(score_grad, 0)).reshape(ZWIN, HEADS_F, window * window)
        update = jnp.zeros((ZWIN, HEADS_F, POS), jnp.float32).at[:, :, table_index].add(summed)
        return (totals.at[window_kind].add(update), (qkv_grad, token_part))
    fine_table_total, (fine_qkv_grad, fine_token_part) = lax.scan(fine_back, jnp.zeros((lat_windows, ZWIN, HEADS_F, POS), jnp.float32), (fine_windows, attn_grad_windows, fine_kinds))
    grad_proj_f = jnp.dot(fine_mixture.reshape(-1, channels).T, attn_grad_windows.reshape(-1, channels), preferred_element_type=jnp.float32)
    grad_proj_bias_f = lax.optimization_barrier(jnp.sum(fine_attn_grad.astype(jnp.float32), (0, 1, 2, 3)))
    grad_qkv_f = jnp.dot(fine_windows.reshape(-1, channels).T, fine_qkv_grad.reshape(-1, 3 * channels), preferred_element_type=jnp.float32)
    grad_qkv_bias_f = lax.optimization_barrier(jnp.sum(fine_qkv_grad.astype(jnp.float32), (0, 1, 2, 3)))
    normed_grad = jnp.roll(from_windows(fine_token_part, NLAT, NLON), back_by, axis=(1, 2, 3))
    unused, back_fine = jax.vjp(layer_norm, x_wide, fine_gain, fine_shift)
    grad_x, grad_gain_f, grad_shift_f = back_fine(normed_grad.astype(jnp.float32))
    token_grad = (fine_out_grad + grad_x).astype(jnp.bfloat16)
    members = [grad_gain_f, grad_shift_f, grad_qkv_f, grad_qkv_bias_f, grad_proj_f, grad_proj_bias_f, grad_gain_m, grad_shift_m, grad_merge, grad_gain_c, grad_shift_c, grad_qkv_c, grad_qkv_bias_c, grad_proj_c, grad_proj_bias_c]
    param_grads = jnp.concatenate([member.reshape(-1) for member in members]) * norm_factor
    fine_table_grad = fine_table_total.reshape(lat_windows, ZWIN * HEADS_F * POS) * norm_factor
    coarse_table_grad = coarse_split(coarse_table_total) * norm_factor
    return (coarse_out, token_grad, param_grads, fine_table_grad, coarse_table_grad)
```

```python
import functools
import math

import jax
import jax.numpy as jnp
from jax import lax
from jax.experimental import pallas as pl
from jax.experimental.pallas import tpu as pltpu
from jax.sharding import PartitionSpec as P

WZ = 2
WLAT = 6
WLON = 12
HEAD = 32
HEADS_F = 6
HEADS_C = 12
POS = 3312
POSH = 1656
MESH = pl.DeviceIdType.MESH


EPS = 1e-05
NEGATIVE = -1e30


def passed_along(value, axis, steps):
    count = lax.axis_size(axis)
    pairs = [(source, (source + steps) % count) for source in range(count)]
    return lax.ppermute(value, axis, pairs)


def from_partner(block, axis, distance):
    count = lax.axis_size(axis)
    route = []
    for low in range(count):
        high = low | 1 << distance
        if high != low and high < count:
            route += [(low, high), (high, low)]
    return lax.ppermute(block, axis, route)


def layer_norm(volume, scaling, offset):
    centre = volume - jnp.mean(volume, -1, keepdims=True)
    spread = jnp.mean(centre * centre, -1, keepdims=True)
    return centre * lax.rsqrt(spread + EPS) * scaling + offset


def coordinates(depth, height, breadth):
    flattened = jnp.arange(depth * height * breadth, dtype=jnp.int32)
    return (flattened // (height * breadth), flattened // breadth % height, flattened % breadth)


def attend(queries, key_vectors, values, bias_terms, allowed):
    factor = HEAD ** (-0.5)
    scores = (
        jnp.einsum(
            "...qhd,...khd->...hqk", queries, key_vectors, preferred_element_type=jnp.float32
        )
        * factor
        + bias_terms
    )
    scores = jnp.where(allowed, scores, NEGATIVE)
    maximum = jnp.max(scores, -1, keepdims=True)
    weights = jnp.exp(scores - maximum)
    probability = weights / jnp.sum(weights, -1, keepdims=True)
    narrow = probability.astype(jnp.bfloat16)
    mixture = jnp.einsum(
        "...hqk,...khd->...qhd", narrow, values, preferred_element_type=jnp.float32
    )
    return (probability, narrow, mixture.astype(jnp.bfloat16))


def attend_back(queries, key_vectors, values, probability, narrow, mixture_grad):
    factor = HEAD ** (-0.5)
    value_grad = jnp.einsum(
        "...hqk,...qhd->...khd", narrow, mixture_grad, preferred_element_type=jnp.float32
    )
    prob_grad = jnp.einsum(
        "...qhd,...khd->...hqk", mixture_grad, values, preferred_element_type=jnp.float32
    )
    score_grad = probability * (prob_grad - jnp.sum(prob_grad * probability, -1, keepdims=True))
    score_narrow = score_grad.astype(jnp.bfloat16)
    query_grad = (
        jnp.einsum(
            "...hqk,...khd->...qhd", score_narrow, key_vectors, preferred_element_type=jnp.float32
        )
        * factor
    )
    key_grad = (
        jnp.einsum(
            "...hqk,...qhd->...khd", score_narrow, queries, preferred_element_type=jnp.float32
        )
        * factor
    )
    return (query_grad, key_grad, value_grad, score_grad)


def tile_windows(volume):
    samples, levels, rows, cols, width = volume.shape
    shaped = volume.reshape(samples, levels // WZ, WZ, rows // WLAT, WLAT, cols, width).transpose(
        0, 1, 3, 2, 4, 5, 6
    )
    return shaped.reshape(samples, levels // WZ, rows // WLAT, WZ * WLAT * cols, width)


def tile_back(windows, cols):
    samples, zones, blocks, count, width = windows.shape
    shaped = windows.reshape(samples, zones, blocks, WZ, WLAT, cols, width).transpose(
        0, 1, 3, 2, 4, 5, 6
    )
    return shaped.reshape(samples, zones * WZ, blocks * WLAT, cols, width)


def join_columns(own, other, own_first):
    first = jnp.where(own_first, own, other)
    second = jnp.where(own_first, other, own)
    return jnp.concatenate([first, second], -2)


def split_columns(volume, keep_first):
    middle = volume.shape[-2] // 2
    first = volume[..., :middle, :]
    second = volume[..., middle:, :]
    return (jnp.where(keep_first, first, second), jnp.where(keep_first, second, first))


def column_selector(query_cols, offset):
    query_global = jnp.arange(query_cols, dtype=jnp.int32) + offset
    key_cols = jnp.arange(WLON, dtype=jnp.int32)
    diff = (query_global[:, None] - key_cols[None, :] + WLON - 1).reshape(-1)
    return (jnp.arange(2 * WLON - 1, dtype=jnp.int32)[:, None] == diff[None, :]).astype(jnp.float32)


def lat_forward(volume):
    rim = WLAT // 2
    arrived = passed_along(volume[:, :, :rim], "lat", -1)
    return jnp.concatenate([volume[:, :, rim:], arrived], 2)


def lon_forward(volume):
    return passed_along(volume, "lon", -1)


def lat_backward(volume):
    rim = WLAT // 2
    rows = volume.shape[2]
    arrived = passed_along(volume[:, :, rows - rim :], "lat", 1)
    return jnp.concatenate([arrived, volume[:, :, : rows - rim]], 2)


def lon_backward(volume):
    return passed_along(volume, "lon", 1)


def roll_forward(volume):
    volume = lon_forward(lat_forward(volume))
    return jnp.roll(volume, -1, axis=1)


def roll_backward(volume):
    volume = jnp.roll(volume, 1, axis=1)
    return lat_backward(lon_backward(volume))


def gather_group(volume, first_bit, second_bit):
    partner = from_partner(volume, "lon", 0)
    paired = join_columns(volume, partner, first_bit == 0)
    across = from_partner(paired, "lon", 1)
    return join_columns(paired, across, second_bit == 0)


def scatter_group(volume, first_bit, second_bit):
    keeping, sending = split_columns(volume, second_bit == 0)
    column = keeping + from_partner(sending.astype(jnp.bfloat16), "lon", 1).astype(sending.dtype)
    keeping, sending = split_columns(column, first_bit == 0)
    return keeping + from_partner(sending.astype(jnp.bfloat16), "lon", 0).astype(sending.dtype)


def coarse_full_local(table, zones):
    shaped = table.astype(jnp.float32).reshape(
        2, zones, HEADS_C, WZ, WZ, WLAT // 2, WLAT, 2 * WLON - 1
    )
    return shaped.transpose(1, 2, 3, 4, 0, 5, 6, 7).reshape(zones, HEADS_C, POS)


def coarse_split_local(table_grad, zones):
    shaped = table_grad.reshape(zones, HEADS_C, WZ, WZ, 2, WLAT // 2, WLAT, 2 * WLON - 1)
    return shaped.transpose(4, 0, 1, 2, 3, 5, 6, 7).reshape(2, zones * HEADS_C * POSH)


def mesh_parts(lat, lon):
    cores = 2
    xs = 4 if lon % 8 == 0 else 1
    ys = 4 if lat % 4 == 0 else lat
    return (cores, xs, lon // (cores * xs), ys, lat // ys)


def piece_rows(total, lon, ys):
    longest = -(-(127 + total // lon) // 128)
    unit = 16 * ys
    return -(-longest // unit) * unit


def table_rows(count, lon):
    return -(-count // (lon * 128 * 16)) * 16


def pack_body(starts, rows, flat_ref, tables_ref, out_ref):
    for place, start in starts:
        out_ref[place, 0:rows, :] = flat_ref[start : start + rows, :].astype(jnp.bfloat16)
    out_ref[:, rows:, :] = tables_ref[...].astype(jnp.bfloat16)


def pack_pieces(flat, tables, lat, lon):
    cores, xs, zs, ys, hs = mesh_parts(lat, lon)
    total = flat.shape[0]
    rows = piece_rows(total, lon, ys)
    starts = []
    for index in range(lon):
        core, x, z = (index % cores, index // cores % xs, index // (cores * xs))
        starts.append(((core * xs + x) * zs + z, index * (total // lon) // 128))
    height = -(-(max(start for _, start in starts) + rows) // 8) * 8
    flat = jnp.pad(flat, (0, height * 128 - total)).reshape(height, 128)
    return pl.pallas_call(
        functools.partial(pack_body, starts, rows),
        out_shape=jax.ShapeDtypeStruct((lon, rows + tables.shape[1], 128), jnp.bfloat16),
        compiler_params=pltpu.CompilerParams(vmem_limit_bytes=48 * 1024 * 1024),
    )(flat, tables)


def reduce_body(
    dims,
    rows,
    norm_factor,
    g_ref,
    p_ref,
    t_ref,
    r1,
    r2,
    w2,
    r3,
    w3,
    r4,
    s5,
    r5,
    pf,
    tf,
    s1s,
    s1r,
    s2s,
    s2r,
    s3s,
    s3r,
    s4s,
    s4r,
    s5s,
    s5r,
    t4s,
    t4r,
    s6s,
    s6r,
    t6s,
    t6r,
    t7s,
    t7r,
):
    cores, xs, zs, ys, hs = dims
    chunk = rows // ys
    lat = lax.axis_index("lat")
    lon = lax.axis_index("lon")
    core = lax.rem(lon, cores)
    x = lax.rem(lon // cores, xs)
    z = lon // (cores * xs)
    y = lax.rem(lat, ys)
    h = lat // ys

    def lon_of(core_at, x_at, z_at):
        return (z_at * xs + x_at) * cores + core_at

    def core_peer():
        return (lat, lon_of(1 - core, x, z))

    def x_at(d):
        return lax.rem(x + d, xs)

    def z_at(d):
        return lax.rem(z + d, zs)

    def y_at(d):
        return lax.rem(y + d, ys)

    def x_peer(d):
        return (lat, lon_of(core, x_at(d), z))

    def z_peer(d):
        return (lat, lon_of(core, x, z_at(d)))

    def y_peer(d):
        return (h * ys + y_at(d), lon)

    def h_peer():
        return (lax.rem(h + 1, hs) * ys + y, lon)

    peers = [core_peer()]
    peers += [x_peer(d) for d in range(1, xs)]
    peers += [y_peer(d) for d in range(1, ys)]
    peers += [z_peer(d) for d in range(1, zs)]
    if hs > 1:
        peers.append(h_peer())
    barrier = pltpu.get_barrier_semaphore()
    for peer in peers:
        pl.semaphore_signal(barrier, inc=1, device_id=peer, device_id_type=MESH)
    pl.semaphore_wait(barrier, len(peers))

    def send(src, dst, send_sem, recv_sem, peer):
        copy = pltpu.make_async_remote_copy(
            src_ref=src,
            dst_ref=dst,
            send_sem=send_sem,
            recv_sem=recv_sem,
            device_id=peer,
            device_id_type=MESH,
        )
        copy.start()
        return copy

    pending = []
    order = [d % xs for d in range(1, xs + 1)]
    first = {}
    for d in order:
        src = g_ref.at[pl.ds(((1 - core) * xs + x_at(d)) * zs, zs)]
        first[d] = send(src, r1.at[d], s1s.at[d], s1r.at[d], core_peer())
        pending.append(first[d])
    second = []
    for d in order:
        first[d].wait_recv()
        base = (core * xs + x_at(d)) * zs

        def add_pair(i, carry):
            r1[d, i] = (
                r1[d, i].astype(jnp.float32) + g_ref[base + i].astype(jnp.float32)
            ).astype(jnp.bfloat16)
            return carry

        lax.fori_loop(0, zs, add_pair, 0)
        if d > 0:
            copy = send(r1.at[d], r2.at[d - 1], s2s.at[d - 1], s2r.at[d - 1], x_peer(d))
            second.append(copy)
            pending.append(copy)
    for copy in second:
        copy.wait_recv()

    def add_x(i, carry):
        total = r1[0, i].astype(jnp.float32)
        for d in range(1, xs):
            total = total + r2[d - 1, i].astype(jnp.float32)
        w2[i] = total.astype(jnp.bfloat16)
        return carry

    lax.fori_loop(0, zs, add_x, 0)

    third = []
    for d in range(1, ys):
        src = w2.at[:, pl.ds(pl.multiple_of(y_at(d) * chunk, 16), chunk)]
        copy = send(src, r3.at[d - 1], s3s.at[d - 1], s3r.at[d - 1], y_peer(d))
        third.append(copy)
        pending.append(copy)
    for copy in third:
        copy.wait_recv()

    def add_y(i, carry):
        total = w2[i, pl.ds(pl.multiple_of(y * chunk, 16), chunk), :].astype(jnp.float32)
        for d in range(1, ys):
            total = total + r3[d - 1, i].astype(jnp.float32)
        w3[i, 0:chunk, :] = total.astype(jnp.bfloat16)
        w3[i, chunk:, :] = w2[i, rows:, :]
        return carry

    lax.fori_loop(0, zs, add_y, 0)

    fourth = []
    for d in range(1, zs):
        copy = send(w3.at[z_at(d)], r4.at[d - 1], s4s.at[d - 1], s4r.at[d - 1], z_peer(d))
        fourth.append(copy)
        pending.append(copy)
    for copy in fourth:
        copy.wait_recv()
    total = w3[z].astype(jnp.float32)
    for d in range(1, zs):
        total = total + r4[d - 1].astype(jnp.float32)

    s5[...] = total[:chunk]
    if hs > 1:
        fifth = send(s5, r5, s5s.at[0], s5r.at[0], h_peer())
        pending.append(fifth)
    tf[core, x, z] = (total[chunk:] * norm_factor).astype(jnp.bfloat16)
    table_z = []
    for d in range(1, zs):
        copy = send(
            tf.at[core, x, z], tf.at[core, x, z], t4s.at[d - 1], t4r.at[d - 1], z_peer(d)
        )
        table_z.append(copy)
        pending.append(copy)
    share = s5[...]
    if hs > 1:
        fifth.wait_recv()
        share = share + r5[...]
    mine = pl.ds(pl.multiple_of(y * chunk, 8), chunk)
    pf[mine, :] = share * norm_factor
    sixth = []
    for d in range(1, ys):
        copy = send(pf.at[mine], pf.at[mine], s6s.at[d - 1], s6r.at[d - 1], y_peer(d))
        sixth.append(copy)
        pending.append(copy)
    for copy in table_z:
        copy.wait_recv()
    table_x = []
    for d in range(1, xs):
        copy = send(tf.at[core, x], tf.at[core, x], t6s.at[d - 1], t6r.at[d - 1], x_peer(d))
        table_x.append(copy)
        pending.append(copy)
    for copy in table_x:
        copy.wait_recv()
    table_core = send(tf.at[core], tf.at[core], t7s.at[0], t7r.at[0], core_peer())
    pending.append(table_core)
    for copy in sixth:
        copy.wait_recv()
    p_ref[...] = pf[...]
    table_core.wait_recv()
    t_ref[...] = tf[...]
    for copy in pending:
        copy.wait_send()


def reduce_all(pieces, rows, norm_factor, lat, lon):
    dims = mesh_parts(lat, lon)
    cores, xs, zs, ys, hs = dims
    height = pieces.shape[1]
    trows = height - rows
    chunk = rows // ys
    bf16 = jnp.bfloat16
    sem = pltpu.SemaphoreType.DMA
    counts = [xs, xs - 1, ys - 1, zs - 1, 1, zs - 1, ys - 1, xs - 1, 1]
    sems = []
    for count in counts:
        sems += [sem((max(count, 1),)), sem((max(count, 1),))]
    vmem = pl.BlockSpec(memory_space=pltpu.VMEM)
    return pl.pallas_call(
        functools.partial(reduce_body, dims, rows, norm_factor),
        out_shape=(
            jax.ShapeDtypeStruct((rows, 128), jnp.float32),
            jax.ShapeDtypeStruct((cores, xs, zs, trows, 128), bf16),
        ),
        in_specs=[vmem],
        out_specs=(vmem, vmem),
        scratch_shapes=[
            pltpu.VMEM((xs, zs, height, 128), bf16),
            pltpu.VMEM((max(xs - 1, 1), zs, height, 128), bf16),
            pltpu.VMEM((zs, height, 128), bf16),
            pltpu.VMEM((max(ys - 1, 1), zs, chunk, 128), bf16),
            pltpu.VMEM((zs, chunk + trows, 128), bf16),
            pltpu.VMEM((max(zs - 1, 1), chunk + trows, 128), bf16),
            pltpu.VMEM((chunk, 128), jnp.float32),
            pltpu.VMEM((chunk, 128), jnp.float32),
            pltpu.VMEM((rows, 128), jnp.float32),
            pltpu.VMEM((cores, xs, zs, trows, 128), bf16),
        ]
        + sems,
        compiler_params=pltpu.CompilerParams(
            collective_id=7, has_side_effects=True, vmem_limit_bytes=48 * 1024 * 1024
        ),
        name="grad_reduce",
    )(pieces)


def reduce_grads(local_grads, table_parts, norm_factor):
    lat = lax.axis_size("lat")
    lon = lax.axis_size("lon")
    cores, xs, zs, ys, hs = mesh_parts(lat, lon)
    total = local_grads.shape[0]
    tables = jnp.concatenate([part.reshape(-1) for part in table_parts])
    count = tables.shape[0]
    trows = table_rows(count, lon)
    tables = jnp.pad(tables, (0, lon * trows * 128 - count)).reshape(lon, trows, 128)
    pieces = pack_pieces(local_grads, tables, lat, lon)
    owned, table_sum = reduce_all(
        pieces, pieces.shape[1] - trows, norm_factor, lat, lon
    )
    segment = total // lon
    shift = lax.rem(lax.axis_index("lon") * segment, 128)
    params = lax.dynamic_slice(owned.reshape(-1), (shift,), (segment,))
    table_flat = table_sum.reshape(-1)[:count].astype(jnp.float32)
    outs = []
    at = 0
    for part in table_parts:
        outs.append(table_flat[at : at + part.size].reshape(part.shape))
        at += part.size
    return (params, outs)


def shards(
    tokens,
    fine_gain,
    fine_shift,
    fine_qkv,
    fine_qkv_bias,
    fine_proj,
    fine_proj_bias,
    fine_table,
    merge_gain,
    merge_shift,
    merge_weight,
    coarse_gain,
    coarse_shift,
    coarse_qkv,
    coarse_qkv_bias,
    coarse_proj,
    coarse_proj_bias,
    coarse_table,
    cotangent,
):
    samples, levels, lat_rows, lon_cols, channels = tokens.shape
    coarse_width = coarse_qkv.shape[0]
    zones = levels // WZ
    lat_wins = lat_rows // WLAT
    half_rows = lat_rows // 2
    half_cols = lon_cols // 2
    window = WZ * WLAT * WLON
    fine_count = WZ * WLAT * lon_cols
    coarse_count = WZ * WLAT * half_cols
    spans = 2 * WLON - 1
    lon_index = lax.axis_index("lon")
    fine_parity = lon_index % 2
    first_bit = lon_index % 2
    second_bit = lon_index // 2 % 2
    group_pos = lon_index % 4
    lat_last = lax.axis_index("lat") == lax.axis_size("lat") - 1
    norm_factor = 1.0 / math.sqrt(
        samples * levels * lat_rows * lon_cols * lax.axis_size("lat") * lax.axis_size("lon") / 4
    )
    level_pos, lat_pos, lon_pos = coordinates(WZ, WLAT, WLON)
    own_level, own_lat, own_lon = coordinates(WZ, WLAT, lon_cols)
    level_ok = (own_level[:, None] == level_pos[None]) | (jnp.arange(zones) < zones - 1)[
        :, None, None
    ]
    lat_same = (own_lat[:, None] < WLAT // 2) == (lat_pos[None] < WLAT // 2)
    last_window = lat_last & (jnp.arange(lat_wins) == lat_wins - 1)
    allowed_fine = (
        level_ok[:, None] & (lat_same[None] | jnp.logical_not(last_window)[:, None, None])[None]
    )[:, :, None]
    fine_select = column_selector(lon_cols, lon_cols * fine_parity)
    fine_grid = fine_table.astype(jnp.float32).reshape(
        lat_wins, zones, HEADS_F, WZ, WZ, WLAT, WLAT, spans
    )
    fine_terms = jnp.dot(fine_grid, fine_select, precision=lax.Precision.HIGHEST)
    fine_terms = fine_terms.reshape(lat_wins, zones, HEADS_F, WZ, WZ, WLAT, WLAT, lon_cols, WLON)
    fine_terms = fine_terms.transpose(1, 0, 2, 3, 5, 7, 4, 6, 8).reshape(
        zones, lat_wins, HEADS_F, fine_count, window
    )
    x_wide = tokens.astype(jnp.float32)
    normed = layer_norm(x_wide, fine_gain, fine_shift).astype(jnp.bfloat16)
    window_tile = tile_windows(roll_forward(normed))
    fine_qkv_out = (
        jnp.dot(window_tile, fine_qkv, preferred_element_type=jnp.float32) + fine_qkv_bias
    ).astype(jnp.bfloat16)
    own_pairs = fine_qkv_out[..., channels:]
    lead = own_pairs.shape[:3]
    partner_pairs = from_partner(own_pairs, "lon", 0)
    joined = join_columns(
        own_pairs.reshape(lead + (WZ, WLAT, lon_cols, 2 * channels)),
        partner_pairs.reshape(lead + (WZ, WLAT, lon_cols, 2 * channels)),
        fine_parity == 0,
    )
    joined = joined.reshape(lead + (window, 2 * channels))
    query_f = fine_qkv_out[..., :channels].reshape(lead + (fine_count, HEADS_F, HEAD))
    keys_f = joined[..., :channels].reshape(lead + (window, HEADS_F, HEAD))
    values_f = joined[..., channels:].reshape(lead + (window, HEADS_F, HEAD))
    probs_f, narrow_f, mixture_f = attend(query_f, keys_f, values_f, fine_terms, allowed_fine)
    mixture_f = mixture_f.reshape(lead + (fine_count, channels))
    attn_tile = (
        jnp.dot(mixture_f, fine_proj, preferred_element_type=jnp.float32) + fine_proj_bias
    ).astype(jnp.bfloat16)
    fine_attn = roll_backward(tile_back(attn_tile, lon_cols))
    fine_out = (x_wide + fine_attn.astype(jnp.float32)).astype(jnp.bfloat16)
    quartet = fine_out.reshape(samples, levels, half_rows, 2, half_cols, 2, channels).transpose(
        0, 1, 2, 4, 5, 3, 6
    )
    quartet = quartet.reshape(samples, levels, half_rows, half_cols, 4 * channels)
    quartet_wide = quartet.astype(jnp.float32)
    merged_norm = layer_norm(quartet_wide, merge_gain, merge_shift).astype(jnp.bfloat16)
    coarse = jnp.dot(merged_norm, merge_weight, preferred_element_type=jnp.float32).astype(
        jnp.bfloat16
    )
    coarse_wide = coarse.astype(jnp.float32)
    coarse_norm = layer_norm(coarse_wide, coarse_gain, coarse_shift).astype(jnp.bfloat16)
    full_table = coarse_full_local(coarse_table, zones).reshape(
        zones, HEADS_C, WZ, WZ, WLAT, WLAT, spans
    )
    coarse_select = column_selector(half_cols, half_cols * group_pos)
    own_qkv = (
        jnp.dot(coarse_norm, coarse_qkv, preferred_element_type=jnp.float32) + coarse_qkv_bias
    ).astype(jnp.bfloat16)
    group_pairs = gather_group(own_qkv[..., coarse_width:], first_bit, second_bit)
    group_pairs = tile_windows(group_pairs)
    clead = group_pairs.shape[:3]
    keys_c = group_pairs[..., :coarse_width].reshape(clead + (window, HEADS_C, HEAD))
    values_c = group_pairs[..., coarse_width:].reshape(clead + (window, HEADS_C, HEAD))
    query_c = tile_windows(own_qkv[..., :coarse_width]).reshape(
        clead + (coarse_count, HEADS_C, HEAD)
    )
    coarse_terms = jnp.dot(full_table, coarse_select, precision=lax.Precision.HIGHEST)
    coarse_terms = coarse_terms.reshape(zones, HEADS_C, WZ, WZ, WLAT, WLAT, half_cols, WLON)
    coarse_terms = coarse_terms.transpose(0, 1, 2, 4, 6, 3, 5, 7).reshape(
        zones, HEADS_C, coarse_count, window
    )[:, None]
    probs_c, narrow_c, mixture_c = attend(query_c, keys_c, values_c, coarse_terms, True)
    mixture_c = mixture_c.reshape(clead + (coarse_count, coarse_width))
    attn_windows = (
        jnp.dot(mixture_c, coarse_proj, preferred_element_type=jnp.float32) + coarse_proj_bias
    ).astype(jnp.bfloat16)
    coarse_attn = tile_back(attn_windows, half_cols)
    cot_windows = tile_windows(cotangent)
    grad_proj_c = jnp.dot(
        mixture_c.reshape(-1, coarse_width).T,
        cot_windows.reshape(-1, coarse_width),
        preferred_element_type=jnp.float32,
    )
    mixture_grad_c = jnp.dot(cot_windows, coarse_proj.T, preferred_element_type=jnp.float32).astype(
        jnp.bfloat16
    )
    mixture_grad_c = mixture_grad_c.reshape(clead + (coarse_count, HEADS_C, HEAD))
    query_grad_c, key_grad_c, value_grad_c, score_grad_c = attend_back(
        query_c, keys_c, values_c, probs_c, narrow_c, mixture_grad_c
    )
    group_grad = jnp.concatenate(
        [
            key_grad_c.reshape(clead + (window, coarse_width)),
            value_grad_c.reshape(clead + (window, coarse_width)),
        ],
        -1,
    )
    own_pair_grad = scatter_group(tile_back(group_grad, WLON), first_bit, second_bit)
    query_tile = tile_back(query_grad_c.reshape(clead + (coarse_count, coarse_width)), half_cols)
    coarse_qkv_grad = jnp.concatenate([query_tile, own_pair_grad], -1).astype(jnp.bfloat16)
    coarse_scores = jnp.sum(score_grad_c, 0).reshape(
        zones, HEADS_C, WZ, WLAT, half_cols, WZ, WLAT, WLON
    )
    coarse_scores = coarse_scores.transpose(0, 1, 2, 5, 3, 6, 4, 7).reshape(
        zones, HEADS_C, WZ, WZ, WLAT, WLAT, half_cols * WLON
    )
    coarse_table_part = jnp.dot(
        coarse_scores, coarse_select.T, precision=lax.Precision.HIGHEST
    ).reshape(zones, HEADS_C, POS)
    coarse_out = (coarse_wide + coarse_attn.astype(jnp.float32)).astype(jnp.bfloat16)
    grad_proj_bias_c = jnp.sum(cotangent.astype(jnp.float32), (0, 1, 2, 3))
    grad_qkv_c = jnp.dot(
        coarse_norm.reshape(-1, coarse_width).T,
        coarse_qkv_grad.reshape(-1, 3 * coarse_width),
        preferred_element_type=jnp.float32,
    )
    grad_qkv_bias_c = jnp.sum(coarse_qkv_grad.astype(jnp.float32), (0, 1, 2, 3))
    grad_norm_c = jnp.dot(coarse_qkv_grad, coarse_qkv.T, preferred_element_type=jnp.float32)
    unused, back_coarse = jax.vjp(layer_norm, coarse_wide, coarse_gain, coarse_shift)
    grad_c, grad_gain_c, grad_shift_c = back_coarse(grad_norm_c)
    coarse_grad = (cotangent.astype(jnp.float32) + grad_c).astype(jnp.bfloat16)
    grad_merge = jnp.dot(
        merged_norm.reshape(-1, 4 * channels).T,
        coarse_grad.reshape(-1, coarse_width),
        preferred_element_type=jnp.float32,
    )
    grad_merged = jnp.dot(coarse_grad, merge_weight.T, preferred_element_type=jnp.float32)
    unused, back_merge = jax.vjp(layer_norm, quartet_wide, merge_gain, merge_shift)
    grad_quartet, grad_gain_m, grad_shift_m = back_merge(grad_merged)
    fine_out_grad = grad_quartet.reshape(
        samples, levels, half_rows, half_cols, 2, 2, channels
    ).transpose(0, 1, 2, 5, 3, 4, 6)
    fine_out_grad = fine_out_grad.reshape(samples, levels, lat_rows, lon_cols, channels)
    fine_attn_grad = fine_out_grad.astype(jnp.bfloat16)
    grad_tile = tile_windows(roll_forward(fine_attn_grad))
    grad_proj_f = jnp.dot(
        mixture_f.reshape(-1, channels).T,
        grad_tile.reshape(-1, channels),
        preferred_element_type=jnp.float32,
    )
    grad_proj_bias_f = jnp.sum(fine_attn_grad.astype(jnp.float32), (0, 1, 2, 3))
    mixture_grad_f = jnp.dot(grad_tile, fine_proj.T, preferred_element_type=jnp.float32).astype(
        jnp.bfloat16
    )
    mixture_grad_f = mixture_grad_f.reshape(lead + (fine_count, HEADS_F, HEAD))
    query_grad_f, key_grad_f, value_grad_f, score_grad_f = attend_back(
        query_f, keys_f, values_f, probs_f, narrow_f, mixture_grad_f
    )
    pair_grad = jnp.concatenate(
        [
            key_grad_f.reshape(lead + (window, channels)),
            value_grad_f.reshape(lead + (window, channels)),
        ],
        -1,
    )
    pair_grad = pair_grad.reshape(lead + (WZ, WLAT, WLON, 2 * channels))
    keeping, sending = split_columns(pair_grad, fine_parity == 0)
    own_pair_f = keeping + from_partner(sending.astype(jnp.bfloat16), "lon", 0).astype(
        sending.dtype
    )
    fine_qkv_grad = jnp.concatenate(
        [
            query_grad_f.reshape(lead + (fine_count, channels)),
            own_pair_f.reshape(lead + (fine_count, 2 * channels)),
        ],
        -1,
    ).astype(jnp.bfloat16)
    grad_qkv_f = jnp.dot(
        window_tile.reshape(-1, channels).T,
        fine_qkv_grad.reshape(-1, 3 * channels),
        preferred_element_type=jnp.float32,
    )
    grad_qkv_bias_f = jnp.sum(fine_qkv_grad.astype(jnp.float32), (0, 1, 2, 3))
    tile_token_grad = jnp.dot(fine_qkv_grad, fine_qkv.T, preferred_element_type=jnp.float32).astype(
        jnp.bfloat16
    )
    normed_grad = roll_backward(tile_back(tile_token_grad, lon_cols))
    unused, back_fine = jax.vjp(layer_norm, x_wide, fine_gain, fine_shift)
    grad_x, grad_gain_f, grad_shift_f = back_fine(normed_grad.astype(jnp.float32))
    token_grad = (fine_out_grad + grad_x).astype(jnp.bfloat16)
    fine_scores = jnp.sum(score_grad_f, 0).reshape(
        zones, lat_wins, HEADS_F, WZ, WLAT, lon_cols, WZ, WLAT, WLON
    )
    fine_scores = fine_scores.transpose(1, 0, 2, 3, 6, 4, 7, 5, 8).reshape(
        lat_wins, zones, HEADS_F, WZ, WZ, WLAT, WLAT, lon_cols * WLON
    )
    fine_table_part = jnp.dot(fine_scores, fine_select.T, precision=lax.Precision.HIGHEST)
    fine_table_part = fine_table_part.reshape(lat_wins, zones * HEADS_F * POS)
    coarse_table_rows = coarse_split_local(coarse_table_part, zones)
    members = [
        grad_gain_f,
        grad_shift_f,
        grad_qkv_f,
        grad_qkv_bias_f,
        grad_proj_f,
        grad_proj_bias_f,
        grad_gain_m,
        grad_shift_m,
        grad_merge,
        grad_gain_c,
        grad_shift_c,
        grad_qkv_c,
        grad_qkv_bias_c,
        grad_proj_c,
        grad_proj_bias_c,
    ]
    local_grads = jnp.concatenate([member.reshape(-1) for member in members])
    param_grads, table_totals = reduce_grads(
        local_grads, (fine_table_part, coarse_table_rows), norm_factor
    )
    return (
        coarse_out,
        token_grad,
        param_grads,
        table_totals[0],
        table_totals[1],
    )


def solution(mesh):
    return jax.shard_map(
        shards,
        mesh=mesh,
        in_specs=(
            P(None, None, "lat", "lon", None),
            P(),
            P(),
            P(),
            P(),
            P(),
            P(),
            P("lat", None),
            P(),
            P(),
            P(),
            P(),
            P(),
            P(),
            P(),
            P(),
            P(),
            P("lat", None),
            P(None, None, "lat", "lon", None),
        ),
        out_specs=(
            P(None, None, "lat", "lon", None),
            P(None, None, "lat", "lon", None),
            P("lon"),
            P("lat", None),
            P("lat", None),
        ),
        check_vma=False,
    )
```

```python
import functools
import math

import jax
import jax.numpy as jnp
from jax import lax
from jax.experimental import pallas as pl
from jax.experimental.pallas import tpu as pltpu
from jax.sharding import PartitionSpec as P

HEAD = 32
HEADS_F = 6
HEADS_C = 12
C_F = 192
C_C = 384
SPAN = 23
EPS = 1e-05
NEGATIVE = -1e30
MESH = pl.DeviceIdType.MESH
F32 = jnp.float32
BF16 = jnp.bfloat16
MIB = 1024 * 1024
VMEM_BYTES = 60 * MIB

LOW, MID, TOP = (0, 80, 224)
PARAMS = 1037184
TABLE_ROWS = 2048
FINE = 304
SIDE = 80
COARSE = 80
PART_C, PART_A, PART_B, PART_Q, PART_END = (0, 256, 688, 928, 1792)


def whole(x, n):
    return jnp.floor((x + 0.5) * (1.0 / n))


def rest(x, n):
    return x - n * whole(x, n)


def down_rows(n):
    return lax.broadcasted_iota(jnp.int32, (n, 1), 0).astype(F32)


def along_lanes(n):
    return lax.broadcasted_iota(jnp.int32, (1, n), 1).astype(F32)


def match(a, b):
    return jnp.where(a == b, 1.0, 0.0).astype(BF16)


def fine_row(zone, zq, row, col):
    low = LOW + zone * 40 + (zq * 3 + row) * 6 + col
    mid = MID + zone * 72 + (zq * 6 + row - 3) * 6 + col
    top = TOP + zone * 40 + (zq * 3 + row - 9) * 6 + col
    return jnp.where(row < 3, low, jnp.where(row < 9, mid, top))


def fine_order():
    at = down_rows(FINE)
    low, top = (at < MID, at >= TOP)
    edge = jnp.where(top, at - TOP, at)
    mid = at - MID
    in_edge = low | top
    part = rest(edge, 40)
    zone = jnp.where(in_edge, whole(edge, 40), whole(mid, 72))
    zq = jnp.where(in_edge, whole(part, 18), whole(rest(mid, 72), 36))
    row = jnp.where(
        in_edge,
        whole(rest(part, 18), 6) + jnp.where(top, 9.0, 0.0),
        3 + whole(rest(mid, 36), 6),
    )
    col = jnp.where(in_edge, rest(part, 6), rest(mid, 6))
    code = (row * 6 + col) * 4 + rest(2 * zone + zq + 1, 4)
    return match(jnp.where(in_edge & (part >= 36), -1.0, code), along_lanes(288))


def coarse_place(at):
    part = rest(at, 40)
    return (whole(at, 40), whole(part, 18), whole(rest(part, 18), 3), rest(part, 3), part < 36)


def coarse_order():
    zone, zq, row, col, valid = coarse_place(down_rows(COARSE))
    code = (row * 3 + col) * 4 + 2 * zone + zq
    return match(jnp.where(valid, code, -1.0), along_lanes(72))


def quartet_order():
    at = down_rows(4 * COARSE)
    p = whole(at, COARSE)
    zone, zq, row, col, valid = coarse_place(rest(at, COARSE))
    rolled = rest(2 * zone + zq + 3, 4)
    source = fine_row(
        whole(rolled, 2), rest(rolled, 2), 2 * row + rest(p, 2), 2 * col + whole(p, 2)
    )
    return match(jnp.where(valid, source, -1.0), along_lanes(FINE))


def head_rows(heads, lats, cols, tokens, block):
    at = down_rows(block * cols)
    part = rest(at, block)
    h = whole(part, 2 * lats)
    zq = whole(rest(part, 2 * lats), lats)
    code = (zq * lats + rest(part, lats)) * cols + whole(at, block)
    valid = part < heads * 2 * lats
    head = jnp.where(valid, h, -1.0)
    mask = match(head, whole(along_lanes(heads * HEAD), HEAD)).astype(F32)
    return (match(jnp.where(valid, code, -1.0), along_lanes(tokens)), mask, zq)


def pair_keys(size, half):
    u = along_lanes(size)
    if size == 144:
        source, part = (whole(u, 72), rest(u, 72))
        zk, ak, valid = (whole(part, 36), whole(rest(part, 36), 6), part >= 0)
    else:
        slot, part = (whole(u, 40), rest(u, 40))
        source = rest(slot, 2)
        zk = whole(part, 18)
        ak = 3 * whole(slot, 2) + whole(rest(part, 18), 6)
        valid = part < 36
    return (zk, ak, rest(part, 6) + 6 * jnp.abs(half - source), valid)


def group_keys():
    u = along_lanes(160)
    part = rest(u, 40)
    zk, ak = (whole(part, 18), whole(rest(part, 18), 3))
    return (zk, ak, rest(part, 3) + 3 * whole(u, 40), part < 36)


def toeplitz(keys, cols, shift):
    zk, ak, col, valid = keys
    at = down_rows(384)
    tail = at >= 256
    level = jnp.where(tail, whole(at - 256, 64), whole(at, 128))
    entry = jnp.where(tail, 128 + rest(at, 64), rest(at, 128))
    code = (level * 6 + whole(entry, SPAN)) * 64 + rest(entry, SPAN)
    code = jnp.where(entry < 138, code, -1.0)
    key_code = jnp.where(valid, (zk * 6 + ak) * 64 - col + shift + 11, -100.0)
    return [match(code, key_code + oq) for oq in range(cols)]


def table_lanes(zk):
    entry = down_rows(138)
    return match(
        jnp.where(entry < 128, zk * 128 + entry, 256 + zk * 64 + entry - 128), along_lanes(384)
    )


def table_rows(kind, zk):
    if kind == "q":
        at = down_rows(288)
        part = rest(at, 144)
        aq = rest(part, 6)
        lead = (whole(aq, 3) * 2 + whole(at, 144)) * HEADS_C + whole(part, 12)
        zq = whole(rest(part, 12), 6)
        return match(((lead * 2 + zq) * 2 + zk) * 3 + rest(aq, 3), along_lanes(576))
    if kind == "a":
        at, block, lats, first = (down_rows(144), 72, 6, 0)
    else:
        at, block, lats, first = (down_rows(80), 40, 3, 3 if kind == "c" else 0)
    part = rest(at, block)
    lead = whole(at, block) * HEADS_F + whole(part, 2 * lats)
    zq = whole(rest(part, 2 * lats), lats)
    code = ((lead * 2 + zq) * 2 + zk) * 6 + rest(part, lats) + first
    return match(jnp.where(part < 12 * lats, code, -1.0), along_lanes(288))


def dot(a, b):
    return jnp.dot(a.astype(BF16), b.astype(BF16), preferred_element_type=F32)


def dot_nt(a, b):
    return lax.dot_general(
        a.astype(BF16), b.astype(BF16), (((1,), (1,)), ((), ())), preferred_element_type=F32
    )


def dot_tn(a, b):
    return lax.dot_general(
        a.astype(BF16), b.astype(BF16), (((0,), (0,)), ((), ())), preferred_element_type=F32
    )


def rounded(value):
    return value.astype(BF16).astype(F32)


def norm_parts(volume):
    centre = volume - jnp.mean(volume, -1, keepdims=True)
    spread = jnp.mean(centre * centre, -1, keepdims=True)
    scale = lax.rsqrt(spread + EPS)
    return (centre * scale, scale)


def norm_back(hat, scale, grad, gain):
    inner = grad * gain
    return scale * (
        inner
        - jnp.mean(inner, -1, keepdims=True)
        - hat * jnp.mean(inner * hat, -1, keepdims=True)
    )


def column_sum(value):
    return jnp.sum(value, 0, keepdims=True)


def attend(queries, keys, values, rows, mask, bias):
    packed = dot(rows, queries) * mask
    scores = dot_nt(packed, keys) * HEAD ** (-0.5) + bias
    weights = jnp.exp(scores - jnp.max(scores, -1, keepdims=True))
    probs = weights / jnp.sum(weights, -1, keepdims=True)
    mixture = dot(probs, values) * mask
    return (probs, dot_tn(rows, mixture))


def attend_back(queries, keys, values, rows, mask, probs, mixture_grad, toep, block):
    factor = HEAD ** (-0.5)
    packed = dot(rows, queries) * mask
    grad = dot(rows, mixture_grad) * mask
    value_grad = dot_tn(probs, grad)
    prob_grad = dot_nt(grad, values)
    score_grad = probs * (prob_grad - jnp.sum(prob_grad * probs, -1, keepdims=True))
    query_grad = dot_tn(rows, dot(score_grad, keys) * factor * mask)
    key_grad = dot_tn(score_grad, packed) * factor
    table = None
    for oq, select in enumerate(toep):
        part = dot_nt(score_grad[oq * block : (oq + 1) * block], select)
        table = part if table is None else table + part
    return (query_grad, key_grad, value_grad, table)


def lasting(micros):
    return pl.CostEstimate(flops=0, bytes_accessed=int(micros * 3.69e6), transcendentals=0)


def call(body, outs, args, scratch, name, micros, in_place=(), limit=VMEM_BYTES):
    vmem = pl.BlockSpec(memory_space=pltpu.VMEM)
    away = pl.BlockSpec(memory_space=pltpu.HBM)
    return pl.pallas_call(
        body,
        out_shape=tuple(jax.ShapeDtypeStruct(shape, dtype) for shape, dtype in outs),
        in_specs=[away if at in in_place else vmem for at in range(len(args))],
        out_specs=(vmem,) * len(outs),
        scratch_shapes=list(scratch),
        compiler_params=pltpu.CompilerParams(vmem_limit_bytes=limit),
        cost_estimate=lasting(micros),
        name=name,
    )(*args)


def vector(ref):
    return ref[...].reshape(1, -1)


def query_half():
    return 1 - lax.rem(lax.axis_index("lon"), 2)


def packed_side(value):
    tail = jnp.concatenate([value[0:40, 128:192], value[40:80, 128:192]], 1)
    return jnp.concatenate([value[:, 0:128], tail, jnp.zeros((8, 128), value.dtype)], 0)


def unpacked_side(block):
    tail = jnp.concatenate([block[80:120, 0:64], block[80:120, 64:128]], 0)
    return jnp.concatenate([block[0:80, :], tail], 1)


def lane_blocks(pieces):
    blocks = []
    for a, b in zip(pieces[::2], pieces[1::2]):
        blocks += [a[:, 0:128], jnp.concatenate([a[:, 128:192], b[:, 0:64]], 1), b[:, 64:192]]
    return blocks


def partner_of(lon, count):
    odd = lax.rem(lon, 2)
    return lax.rem(lon + 2 * odd - 1 + count, count)


def ring_positions():
    lat_count, lon_count = (lax.axis_size("lat"), lax.axis_size("lon"))
    lat, lon = (lax.axis_index("lat"), lax.axis_index("lon"))
    up = lax.rem(lat + 1, lat_count)
    down = lax.rem(lat + lat_count - 1, lat_count)
    return (lat, lon, up, down, partner_of(lon, lon_count))


def meet(peers):
    barrier = pltpu.get_barrier_semaphore()
    for peer in peers:
        pl.semaphore_signal(barrier, inc=1, device_id=peer, device_id_type=MESH)
    pl.semaphore_wait(barrier, len(peers))


def start_copy(src, dst, send_sem, recv_sem, peer):
    copy = pltpu.make_async_remote_copy(
        src_ref=src,
        dst_ref=dst,
        send_sem=send_sem,
        recv_sem=recv_sem,
        device_id=peer,
        device_id_type=MESH,
    )
    copy.start()
    return copy


def exchange(sends, send_sems, recv_sems):
    copies = []
    for at, (src, dst, peer) in enumerate(sends):
        copies.append(start_copy(src, dst, send_sems.at[at], recv_sems.at[at], peer))
    for copy in copies:
        copy.wait_recv()
    for copy in copies:
        copy.wait_send()


def exchange_call(body, outs, args, scratch, counts, collective_id, name, micros):
    vmem = pl.BlockSpec(memory_space=pltpu.VMEM)
    sem = pltpu.SemaphoreType.DMA
    return pl.pallas_call(
        body,
        out_shape=tuple(jax.ShapeDtypeStruct(shape, dtype) for shape, dtype in outs),
        in_specs=[vmem] * len(args),
        out_specs=(vmem,) * len(outs),
        scratch_shapes=list(scratch) + [sem((count,)) for count in counts for _ in range(2)],
        compiler_params=pltpu.CompilerParams(
            collective_id=collective_id, has_side_effects=True, vmem_limit_bytes=VMEM_BYTES
        ),
        cost_estimate=lasting(micros),
        name=name,
    )(*args)


def halo_body(x_ref, low_ref, high_ref, tab_ref, *refs):
    outs, bufs, (ss, rs, ts, tr) = (refs[:6], refs[6:12], refs[12:])
    par, upo, upp, dno, dnp, tab = bufs
    lat, lon, up, down, partner = ring_positions()
    size = tab.shape[0]
    rank = lax.rem(lon, size)
    others = [lax.rem(rank + d, size) for d in range(1, size)]
    near = [(lat, lon - rank + other) for other in others]
    beside = (lat, partner)
    meet([beside, (up, lon), (down, lon)] + near)
    x_copy = start_copy(x_ref, par, ss.at[0], rs.at[0], beside)
    low_copy = start_copy(low_ref, upo, ss.at[1], rs.at[1], (down, lon))
    high_copy = start_copy(high_ref, dno, ss.at[2], rs.at[2], (up, lon))
    table_copy = start_copy(tab_ref.at[rank], tab.at[rank], ss.at[3], rs.at[3], (up, lon))
    copies = [x_copy, low_copy, high_copy, table_copy]
    low_copy.wait_recv()
    relays = [start_copy(upo, upp, ss.at[4], rs.at[4], beside)]
    high_copy.wait_recv()
    relays.append(start_copy(dno, dnp, ss.at[5], rs.at[5], beside))
    table_copy.wait_recv()
    for d, peer in enumerate(near):
        relays.append(start_copy(tab.at[rank], tab.at[rank], ts.at[d], tr.at[d], peer))
    x_copy.wait_recv()
    for copy in relays:
        copy.wait_recv()
    for copy in copies + relays:
        copy.wait_send()
    for out, buf in zip(outs, bufs):
        out[...] = buf[...]


def group_body(own_ref, out_ref, buf, ss, rs):
    lat, lon = (lax.axis_index("lat"), lax.axis_index("lon"))
    place = lax.rem(lon, 4)
    others = [lax.rem(place + d, 4) for d in range(1, 4)]
    peers = [(lat, lon - place + other) for other in others]
    meet(peers)
    buf[place] = own_ref[...]
    exchange([(own_ref, buf.at[place], peer) for peer in peers], ss, rs)
    out_ref[...] = buf[...]


def ungroup_body(parts_ref, out_ref, buf, ss, rs):
    lat, lon = (lax.axis_index("lat"), lax.axis_index("lon"))
    place = lax.rem(lon, 4)
    others = [lax.rem(place + d, 4) for d in range(1, 4)]
    peers = [(lat, lon - place + other) for other in others]
    meet(peers)
    exchange(
        [(parts_ref.at[other], buf.at[d], peers[d]) for d, other in enumerate(others)], ss, rs
    )
    total = parts_ref[place].astype(F32)
    for d in range(3):
        total = total + buf[d].astype(F32)
    out_ref[...] = total


def spread(kind, table):
    total = None
    for zk in range(2):
        part = dot(dot(table_rows(kind, zk), table), table_lanes(zk))
        total = part if total is None else total + part
    return total


def bias_rows(table, toep, zone, block):
    rows = table[zone * block : (zone + 1) * block]
    return jnp.concatenate([dot(rows, select) for select in toep], 0)


def banned(keys, zq, zone):
    ban = jnp.where(keys[3], 0.0, NEGATIVE)
    if zone == 1:
        ban = ban + jnp.where(zq == keys[0], 0.0, NEGATIVE)
    return ban


def fetch_groups(stage, ref):
    rows, cols = ref.shape[:2]
    for row in range(rows):
        for col in range(cols):
            at = (row * cols + col) * 4
            stage[at : at + 4, :] = ref[row, col].astype(F32)


def store_groups(ref, stage):
    rows, cols = ref.shape[:2]
    for row in range(rows):
        for col in range(cols):
            at = (row * cols + col) * 4
            ref[row, col] = stage[at : at + 4, :].astype(BF16)


def prepare_body(x_ref, tf_ref, own_out, low_out, high_out, tab_out, stage):
    fetch_groups(stage, x_ref)
    tokens = dot(fine_order(), stage[...])
    own_out[...] = tokens.astype(BF16)
    low_out[...] = packed_side(tokens[LOW : LOW + SIDE]).astype(BF16)
    high_out[...] = packed_side(tokens[TOP : TOP + SIDE]).astype(BF16)
    table = spread("c", tf_ref[288:576, :])
    pieces = [table[:, c * 128 : (c + 1) * 128] for c in range(3)]
    block = jnp.concatenate(pieces + [jnp.zeros((16, 128), F32)], 0).astype(BF16)
    size = tab_out.shape[1]
    for place in range(tab_out.shape[0]):
        tab_out[place] = block[place * size : (place + 1) * size, :]


def fine_kinds():
    half = query_half().astype(F32)
    rows_a, mask_a, zq_a = head_rows(HEADS_F, 6, 6, 72, 72)
    rows_b, mask_b, zq_b = head_rows(HEADS_F, 3, 6, 40, 40)
    keys_a, keys_b = (pair_keys(144, half), pair_keys(160, half))
    toep_a, toep_b = (toeplitz(keys_a, 6, 6 * half), toeplitz(keys_b, 6, 6 * half))
    mid = (rows_a, mask_a, zq_a, keys_a, toep_a, 72)
    edge = (rows_b, mask_b, zq_b, keys_b, toep_b, 40)
    return {"a": mid, "b": edge, "c": edge}


def fine_windows(zone):
    edge = zone * 40
    return (
        ("a", (MID + zone * 72, 72), [(0, MID + zone * 72, 72), (1, MID + zone * 72, 72)]),
        ("b", (TOP + edge, 40), [(0, TOP + edge, 40), (1, TOP + edge, 40), (2, edge, 40), (3, edge, 40)]),
        ("c", (LOW + edge, 40), [(4, edge, 40), (5, edge, 40), (0, LOW + edge, 40), (1, LOW + edge, 40)]),
    )


SOURCES = (0, FINE, 2 * FINE, 2 * FINE + SIDE, 2 * FINE + 2 * SIDE, 2 * FINE + 3 * SIDE)
ALL_ROWS = 2 * FINE + 4 * SIDE


def gathered(ref, pieces):
    return jnp.concatenate(
        [ref[SOURCES[source] + start : SOURCES[source] + start + count, :] for source, start, count in pieces],
        0,
    )


def fine_forward_body(
    own_ref,
    par_ref,
    upo_ref,
    upp_ref,
    dno_ref,
    dnp_ref,
    gain_ref,
    shift_ref,
    qkv_ref,
    qkv_bias_ref,
    proj_ref,
    proj_bias_ref,
    merge_gain_ref,
    merge_shift_ref,
    merge_ref,
    coarse_gain_ref,
    coarse_shift_ref,
    tf_ref,
    tp_ref,
    hat_out,
    normed,
    q_out,
    k_out,
    v_out,
    probs_a,
    probs_b,
    probs_c,
    mix_out,
    fine_out,
    merged_out,
    coarse_out,
    cnorm_out,
):
    gain, shift = (vector(gain_ref), vector(shift_ref))
    own = own_ref[...].astype(F32)
    for place, tokens in enumerate(
        [own, par_ref[...].astype(F32)]
        + [unpacked_side(ref[...].astype(F32)) for ref in (upo_ref, upp_ref, dno_ref, dnp_ref)]
    ):
        hat, _ = norm_parts(tokens)
        at = slice(SOURCES[place], SOURCES[place] + tokens.shape[0])
        hat_out[at, :] = hat
        normed[at, :] = (hat * gain + shift).astype(BF16)
    bias = vector(qkv_bias_ref)
    q_out[...] = rounded(dot(normed[0:FINE, :], qkv_ref[:, 0:C_F]) + bias[:, 0:C_F])
    k_out[...] = rounded(dot(normed[...], qkv_ref[:, C_F : 2 * C_F]) + bias[:, C_F : 2 * C_F])
    v_out[...] = rounded(dot(normed[...], qkv_ref[:, 2 * C_F :]) + bias[:, 2 * C_F :])
    tables = {
        "a": spread("a", tf_ref[0:288, :]),
        "b": spread("b", tf_ref[288:576, :]),
        "c": jnp.concatenate([tp_ref[c * 80 : (c + 1) * 80, :].astype(F32) for c in range(3)], 1),
    }
    lat = lax.axis_index("lat")
    late = along_lanes(160) >= 80
    edges = {
        "a": 0.0,
        "b": jnp.where(late & (lat == lax.axis_size("lat") - 1), NEGATIVE, 0.0),
        "c": jnp.where(jnp.logical_not(late) & (lat == 0), NEGATIVE, 0.0),
    }
    kinds = fine_kinds()
    probs_refs = {"a": probs_a, "b": probs_b, "c": probs_c}
    mixtures = {}
    for zone in range(2):
        for name, (start, count), pieces in fine_windows(zone):
            rows, mask, zq, keys, toep, block = kinds[name]
            probs_ref = probs_refs[name]
            bias = bias_rows(tables[name], toep, zone, block) + banned(keys, zq, zone) + edges[name]
            probs, mixture = attend(
                q_out[start : start + count, :],
                gathered(k_out, pieces),
                gathered(v_out, pieces),
                rows,
                mask,
                bias,
            )
            probs_ref[zone] = probs
            mixtures[name, zone] = mixture
    mixture = jnp.concatenate([mixtures[name, zone] for name in "cab" for zone in range(2)], 0)
    mix_out[...] = mixture.astype(BF16)
    attn = rounded(dot(mixture, proj_ref[...]) + vector(proj_bias_ref))
    fine = rounded(own + attn)
    fine_out[...] = fine.astype(BF16)
    quartet = dot(quartet_order(), fine)
    parts = [quartet[p * COARSE : (p + 1) * COARSE] for p in range(4)]
    hats, _ = quartet_norm(parts)
    coarse = None
    gain, shift = (vector(merge_gain_ref), vector(merge_shift_ref))
    for p in range(4):
        at = slice(p * C_F, (p + 1) * C_F)
        value = (hats[p] * gain[:, at] + shift[:, at]).astype(BF16)
        merged_out[p] = value
        part = dot(value, merge_ref[p * C_F : (p + 1) * C_F, :])
        coarse = part if coarse is None else coarse + part
    coarse = rounded(coarse)
    coarse_out[...] = coarse
    hat, _ = norm_parts(coarse)
    cnorm_out[...] = (hat * vector(coarse_gain_ref) + vector(coarse_shift_ref)).astype(BF16)


def quartet_norm(parts):
    width = 4.0 * C_F
    mean = sum(jnp.sum(part, -1, keepdims=True) for part in parts) / width
    centres = [part - mean for part in parts]
    spread = sum(jnp.sum(c * c, -1, keepdims=True) for c in centres) / width
    scale = lax.rsqrt(spread + EPS)
    return ([c * scale for c in centres], scale)


def coarse_body(
    group_ref,
    own_ref,
    coarse_ref,
    cot_ref,
    qkv_ref,
    qkv_bias_ref,
    proj_ref,
    proj_bias_ref,
    tc_ref,
    out_ref,
    parts_out,
    own_out,
    flat_out,
    table_out,
    cot_out,
    stage,
    keys,
    values,
):
    fetch_groups(stage, cot_ref)
    order = coarse_order()
    cot = dot(order, stage[...])
    cot_out[...] = cot
    bias = vector(qkv_bias_ref)
    wide = [slice(i * C_C, (i + 1) * C_C) for i in range(3)]
    queries = rounded(dot(own_ref[...], qkv_ref[:, wide[0]]) + bias[:, wide[0]])
    group = jnp.concatenate([group_ref[g] for g in range(4)], 0)
    keys[...] = rounded(dot(group, qkv_ref[:, wide[1]]) + bias[:, wide[1]])
    values[...] = rounded(dot(group, qkv_ref[:, wide[2]]) + bias[:, wide[2]])
    mixture_grad = rounded(dot_nt(cot, proj_ref[...]))
    rows, mask, zq = head_rows(HEADS_C, 6, 3, 40, 144)
    cells = group_keys()
    toep = toeplitz(cells, 3, 3 * lax.rem(lax.axis_index("lon"), 4).astype(F32))
    table_in = spread("q", tc_ref[...])
    mixtures, query_grads, grads = ([], [], [])
    for zone in range(2):
        here = slice(zone * 40, (zone + 1) * 40)
        at = [slice(g * COARSE + zone * 40, g * COARSE + zone * 40 + 40) for g in range(4)]
        k = jnp.concatenate([keys[there, :] for there in at], 0)
        v = jnp.concatenate([values[there, :] for there in at], 0)
        bias = bias_rows(table_in, toep, zone, 144) + banned(cells, zq, 0)
        probs, mixture = attend(queries[here], k, v, rows, mask, bias)
        dq, dk, dv, table = attend_back(
            queries[here], k, v, rows, mask, probs, mixture_grad[here], toep, 144
        )
        table_out[zone * 144 : (zone + 1) * 144, :] = table
        mixtures.append(mixture)
        query_grads.append(dq)
        grads.append((dk, dv))
    key_grad, value_grad = (
        rounded(
            jnp.concatenate(
                [grads[zone][i][g * 40 : (g + 1) * 40] for g in range(4) for zone in range(2)], 0
            )
        )
        for i in range(2)
    )
    query_grad = jnp.concatenate(query_grads, 0)
    part = dot_nt(key_grad, qkv_ref[:, wide[1]]) + dot_nt(value_grad, qkv_ref[:, wide[2]])
    for g in range(4):
        parts_out[g] = part[g * COARSE : (g + 1) * COARSE].astype(BF16)
    own_out[...] = dot_nt(query_grad, qkv_ref[:, wide[0]])
    for i, (norm, grad) in enumerate(
        ((own_ref[...], query_grad), (group, key_grad), (group, value_grad))
    ):
        weight = dot_tn(norm, grad)
        sums = column_sum(grad)
        for c in range(3):
            lanes = slice(c * 128, (c + 1) * 128)
            flat_out[pl.ds(3 * i + c, C_C, stride=9), :] = weight[:, lanes]
            flat_out[3456 + 3 * i + c : 3457 + 3 * i + c, :] = sums[:, lanes]
    mixture = jnp.concatenate(mixtures, 0)
    flat_store(flat_out, 3465, dot_tn(mixture, cot))
    flat_store(flat_out, 4617, column_sum(cot))
    attn = rounded(dot(mixture, proj_ref[...]) + vector(proj_bias_ref))
    stage[...] = dot_tn(order, coarse_ref[...] + attn)
    store_groups(out_ref, stage)


def flat_store(flat, start, matrix):
    height, width = matrix.shape
    step = width // 128
    for c in range(step):
        lanes = slice(c * 128, (c + 1) * 128)
        if height == 1:
            flat[start + c : start + c + 1, :] = matrix[:, lanes]
        else:
            flat[pl.ds(start + c, height, stride=step), :] = matrix[:, lanes]


def keep_square(square, matrix):
    height = matrix.shape[0]
    square[0, 0:height, :] = matrix[:, 0:128]
    square[1, 0:height, 0:64] = matrix[:, 128:192]


def every_other(square, start):
    take = pl.ds(start, 96, stride=2)
    return jnp.concatenate([square[0, take, :], square[1, take, :][:, 0:64]], 1)


def block_store(flat, start, blocks):
    for c, block in enumerate(blocks):
        if block.shape[0] == 1:
            flat[start + c : start + c + 1, :] = block
        else:
            flat[pl.ds(start + c, block.shape[0], stride=len(blocks)), :] = block


def fine_back_body(
    starts,
    rows,
    part_ref,
    own_part_ref,
    cot_ref,
    coarse_ref,
    merged_ref,
    fine_ref,
    hat_ref,
    normed_ref,
    mix_ref,
    q_ref,
    k_ref,
    v_ref,
    probs_a,
    probs_b,
    probs_c,
    qkv_ref,
    cgain_ref,
    merge_gain_ref,
    merge_ref,
    proj_ref,
    flat_c,
    table_q,
    fog_out,
    own_out,
    par_out,
    upo_out,
    upp_out,
    dno_out,
    dnp_out,
    pieces_out,
    kgrad,
    vgrad,
    flat,
    tables,
    square,
):
    norm_grad = part_ref[...] + own_part_ref[...]
    hat, scale = norm_parts(coarse_ref[...])
    flat_store(flat, 3477, column_sum(norm_grad * hat))
    flat_store(flat, 3480, column_sum(norm_grad))
    coarse_grad = rounded(cot_ref[...] + norm_back(hat, scale, norm_grad, vector(cgain_ref)))
    quartet_sel = quartet_order()
    quartet = dot(quartet_sel, fine_ref[...])
    hats, scale = quartet_norm([quartet[p * COARSE : (p + 1) * COARSE] for p in range(4)])
    inners, gains, shifts = ([], [], [])
    merge_gain = vector(merge_gain_ref)
    for p in range(4):
        at = slice(p * C_F, (p + 1) * C_F)
        flat_store(flat, 1173 + 3 * p * C_F, dot_tn(merged_ref[p], coarse_grad))
        grad = dot_nt(coarse_grad, merge_ref[at, :])
        gains.append(column_sum(grad * hats[p]))
        shifts.append(column_sum(grad))
        inners.append(grad * merge_gain[:, at])
    block_store(flat, 1161, lane_blocks(gains))
    block_store(flat, 1167, lane_blocks(shifts))
    width = 4.0 * C_F
    first = sum(jnp.sum(inner, -1, keepdims=True) for inner in inners) / width
    second = sum(jnp.sum(i * h, -1, keepdims=True) for i, h in zip(inners, hats)) / width
    grads = jnp.concatenate([scale * (i - first - h * second) for i, h in zip(inners, hats)], 0)
    high = rounded(grads)
    attn_grad = dot_tn(quartet_sel, high)
    fog_out[...] = attn_grad + dot_tn(quartet_sel, grads - high)
    mixture_grad = rounded(dot_nt(attn_grad, proj_ref[...]))
    weight = dot_tn(mix_ref[...], attn_grad)
    corner = weight[0:1]
    keep_square(square, jnp.concatenate([weight, column_sum(attn_grad)], 0))
    block_store(flat, 873, lane_blocks([every_other(square, 1), every_other(square, 2)]))
    kinds = fine_kinds()
    places = {"a": (PART_A, probs_a), "b": (PART_B, probs_b), "c": (PART_C, probs_c)}
    query_grads = {}
    for zone in range(2):
        for name, (start, count), pieces in fine_windows(zone):
            rows_at, mask, _, _, toep, block = kinds[name]
            table_at, probs_ref = places[name]
            dq, dk, dv, table = attend_back(
                q_ref[start : start + count, :],
                gathered(k_ref, pieces),
                gathered(v_ref, pieces),
                rows_at,
                mask,
                probs_ref[zone],
                mixture_grad[start : start + count],
                toep,
                block,
            )
            query_grads[name, zone] = dq
            for c in range(3):
                at = table_at + (2 * c + zone) * block
                tables[at : at + block, :] = table[:, c * 128 : (c + 1) * 128]
            at = 0
            for source, begin, size in pieces:
                to = slice(SOURCES[source] + begin, SOURCES[source] + begin + size)
                kgrad[to, :] = rounded(dk[at : at + size])
                vgrad[to, :] = rounded(dv[at : at + size])
                at += size
    query_grad = jnp.concatenate([query_grads[name, zone] for name in "cab" for zone in range(2)], 0)
    part = dot_nt(kgrad[...], qkv_ref[:, C_F : 2 * C_F]) + dot_nt(vgrad[...], qkv_ref[:, 2 * C_F :])
    own = part[0:FINE] + dot_nt(query_grad, qkv_ref[:, 0:C_F])
    own_out[...] = own
    par_out[...] = part[FINE : 2 * FINE].astype(BF16)
    for place, out in enumerate((upo_out, upp_out, dno_out, dnp_out)):
        at = SOURCES[2 + place]
        out[...] = packed_side(part[at : at + SIDE]).astype(BF16)
    hat_grad = column_sum(own * hat_ref[0:FINE, :])
    hat_grad += column_sum(part[FINE:] * hat_ref[FINE:, :])
    block_store(
        flat, 0, lane_blocks([hat_grad, column_sum(own) + column_sum(part[FINE:])])
    )
    evens, odds, sums = ([], [], [])
    for norm, grad in (
        (normed_ref[0:FINE, :], query_grad),
        (normed_ref[...], kgrad[...]),
        (normed_ref[...], vgrad[...]),
    ):
        keep_square(square, dot_tn(norm, grad))
        evens.append(every_other(square, 0))
        odds.append(every_other(square, 1))
        sums.append(column_sum(grad))
    block_store(flat, 3, lane_blocks(evens + odds))
    block_store(flat, 867, lane_blocks(sums + [corner]))
    tables[240:PART_A, :] = jnp.zeros((PART_A - 240, 128), F32)
    tables[PART_END:, :] = jnp.zeros((TABLE_ROWS - PART_END, 128), F32)
    for c in range(3):
        at = PART_Q + 288 * c
        tables[at : at + 288, :] = table_q[:, c * 128 : (c + 1) * 128]
    split = 3483
    trows = TABLE_ROWS // len(starts)
    for place, start in starts:
        end = start + rows
        if start < split:
            size = min(end, split) - start
            value = flat[start : start + size, :]
            if end > split:
                value = jnp.concatenate([value, flat_c[0 : end - split, :]], 0)
        else:
            size = min(end, 8103) - start
            value = flat_c[start - split : start - split + size, :]
            if size < rows:
                value = jnp.concatenate([value, jnp.zeros((rows - size, 128), F32)], 0)
        pieces_out[place, 0:rows, :] = value.astype(BF16)
        pieces_out[place, rows:, :] = tables[place * trows : (place + 1) * trows, :].astype(BF16)


def final_body(
    x_ref,
    gain_ref,
    fog_ref,
    own_ref,
    par_ref,
    low_ref,
    high_ref,
    t_ref,
    token_out,
    fine_out,
    coarse_out,
    stage,
    grad,
):
    grad[...] = own_ref[...] + par_ref[...].astype(F32)
    grad[LOW : LOW + SIDE, :] += unpacked_side(low_ref[...].astype(F32))
    grad[TOP : TOP + SIDE, :] += unpacked_side(high_ref[...].astype(F32))
    hat, scale = norm_parts(x_ref[...].astype(F32))
    total = fog_ref[...] + norm_back(hat, scale, rounded(grad[...]), vector(gain_ref))
    stage[...] = dot_tn(fine_order(), total)
    store_groups(token_out, stage)

    def part(start, height):
        return jnp.concatenate(
            [t_ref[start + c * height : start + (c + 1) * height, :] for c in range(3)], 1
        )

    def natural(kind, block):
        total = None
        for zk in range(2):
            term = dot_tn(table_rows(kind, zk), dot_nt(block, table_lanes(zk)))
            total = term if total is None else total + term
        return total

    fine_out[0:288, :] = natural("a", part(PART_A, 144))
    fine_out[288:576, :] = natural("b", part(PART_B, 80)) + natural("c", part(PART_C, 80))
    coarse_out[...] = natural("q", part(PART_Q, 288))


def mesh_parts(lat, lon):
    cores = 2
    xs = 4 if lon % 8 == 0 else 1
    ys = 4 if lat % 4 == 0 else lat
    return (cores, xs, lon // (cores * xs), ys, lat // ys)


def piece_rows(total, lon, ys):
    longest = -(-(127 + total // lon) // 128)
    unit = 16 * ys
    return -(-longest // unit) * unit


def reduce_body(
    dims,
    rows,
    norm_factor,
    g_ref,
    par_ref,
    upo_ref,
    upp_ref,
    dno_ref,
    dnp_ref,
    p_ref,
    t_ref,
    par_out,
    low_out,
    high_out,
    par_buf,
    up_buf,
    down_buf,
    up_sum,
    down_sum,
    low_buf,
    high_buf,
    ess,
    esr,
    m_head,
    m_tail,
    r1,
    r2,
    w2,
    r3,
    w3,
    r4,
    s5,
    r5,
    pf,
    tf,
    ts,
    tr,
    s1s,
    s1r,
    s2s,
    s2r,
    s3s,
    s3r,
    s4s,
    s4r,
    s5s,
    s5r,
    t4s,
    t4r,
    s6s,
    s6r,
    t6s,
    t6r,
    t7s,
    t7r,
    t8s,
    t8r,
):
    cores, xs, zs, ys, hs = dims
    chunk = rows // ys
    lat = lax.axis_index("lat")
    lon = lax.axis_index("lon")
    core = lax.rem(lon, cores)
    x = lax.rem(lon // cores, xs)
    z = lon // (cores * xs)
    y = lax.rem(lat, ys)
    h = lat // ys

    def lon_of(core_at, x_at, z_at):
        return (z_at * xs + x_at) * cores + core_at

    def core_peer():
        return (lat, lon_of(1 - core, x, z))

    def x_at(d):
        return lax.rem(x + d, xs)

    def z_at(d):
        return lax.rem(z + d, zs)

    def y_at(d):
        return lax.rem(y + d, ys)

    def x_peer(d):
        return (lat, lon_of(core, x_at(d), z))

    def z_peer(d):
        return (lat, lon_of(core, x, z_at(d)))

    def y_peer(d):
        return (h * ys + y_at(d), lon)

    def h_peer():
        return (lax.rem(h + 1, hs) * ys + y, lon)

    peers = [core_peer()]
    peers += [x_peer(d) for d in range(1, xs)]
    peers += [y_peer(d) for d in range(1, ys)]
    peers += [z_peer(d) for d in range(1, zs)]
    if hs > 1:
        peers.append(h_peer())
    lats = ys * hs
    before = (lax.rem(lat + lats - 1, lats), lon)
    after = (lax.rem(lat + 1, lats), lon)
    beside = (lat, partner_of(lon, cores * xs * zs))
    peers += [before, after, beside]
    barrier = pltpu.get_barrier_semaphore()
    for peer in peers:
        pl.semaphore_signal(barrier, inc=1, device_id=peer, device_id_type=MESH)
    pl.semaphore_wait(barrier, len(peers))

    send = start_copy
    edges = [
        send(upp_ref, up_buf, ess.at[0], esr.at[0], beside),
        send(dnp_ref, down_buf, ess.at[1], esr.at[1], beside),
        send(par_ref, par_buf, ess.at[2], esr.at[2], beside),
    ]
    pending = []
    order = (2, 1, 3, 0) if xs == 4 else (0,)
    cut = g_ref.shape[1] // 32 * 16
    head, tail = (pl.ds(0, cut), pl.ds(cut, g_ref.shape[1] - cut))
    first = {}
    for d in order:
        src = g_ref.at[pl.ds(((1 - core) * xs + x_at(d)) * zs, zs)]
        first[d] = send(src, r1.at[d], s1s.at[d], s1r.at[d], core_peer())
        pending.append(first[d])
    second = []

    def hop(at, src, dst, d):
        copy = send(src, dst, s2s.at[at], s2r.at[at], x_peer(d))
        pending.append(copy)
        return copy

    for d in order:
        first[d].wait_recv()
        base = (core * xs + x_at(d)) * zs

        def add_pair(i, carry):
            r1[d, i] = (
                r1[d, i].astype(jnp.float32) + g_ref[base + i].astype(jnp.float32)
            ).astype(jnp.bfloat16)
            return carry

        lax.fori_loop(0, zs, add_pair, 0)
        if d == 2:
            via_right = hop(0, r1.at[2, :, head], m_head, 1)
            via_left = hop(1, r1.at[2, :, tail], m_tail, 3)
        if d == 1:
            second.append(hop(2, r1.at[1, :, tail], r2.at[0, :, tail], 1))
        if d == 3:
            second.append(hop(3, r1.at[3, :, head], r2.at[1, :, head], 3))
    if xs == 4:
        via_right.wait_recv()

        def add_head(i, carry):
            r1[1, i, head, :] = (
                r1[1, i, head, :].astype(jnp.float32) + m_head[i].astype(jnp.float32)
            ).astype(jnp.bfloat16)
            return carry

        lax.fori_loop(0, zs, add_head, 0)
        second.append(hop(4, r1.at[1, :, head], r2.at[0, :, head], 1))
        via_left.wait_recv()

        def add_tail(i, carry):
            r1[3, i, tail, :] = (
                r1[3, i, tail, :].astype(jnp.float32) + m_tail[i].astype(jnp.float32)
            ).astype(jnp.bfloat16)
            return carry

        lax.fori_loop(0, zs, add_tail, 0)
        second.append(hop(5, r1.at[3, :, tail], r2.at[1, :, tail], 3))
    edges[0].wait_recv()
    edges[1].wait_recv()
    up_sum[...] = (upo_ref[...].astype(F32) + up_buf[...].astype(F32)).astype(BF16)
    down_sum[...] = (dno_ref[...].astype(F32) + down_buf[...].astype(F32)).astype(BF16)
    for copy in second:
        copy.wait_recv()

    def add_x(i, carry):
        total = r1[0, i].astype(jnp.float32)
        if xs == 4:
            total = total + r2[0, i].astype(jnp.float32) + r2[1, i].astype(jnp.float32)
        w2[i] = total.astype(jnp.bfloat16)
        return carry

    lax.fori_loop(0, zs, add_x, 0)

    third = []
    for d in range(1, ys):
        src = w2.at[:, pl.ds(pl.multiple_of(y_at(d) * chunk, 16), chunk)]
        copy = send(src, r3.at[d - 1], s3s.at[d - 1], s3r.at[d - 1], y_peer(d))
        third.append(copy)
        pending.append(copy)
    edges.append(send(up_sum, low_buf, ess.at[3], esr.at[3], after))
    edges.append(send(down_sum, high_buf, ess.at[4], esr.at[4], before))
    pending += edges
    for copy in third:
        copy.wait_recv()

    def add_y(i, carry):
        total = w2[i, pl.ds(pl.multiple_of(y * chunk, 16), chunk), :].astype(jnp.float32)
        for d in range(1, ys):
            total = total + r3[d - 1, i].astype(jnp.float32)
        w3[i, 0:chunk, :] = total.astype(jnp.bfloat16)
        w3[i, chunk:, :] = w2[i, rows:, :]
        return carry

    lax.fori_loop(0, zs, add_y, 0)

    fourth = []
    for d in range(1, zs):
        copy = send(w3.at[z_at(d)], r4.at[d - 1], s4s.at[d - 1], s4r.at[d - 1], z_peer(d))
        fourth.append(copy)
        pending.append(copy)
    for copy in fourth:
        copy.wait_recv()
    total = w3[z].astype(jnp.float32)
    for d in range(1, zs):
        total = total + r4[d - 1].astype(jnp.float32)

    s5[...] = total[:chunk].astype(jnp.bfloat16)
    if hs > 1:
        fifth = send(s5, r5, s5s.at[0], s5r.at[0], h_peer())
        pending.append(fifth)
    ts[...] = (total[chunk:] * norm_factor).astype(jnp.bfloat16)
    first_row = ((core * xs + x) * zs + z) * ts.shape[0]
    handed = pltpu.make_async_remote_copy(
        src_ref=ts,
        dst_ref=tr,
        send_sem=t8s.at[0],
        recv_sem=t8r.at[0],
        device_id=before,
        device_id_type=MESH,
    )
    tf[core, x, z] = ts[...]

    @pl.when(first_row < PART_A)
    def _():
        handed.start()
        handed.wait_recv()
        row = first_row + lax.broadcasted_iota(jnp.int32, ts.shape, 0)
        tf[core, x, z] = jnp.where(
            row < PART_A, tr[...].astype(jnp.float32), ts[...].astype(jnp.float32)
        ).astype(jnp.bfloat16)
        handed.wait_send()

    table_z = []
    for d in range(1, zs):
        copy = send(
            tf.at[core, x, z], tf.at[core, x, z], t4s.at[d - 1], t4r.at[d - 1], z_peer(d)
        )
        table_z.append(copy)
        pending.append(copy)
    share = s5[...].astype(jnp.float32)
    if hs > 1:
        fifth.wait_recv()
        share = share + r5[...].astype(jnp.float32)
    mine = pl.ds(pl.multiple_of(y * chunk, 8), chunk)
    pf[mine, :] = share * norm_factor
    sixth = []
    for d in range(1, ys):
        copy = send(pf.at[mine], pf.at[mine], s6s.at[d - 1], s6r.at[d - 1], y_peer(d))
        sixth.append(copy)
        pending.append(copy)
    for copy in table_z:
        copy.wait_recv()
    table_x = []
    for d in range(1, xs):
        copy = send(tf.at[core, x], tf.at[core, x], t6s.at[d - 1], t6r.at[d - 1], x_peer(d))
        table_x.append(copy)
        pending.append(copy)
    for copy in table_x:
        copy.wait_recv()
    table_core = send(tf.at[core], tf.at[core], t7s.at[0], t7r.at[0], core_peer())
    pending.append(table_core)
    for copy in sixth:
        copy.wait_recv()
    p_ref[...] = pf[...]
    for copy in edges[2:]:
        copy.wait_recv()
    par_out[...] = par_buf[...]
    low_out[...] = low_buf[...]
    high_out[...] = high_buf[...]
    table_core.wait_recv()
    t_ref[...] = tf[...]
    for copy in pending:
        copy.wait_send()


def reduce_all(pieces, edges, rows, norm_factor, dims):
    cores, xs, zs, ys, hs = dims
    height = pieces.shape[1]
    trows = height - rows
    chunk = rows // ys
    bf16 = jnp.bfloat16
    sem = pltpu.SemaphoreType.DMA
    cut = height // 32 * 16
    counts = [xs, 6, ys - 1, zs - 1, 1, zs - 1, ys - 1, xs - 1, 1, 1]
    sems = []
    for count in counts:
        sems += [sem((max(count, 1),)), sem((max(count, 1),))]
    vmem = pl.BlockSpec(memory_space=pltpu.VMEM)
    return pl.pallas_call(
        functools.partial(reduce_body, dims, rows, norm_factor),
        out_shape=(
            jax.ShapeDtypeStruct((rows, 128), jnp.float32),
            jax.ShapeDtypeStruct((cores, xs, zs, trows, 128), bf16),
            jax.ShapeDtypeStruct((FINE, C_F), bf16),
            jax.ShapeDtypeStruct((128, 128), bf16),
            jax.ShapeDtypeStruct((128, 128), bf16),
        ),
        in_specs=[vmem] * 6,
        out_specs=(vmem,) * 5,
        scratch_shapes=[pltpu.VMEM((FINE, C_F), bf16)]
        + [pltpu.VMEM((128, 128), bf16)] * 6
        + [sem((5,)), sem((5,))]
        + [pltpu.VMEM((zs, cut, 128), bf16), pltpu.VMEM((zs, height - cut, 128), bf16)]
        + [
            pltpu.VMEM((xs, zs, height, 128), bf16),
            pltpu.VMEM((2, zs, height, 128), bf16),
            pltpu.VMEM((zs, height, 128), bf16),
            pltpu.VMEM((max(ys - 1, 1), zs, chunk, 128), bf16),
            pltpu.VMEM((zs, chunk + trows, 128), bf16),
            pltpu.VMEM((max(zs - 1, 1), chunk + trows, 128), bf16),
            pltpu.VMEM((chunk, 128), bf16),
            pltpu.VMEM((chunk, 128), bf16),
            pltpu.VMEM((rows, 128), jnp.float32),
            pltpu.VMEM((cores, xs, zs, trows, 128), bf16),
            pltpu.VMEM((trows, 128), bf16),
            pltpu.VMEM((trows, 128), bf16),
        ]
        + sems,
        compiler_params=pltpu.CompilerParams(
            collective_id=7, has_side_effects=True, vmem_limit_bytes=VMEM_BYTES
        ),
        cost_estimate=lasting(45),
        name="grad_reduce",
    )(pieces, *edges)


def shards(
    tokens,
    fine_gain,
    fine_shift,
    fine_qkv,
    fine_qkv_bias,
    fine_proj,
    fine_proj_bias,
    fine_table,
    merge_gain,
    merge_shift,
    merge_weight,
    coarse_gain,
    coarse_shift,
    coarse_qkv,
    coarse_qkv_bias,
    coarse_proj,
    coarse_proj_bias,
    coarse_table,
    cotangent,
):
    lat_count, lon_count = (lax.axis_size("lat"), lax.axis_size("lon"))
    lat, lon = (lax.axis_index("lat"), lax.axis_index("lon"))
    norm_factor = 1.0 / math.sqrt(tokens.size // C_F * lat_count * lon_count / 4)
    fine_rows = fine_table.reshape(576, 138)
    coarse_rows = coarse_table.reshape(576, 138)
    cells = tokens[0].transpose(1, 2, 0, 3)
    cot_cells = cotangent[0].transpose(1, 2, 0, 3)

    group = min(8, lon_count)
    side = ((128, 128), BF16)
    own = ((FINE, C_F), BF16)
    table_part = ((group, PART_A // group, 128), BF16)
    x, low, high, table_send = call(
        prepare_body,
        [own, side, side, table_part],
        (cells, fine_rows),
        [pltpu.VMEM((288, C_F), F32)],
        "prepare",
        2,
    )
    halo = [own, side, side, side, side, table_part]
    par, upo, upp, dno, dnp, table_before = exchange_call(
        halo_body,
        halo,
        (x, low, high, table_send),
        [pltpu.VMEM(*s) for s in halo],
        (6, max(group - 1, 1)),
        1,
        "halo",
        10,
    )
    (
        hat,
        normed,
        q,
        k,
        v,
        probs_a,
        probs_b,
        probs_c,
        mixture,
        fine_out,
        merged,
        coarse,
        cnorm,
    ) = call(
        fine_forward_body,
        [
            ((ALL_ROWS, C_F), F32),
            ((ALL_ROWS, C_F), BF16),
            ((FINE, C_F), F32),
            ((ALL_ROWS, C_F), F32),
            ((ALL_ROWS, C_F), F32),
            ((2, 432, 144), F32),
            ((2, 240, 160), F32),
            ((2, 240, 160), F32),
            own,
            own,
            ((4, COARSE, C_F), BF16),
            ((COARSE, C_C), F32),
            ((COARSE, C_C), BF16),
        ],
        (
            x,
            par,
            upo,
            upp,
            dno,
            dnp,
            fine_gain,
            fine_shift,
            fine_qkv,
            fine_qkv_bias,
            fine_proj,
            fine_proj_bias,
            merge_gain,
            merge_shift,
            merge_weight,
            coarse_gain,
            coarse_shift,
            fine_rows,
            table_before.reshape(PART_A, 128),
        ),
        (),
        "fine_forward",
        10,
    )
    gathered_to = [((4, COARSE, C_C), BF16)]
    (gathered_norm,) = exchange_call(
        group_body, gathered_to, (cnorm,), [pltpu.VMEM(*gathered_to[0])], (3,), 2, "coarse_gather", 5
    )
    coarse_out, parts, own_part, flat_c, table_q, cot = call(
        coarse_body,
        [
            ((6, 3, 4, C_C), BF16),
            ((4, COARSE, C_C), BF16),
            ((COARSE, C_C), F32),
            ((4620, 128), F32),
            ((288, 384), F32),
            ((COARSE, C_C), F32),
        ],
        (
            gathered_norm,
            cnorm,
            coarse,
            cot_cells,
            coarse_qkv,
            coarse_qkv_bias,
            coarse_proj,
            coarse_proj_bias,
            coarse_rows,
        ),
        [
            pltpu.VMEM((72, C_C), F32),
            pltpu.VMEM((4 * COARSE, C_C), F32),
            pltpu.VMEM((4 * COARSE, C_C), F32),
        ],
        "coarse_attention",
        7,
    )
    (norm_part,) = exchange_call(
        ungroup_body,
        [((COARSE, C_C), F32)],
        (parts,),
        [pltpu.VMEM((3, COARSE, C_C), BF16)],
        (3,),
        3,
        "coarse_scatter",
        5,
    )
    dims = mesh_parts(lat_count, lon_count)
    cores, xs, zs, ys, hs = dims
    segment = PARAMS // lon_count
    rows = piece_rows(PARAMS, lon_count, ys)
    starts = []
    for index in range(lon_count):
        core, x_at, z_at = (index % cores, index // cores % xs, index // (cores * xs))
        starts.append(((core * xs + x_at) * zs + z_at, index * segment // 128))
    trows = TABLE_ROWS // lon_count
    fine_out_grad, own_grad, par_grad, upo_grad, upp_grad, dno_grad, dnp_grad, pieces = call(
        functools.partial(fine_back_body, starts, rows),
        [
            ((FINE, C_F), F32),
            ((FINE, C_F), F32),
            own,
            side,
            side,
            side,
            side,
            ((lon_count, rows + trows, 128), BF16),
        ],
        (
            norm_part,
            own_part,
            cot,
            coarse,
            merged,
            fine_out,
            hat,
            normed,
            mixture,
            q,
            k,
            v,
            probs_a,
            probs_b,
            probs_c,
            fine_qkv,
            coarse_gain,
            merge_gain,
            merge_weight,
            fine_proj,
            flat_c,
            table_q,
        ),
        [
            pltpu.VMEM((ALL_ROWS, C_F), F32),
            pltpu.VMEM((ALL_ROWS, C_F), F32),
            pltpu.VMEM((3488, 128), F32),
            pltpu.VMEM((TABLE_ROWS, 128), F32),
            pltpu.VMEM((2, 200, 128), F32),
        ],
        "fine_backward",
        9,
    )
    owned, table_sum, par_back, low_back, high_back = reduce_all(
        pieces, (par_grad, upo_grad, upp_grad, dno_grad, dnp_grad), rows, norm_factor, dims
    )
    shift = lax.rem(lon * segment, 128)
    param_grads = lax.dynamic_slice(owned.reshape(-1), (shift,), (segment,))
    token_grad, fine_total, coarse_total = call(
        final_body,
        [((12, 6, 4, C_F), BF16), ((576, 138), F32), ((576, 138), F32)],
        (
            x,
            fine_gain,
            fine_out_grad,
            own_grad,
            par_back,
            low_back,
            high_back,
            table_sum.reshape(TABLE_ROWS, 128),
        ),
        [pltpu.VMEM((288, C_F), F32), pltpu.VMEM((FINE, C_F), F32)],
        "final",
        2,
    )
    return (
        coarse_out.transpose(2, 0, 1, 3)[None],
        token_grad.transpose(2, 0, 1, 3)[None],
        param_grads,
        fine_total.reshape(2, -1),
        coarse_total.reshape(2, -1),
    )


def solution(mesh):
    tiles = P(None, None, "lat", "lon", None)
    whole = P()
    rows = P("lat", None)
    return jax.shard_map(
        shards,
        mesh=mesh,
        in_specs=(tiles,) + (whole,) * 6 + (rows,) + (whole,) * 9 + (rows, tiles),
        out_specs=(tiles, tiles, P("lon"), rows, rows),
        check_vma=False,
    )
```

```python
import functools
import math

import jax
import jax.numpy as jnp
from jax import lax
from jax.experimental import pallas as pl
from jax.experimental.pallas import tpu as pltpu
from jax.sharding import PartitionSpec as P

HEAD = 32
HEADS_F = 6
HEADS_C = 12
C_F = 192
C_C = 384
SPAN = 23
EPS = 1e-05
NEGATIVE = -1e30
MESH = pl.DeviceIdType.MESH
F32 = jnp.float32
BF16 = jnp.bfloat16
MIB = 1024 * 1024
VMEM_BYTES = 28 * MIB

LOW, MID, TOP = (0, 80, 224)
PARAMS = 1037184
TABLE_ROWS = 2048
FINE = 304
SIDE = 80
COARSE = 80
PART_C, PART_A, PART_B, PART_Q, PART_END = (0, 256, 688, 928, 1792)


def whole(x, n):
    return jnp.floor((x + 0.5) * (1.0 / n))


def rest(x, n):
    return x - n * whole(x, n)


def down_rows(n):
    return lax.broadcasted_iota(jnp.int32, (n, 1), 0).astype(F32)


def along_lanes(n):
    return lax.broadcasted_iota(jnp.int32, (1, n), 1).astype(F32)


def match(a, b):
    return jnp.where(a == b, 1.0, 0.0).astype(BF16)


def fine_row(zone, zq, row, col):
    low = LOW + zone * 40 + (zq * 3 + row) * 6 + col
    mid = MID + zone * 72 + (zq * 6 + row - 3) * 6 + col
    top = TOP + zone * 40 + (zq * 3 + row - 9) * 6 + col
    return jnp.where(row < 3, low, jnp.where(row < 9, mid, top))


def fine_order():
    at = down_rows(FINE)
    low, top = (at < MID, at >= TOP)
    edge = jnp.where(top, at - TOP, at)
    mid = at - MID
    in_edge = low | top
    part = rest(edge, 40)
    zone = jnp.where(in_edge, whole(edge, 40), whole(mid, 72))
    zq = jnp.where(in_edge, whole(part, 18), whole(rest(mid, 72), 36))
    row = jnp.where(
        in_edge,
        whole(rest(part, 18), 6) + jnp.where(top, 9.0, 0.0),
        3 + whole(rest(mid, 36), 6),
    )
    col = jnp.where(in_edge, rest(part, 6), rest(mid, 6))
    code = (row * 6 + col) * 4 + rest(2 * zone + zq + 1, 4)
    return match(jnp.where(in_edge & (part >= 36), -1.0, code), along_lanes(288))


def coarse_place(at):
    part = rest(at, 40)
    return (whole(at, 40), whole(part, 18), whole(rest(part, 18), 3), rest(part, 3), part < 36)


def coarse_order():
    zone, zq, row, col, valid = coarse_place(down_rows(COARSE))
    code = (row * 3 + col) * 4 + 2 * zone + zq
    return match(jnp.where(valid, code, -1.0), along_lanes(72))


def quartet_order():
    at = down_rows(4 * COARSE)
    p = whole(at, COARSE)
    zone, zq, row, col, valid = coarse_place(rest(at, COARSE))
    rolled = rest(2 * zone + zq + 3, 4)
    source = fine_row(
        whole(rolled, 2), rest(rolled, 2), 2 * row + rest(p, 2), 2 * col + whole(p, 2)
    )
    return match(jnp.where(valid, source, -1.0), along_lanes(FINE))


def head_rows(heads, lats, cols, tokens, block):
    at = down_rows(block * cols)
    part = rest(at, block)
    h = whole(part, 2 * lats)
    zq = whole(rest(part, 2 * lats), lats)
    code = (zq * lats + rest(part, lats)) * cols + whole(at, block)
    valid = part < heads * 2 * lats
    head = jnp.where(valid, h, -1.0)
    mask = match(head, whole(along_lanes(heads * HEAD), HEAD)).astype(F32)
    return (match(jnp.where(valid, code, -1.0), along_lanes(tokens)), mask, zq)


def pair_keys(size, half):
    u = along_lanes(size)
    if size == 144:
        source, part = (whole(u, 72), rest(u, 72))
        zk, ak, valid = (whole(part, 36), whole(rest(part, 36), 6), part >= 0)
    else:
        slot, part = (whole(u, 40), rest(u, 40))
        source = rest(slot, 2)
        zk = whole(part, 18)
        ak = 3 * whole(slot, 2) + whole(rest(part, 18), 6)
        valid = part < 36
    return (zk, ak, rest(part, 6) + 6 * jnp.abs(half - source), valid)


def group_keys():
    u = along_lanes(160)
    part = rest(u, 40)
    zk, ak = (whole(part, 18), whole(rest(part, 18), 3))
    return (zk, ak, rest(part, 3) + 3 * whole(u, 40), part < 36)


def toeplitz(keys, cols, shift):
    zk, ak, col, valid = keys
    at = down_rows(384)
    tail = at >= 256
    level = jnp.where(tail, whole(at - 256, 64), whole(at, 128))
    entry = jnp.where(tail, 128 + rest(at, 64), rest(at, 128))
    code = (level * 6 + whole(entry, SPAN)) * 64 + rest(entry, SPAN)
    code = jnp.where(entry < 138, code, -1.0)
    key_code = jnp.where(valid, (zk * 6 + ak) * 64 - col + shift + 11, -100.0)
    return [match(code, key_code + oq) for oq in range(cols)]


def table_lanes(zk):
    entry = down_rows(138)
    return match(
        jnp.where(entry < 128, zk * 128 + entry, 256 + zk * 64 + entry - 128), along_lanes(384)
    )


def table_rows(kind, zk):
    if kind == "q":
        at = down_rows(288)
        part = rest(at, 144)
        aq = rest(part, 6)
        lead = (whole(aq, 3) * 2 + whole(at, 144)) * HEADS_C + whole(part, 12)
        zq = whole(rest(part, 12), 6)
        return match(((lead * 2 + zq) * 2 + zk) * 3 + rest(aq, 3), along_lanes(576))
    if kind == "a":
        at, block, lats, first = (down_rows(144), 72, 6, 0)
    else:
        at, block, lats, first = (down_rows(80), 40, 3, 3 if kind == "c" else 0)
    part = rest(at, block)
    lead = whole(at, block) * HEADS_F + whole(part, 2 * lats)
    zq = whole(rest(part, 2 * lats), lats)
    code = ((lead * 2 + zq) * 2 + zk) * 6 + rest(part, lats) + first
    return match(jnp.where(part < 12 * lats, code, -1.0), along_lanes(288))


def dot(a, b):
    return jnp.dot(a.astype(BF16), b.astype(BF16), preferred_element_type=F32)


def dot_nt(a, b):
    return lax.dot_general(
        a.astype(BF16), b.astype(BF16), (((1,), (1,)), ((), ())), preferred_element_type=F32
    )


def dot_tn(a, b):
    return lax.dot_general(
        a.astype(BF16), b.astype(BF16), (((0,), (0,)), ((), ())), preferred_element_type=F32
    )


def rounded(value):
    return value.astype(BF16).astype(F32)


def norm_parts(volume):
    centre = volume - jnp.mean(volume, -1, keepdims=True)
    spread = jnp.mean(centre * centre, -1, keepdims=True)
    scale = lax.rsqrt(spread + EPS)
    return (centre * scale, scale)


def norm_back(hat, scale, grad, gain):
    inner = grad * gain
    return scale * (
        inner
        - jnp.mean(inner, -1, keepdims=True)
        - hat * jnp.mean(inner * hat, -1, keepdims=True)
    )


def column_sum(value):
    return jnp.sum(value, 0, keepdims=True)


def attend(queries, keys, values, rows, mask, bias):
    packed = dot(rows, queries) * mask
    scores = dot_nt(packed, keys) * HEAD ** (-0.5) + bias
    weights = jnp.exp(scores - jnp.max(scores, -1, keepdims=True))
    probs = weights / jnp.sum(weights, -1, keepdims=True)
    mixture = dot(probs, values) * mask
    return (probs, dot_tn(rows, mixture))


def attend_back(queries, keys, values, rows, mask, probs, mixture_grad, toep, block):
    factor = HEAD ** (-0.5)
    packed = dot(rows, queries) * mask
    grad = dot(rows, mixture_grad) * mask
    value_grad = dot_tn(probs, grad)
    prob_grad = dot_nt(grad, values)
    score_grad = probs * (prob_grad - jnp.sum(prob_grad * probs, -1, keepdims=True))
    query_grad = dot_tn(rows, dot(score_grad, keys) * factor * mask)
    key_grad = dot_tn(score_grad, packed) * factor
    table = None
    for oq, select in enumerate(toep):
        part = dot_nt(score_grad[oq * block : (oq + 1) * block], select)
        table = part if table is None else table + part
    return (query_grad, key_grad, value_grad, table)


def lasting(micros):
    return pl.CostEstimate(flops=int(micros * 2.0e9), bytes_accessed=int(micros * 3.69e6), transcendentals=int(micros * 1e6))


def call(body, outs, args, scratch, name, micros, in_place=(), limit=VMEM_BYTES):
    vmem = pl.BlockSpec(memory_space=pltpu.VMEM)
    away = pl.BlockSpec(memory_space=pltpu.HBM)
    return pl.pallas_call(
        body,
        out_shape=tuple(jax.ShapeDtypeStruct(shape, dtype) for shape, dtype in outs),
        in_specs=[away if at in in_place else vmem for at in range(len(args))],
        out_specs=(vmem,) * len(outs),
        scratch_shapes=list(scratch),
        compiler_params=pltpu.CompilerParams(vmem_limit_bytes=limit),
        cost_estimate=lasting(micros),
        name=name,
    )(*args)


def vector(ref):
    return ref[...].reshape(1, -1)


def query_half():
    return 1 - lax.rem(lax.axis_index("lon"), 2)


def packed_side(value):
    tail = jnp.concatenate([value[0:40, 128:192], value[40:80, 128:192]], 1)
    return jnp.concatenate([value[:, 0:128], tail, jnp.zeros((8, 128), value.dtype)], 0)


def unpacked_side(block):
    tail = jnp.concatenate([block[80:120, 0:64], block[80:120, 64:128]], 0)
    return jnp.concatenate([block[0:80, :], tail], 1)


def lane_blocks(pieces):
    blocks = []
    for a, b in zip(pieces[::2], pieces[1::2]):
        blocks += [a[:, 0:128], jnp.concatenate([a[:, 128:192], b[:, 0:64]], 1), b[:, 64:192]]
    return blocks


def partner_of(lon, count):
    odd = lax.rem(lon, 2)
    return lax.rem(lon + 2 * odd - 1 + count, count)


def ring_positions():
    lat_count, lon_count = (lax.axis_size("lat"), lax.axis_size("lon"))
    lat, lon = (lax.axis_index("lat"), lax.axis_index("lon"))
    up = lax.rem(lat + 1, lat_count)
    down = lax.rem(lat + lat_count - 1, lat_count)
    return (lat, lon, up, down, partner_of(lon, lon_count))


def meet(peers):
    barrier = pltpu.get_barrier_semaphore()
    for peer in peers:
        pl.semaphore_signal(barrier, inc=1, device_id=peer, device_id_type=MESH)
    pl.semaphore_wait(barrier, len(peers))


def start_copy(src, dst, send_sem, recv_sem, peer):
    copy = pltpu.make_async_remote_copy(
        src_ref=src,
        dst_ref=dst,
        send_sem=send_sem,
        recv_sem=recv_sem,
        device_id=peer,
        device_id_type=MESH,
    )
    copy.start()
    return copy


def exchange(sends, send_sems, recv_sems):
    copies = []
    for at, (src, dst, peer) in enumerate(sends):
        copies.append(start_copy(src, dst, send_sems.at[at], recv_sems.at[at], peer))
    for copy in copies:
        copy.wait_recv()
    for copy in copies:
        copy.wait_send()


def exchange_call(body, outs, args, scratch, counts, collective_id, name, micros):
    vmem = pl.BlockSpec(memory_space=pltpu.VMEM)
    sem = pltpu.SemaphoreType.DMA
    return pl.pallas_call(
        body,
        out_shape=tuple(jax.ShapeDtypeStruct(shape, dtype) for shape, dtype in outs),
        in_specs=[vmem] * len(args),
        out_specs=(vmem,) * len(outs),
        scratch_shapes=list(scratch) + [sem((count,)) for count in counts for _ in range(2)],
        compiler_params=pltpu.CompilerParams(
            collective_id=collective_id, has_side_effects=True, vmem_limit_bytes=VMEM_BYTES
        ),
        cost_estimate=lasting(micros),
        name=name,
    )(*args)


def halo_body(x_ref, low_ref, high_ref, tab_ref, *refs):
    outs, bufs, (ss, rs, ts, tr) = (refs[:6], refs[6:12], refs[12:])
    par, upo, upp, dno, dnp, tab = bufs
    lat, lon, up, down, partner = ring_positions()
    size = tab.shape[0]
    rank = lax.rem(lon, size)
    others = [lax.rem(rank + d, size) for d in range(1, size)]
    near = [(lat, lon - rank + other) for other in others]
    beside = (lat, partner)
    meet([beside, (up, lon), (down, lon)] + near)
    x_copy = start_copy(x_ref, par, ss.at[0], rs.at[0], beside)
    low_copy = start_copy(low_ref, upo, ss.at[1], rs.at[1], (down, lon))
    high_copy = start_copy(high_ref, dno, ss.at[2], rs.at[2], (up, lon))
    table_copy = start_copy(tab_ref.at[rank], tab.at[rank], ss.at[3], rs.at[3], (up, lon))
    copies = [x_copy, low_copy, high_copy, table_copy]
    low_copy.wait_recv()
    relays = [start_copy(upo, upp, ss.at[4], rs.at[4], beside)]
    high_copy.wait_recv()
    relays.append(start_copy(dno, dnp, ss.at[5], rs.at[5], beside))
    table_copy.wait_recv()
    for d, peer in enumerate(near):
        relays.append(start_copy(tab.at[rank], tab.at[rank], ts.at[d], tr.at[d], peer))
    x_copy.wait_recv()
    for copy in relays:
        copy.wait_recv()
    for copy in copies + relays:
        copy.wait_send()
    for out, buf in zip(outs, bufs):
        out[...] = buf[...]


def group_body(own_ref, out_ref, buf, ss, rs):
    lat, lon = (lax.axis_index("lat"), lax.axis_index("lon"))
    place = lax.rem(lon, 4)
    others = [lax.rem(place + d, 4) for d in range(1, 4)]
    peers = [(lat, lon - place + other) for other in others]
    meet(peers)
    buf[place] = own_ref[...]
    exchange([(own_ref, buf.at[place], peer) for peer in peers], ss, rs)
    out_ref[...] = buf[...]


def ungroup_body(parts_ref, out_ref, buf, ss, rs):
    lat, lon = (lax.axis_index("lat"), lax.axis_index("lon"))
    place = lax.rem(lon, 4)
    others = [lax.rem(place + d, 4) for d in range(1, 4)]
    peers = [(lat, lon - place + other) for other in others]
    meet(peers)
    exchange(
        [(parts_ref.at[other], buf.at[d], peers[d]) for d, other in enumerate(others)], ss, rs
    )
    total = parts_ref[place].astype(F32)
    for d in range(3):
        total = total + buf[d].astype(F32)
    out_ref[...] = total


def spread(kind, table):
    total = None
    for zk in range(2):
        part = dot(dot(table_rows(kind, zk), table), table_lanes(zk))
        total = part if total is None else total + part
    return total


def bias_rows(table, toep, zone, block):
    rows = table[zone * block : (zone + 1) * block]
    return jnp.concatenate([dot(rows, select) for select in toep], 0)


def banned(keys, zq, zone):
    ban = jnp.where(keys[3], 0.0, NEGATIVE)
    if zone == 1:
        ban = ban + jnp.where(zq == keys[0], 0.0, NEGATIVE)
    return ban


def fetch_groups(stage, ref):
    rows, cols = ref.shape[:2]
    for row in range(rows):
        for col in range(cols):
            at = (row * cols + col) * 4
            stage[at : at + 4, :] = ref[row, col].astype(F32)


def store_groups(ref, stage):
    rows, cols = ref.shape[:2]
    for row in range(rows):
        for col in range(cols):
            at = (row * cols + col) * 4
            ref[row, col] = stage[at : at + 4, :].astype(BF16)


def prepare_body(x_ref, tf_ref, own_out, low_out, high_out, tab_out, stage):
    fetch_groups(stage, x_ref)
    tokens = dot(fine_order(), stage[...])
    own_out[...] = tokens.astype(BF16)
    low_out[...] = packed_side(tokens[LOW : LOW + SIDE]).astype(BF16)
    high_out[...] = packed_side(tokens[TOP : TOP + SIDE]).astype(BF16)
    table = spread("c", tf_ref[288:576, :])
    pieces = [table[:, c * 128 : (c + 1) * 128] for c in range(3)]
    block = jnp.concatenate(pieces + [jnp.zeros((16, 128), F32)], 0).astype(BF16)
    size = tab_out.shape[1]
    for place in range(tab_out.shape[0]):
        tab_out[place] = block[place * size : (place + 1) * size, :]


def fine_kinds():
    half = query_half().astype(F32)
    rows_a, mask_a, zq_a = head_rows(HEADS_F, 6, 6, 72, 72)
    rows_b, mask_b, zq_b = head_rows(HEADS_F, 3, 6, 40, 40)
    keys_a, keys_b = (pair_keys(144, half), pair_keys(160, half))
    toep_a, toep_b = (toeplitz(keys_a, 6, 6 * half), toeplitz(keys_b, 6, 6 * half))
    mid = (rows_a, mask_a, zq_a, keys_a, toep_a, 72)
    edge = (rows_b, mask_b, zq_b, keys_b, toep_b, 40)
    return {"a": mid, "b": edge, "c": edge}


def bias_body(tf_ref, tp_ref, tc_ref, out_a, out_b, out_c, out_q):
    tables = {
        "a": spread("a", tf_ref[0:288, :]),
        "b": spread("b", tf_ref[288:576, :]),
        "c": jnp.concatenate([tp_ref[c * 80 : (c + 1) * 80, :].astype(F32) for c in range(3)], 1),
    }
    lat = lax.axis_index("lat")
    late = along_lanes(160) >= 80
    edges = {
        "a": 0.0,
        "b": jnp.where(late & (lat == lax.axis_size("lat") - 1), NEGATIVE, 0.0),
        "c": jnp.where(jnp.logical_not(late) & (lat == 0), NEGATIVE, 0.0),
    }
    kinds = fine_kinds()
    for name, out in (("a", out_a), ("b", out_b), ("c", out_c)):
        _, _, zq, keys, toep, block = kinds[name]
        for zone in range(2):
            terms = bias_rows(tables[name], toep, zone, block)
            out[zone] = terms + banned(keys, zq, zone) + edges[name]
    _, _, zq = head_rows(HEADS_C, 6, 3, 40, 144)
    cells = group_keys()
    toep = toeplitz(cells, 3, 3 * lax.rem(lax.axis_index("lon"), 4).astype(F32))
    table = spread("q", tc_ref[...])
    for zone in range(2):
        out_q[zone] = bias_rows(table, toep, zone, 144) + banned(cells, zq, 0)


def fine_windows(zone):
    edge = zone * 40
    return (
        ("a", (MID + zone * 72, 72), [(0, MID + zone * 72, 72), (1, MID + zone * 72, 72)]),
        ("b", (TOP + edge, 40), [(0, TOP + edge, 40), (1, TOP + edge, 40), (2, edge, 40), (3, edge, 40)]),
        ("c", (LOW + edge, 40), [(4, edge, 40), (5, edge, 40), (0, LOW + edge, 40), (1, LOW + edge, 40)]),
    )


SOURCES = (0, FINE, 2 * FINE, 2 * FINE + SIDE, 2 * FINE + 2 * SIDE, 2 * FINE + 3 * SIDE)
ALL_ROWS = 2 * FINE + 4 * SIDE


def gathered(ref, pieces):
    return jnp.concatenate(
        [ref[SOURCES[source] + start : SOURCES[source] + start + count, :] for source, start, count in pieces],
        0,
    )


def fine_forward_body(
    own_ref,
    par_ref,
    upo_ref,
    upp_ref,
    dno_ref,
    dnp_ref,
    gain_ref,
    shift_ref,
    qkv_ref,
    qkv_bias_ref,
    proj_ref,
    proj_bias_ref,
    merge_gain_ref,
    merge_shift_ref,
    merge_ref,
    coarse_gain_ref,
    coarse_shift_ref,
    bias_a,
    bias_b,
    bias_c,
    hat_out,
    normed,
    q_out,
    k_out,
    v_out,
    probs_a,
    probs_b,
    probs_c,
    mix_out,
    fine_out,
    merged_out,
    coarse_out,
    cnorm_out,
):
    gain, shift = (vector(gain_ref), vector(shift_ref))
    own = own_ref[...].astype(F32)
    for place, tokens in enumerate(
        [own, par_ref[...].astype(F32)]
        + [unpacked_side(ref[...].astype(F32)) for ref in (upo_ref, upp_ref, dno_ref, dnp_ref)]
    ):
        hat, _ = norm_parts(tokens)
        at = slice(SOURCES[place], SOURCES[place] + tokens.shape[0])
        hat_out[at, :] = hat
        normed[at, :] = (hat * gain + shift).astype(BF16)
    bias = vector(qkv_bias_ref)
    q_out[...] = rounded(dot(normed[0:FINE, :], qkv_ref[:, 0:C_F]) + bias[:, 0:C_F])
    k_out[...] = rounded(dot(normed[...], qkv_ref[:, C_F : 2 * C_F]) + bias[:, C_F : 2 * C_F])
    v_out[...] = rounded(dot(normed[...], qkv_ref[:, 2 * C_F :]) + bias[:, 2 * C_F :])
    kinds = fine_kinds()
    probs_refs = {"a": (bias_a, probs_a), "b": (bias_b, probs_b), "c": (bias_c, probs_c)}
    mixtures = {}
    for zone in range(2):
        for name, (start, count), pieces in fine_windows(zone):
            rows, mask = kinds[name][:2]
            bias_ref, probs_ref = probs_refs[name]
            probs, mixture = attend(
                q_out[start : start + count, :],
                gathered(k_out, pieces),
                gathered(v_out, pieces),
                rows,
                mask,
                bias_ref[zone],
            )
            probs_ref[zone] = probs
            mixtures[name, zone] = mixture
    mixture = jnp.concatenate([mixtures[name, zone] for name in "cab" for zone in range(2)], 0)
    mix_out[...] = mixture.astype(BF16)
    attn = rounded(dot(mixture, proj_ref[...]) + vector(proj_bias_ref))
    fine = rounded(own + attn)
    fine_out[...] = fine.astype(BF16)
    quartet = dot(quartet_order(), fine)
    parts = [quartet[p * COARSE : (p + 1) * COARSE] for p in range(4)]
    hats, _ = quartet_norm(parts)
    coarse = None
    gain, shift = (vector(merge_gain_ref), vector(merge_shift_ref))
    for p in range(4):
        at = slice(p * C_F, (p + 1) * C_F)
        value = (hats[p] * gain[:, at] + shift[:, at]).astype(BF16)
        merged_out[p] = value
        part = dot(value, merge_ref[p * C_F : (p + 1) * C_F, :])
        coarse = part if coarse is None else coarse + part
    coarse = rounded(coarse)
    coarse_out[...] = coarse
    hat, _ = norm_parts(coarse)
    cnorm_out[...] = (hat * vector(coarse_gain_ref) + vector(coarse_shift_ref)).astype(BF16)


def quartet_norm(parts):
    width = 4.0 * C_F
    mean = sum(jnp.sum(part, -1, keepdims=True) for part in parts) / width
    centres = [part - mean for part in parts]
    spread = sum(jnp.sum(c * c, -1, keepdims=True) for c in centres) / width
    scale = lax.rsqrt(spread + EPS)
    return ([c * scale for c in centres], scale)


def coarse_body(
    group_ref,
    own_ref,
    coarse_ref,
    cot_ref,
    qkv_ref,
    qkv_bias_ref,
    proj_ref,
    proj_bias_ref,
    bias_ref,
    out_ref,
    parts_out,
    own_out,
    flat_out,
    table_out,
    cot_out,
    stage,
    keys,
    values,
):
    fetch_groups(stage, cot_ref)
    order = coarse_order()
    cot = dot(order, stage[...])
    cot_out[...] = cot
    bias = vector(qkv_bias_ref)
    wide = [slice(i * C_C, (i + 1) * C_C) for i in range(3)]
    queries = rounded(dot(own_ref[...], qkv_ref[:, wide[0]]) + bias[:, wide[0]])
    group = jnp.concatenate([group_ref[g] for g in range(4)], 0)
    keys[...] = rounded(dot(group, qkv_ref[:, wide[1]]) + bias[:, wide[1]])
    values[...] = rounded(dot(group, qkv_ref[:, wide[2]]) + bias[:, wide[2]])
    mixture_grad = rounded(dot_nt(cot, proj_ref[...]))
    rows, mask, _ = head_rows(HEADS_C, 6, 3, 40, 144)
    toep = toeplitz(group_keys(), 3, 3 * lax.rem(lax.axis_index("lon"), 4).astype(F32))
    mixtures, query_grads, grads = ([], [], [])
    for zone in range(2):
        here = slice(zone * 40, (zone + 1) * 40)
        at = [slice(g * COARSE + zone * 40, g * COARSE + zone * 40 + 40) for g in range(4)]
        k = jnp.concatenate([keys[there, :] for there in at], 0)
        v = jnp.concatenate([values[there, :] for there in at], 0)
        probs, mixture = attend(queries[here], k, v, rows, mask, bias_ref[zone])
        dq, dk, dv, table = attend_back(
            queries[here], k, v, rows, mask, probs, mixture_grad[here], toep, 144
        )
        table_out[zone * 144 : (zone + 1) * 144, :] = table
        mixtures.append(mixture)
        query_grads.append(dq)
        grads.append((dk, dv))
    key_grad, value_grad = (
        rounded(
            jnp.concatenate(
                [grads[zone][i][g * 40 : (g + 1) * 40] for g in range(4) for zone in range(2)], 0
            )
        )
        for i in range(2)
    )
    query_grad = jnp.concatenate(query_grads, 0)
    part = dot_nt(key_grad, qkv_ref[:, wide[1]]) + dot_nt(value_grad, qkv_ref[:, wide[2]])
    for g in range(4):
        parts_out[g] = part[g * COARSE : (g + 1) * COARSE].astype(BF16)
    own_out[...] = dot_nt(query_grad, qkv_ref[:, wide[0]])
    for i, (norm, grad) in enumerate(
        ((own_ref[...], query_grad), (group, key_grad), (group, value_grad))
    ):
        weight = dot_tn(norm, grad)
        sums = column_sum(grad)
        for c in range(3):
            lanes = slice(c * 128, (c + 1) * 128)
            flat_out[pl.ds(3 * i + c, C_C, stride=9), :] = weight[:, lanes]
            flat_out[3456 + 3 * i + c : 3457 + 3 * i + c, :] = sums[:, lanes]
    mixture = jnp.concatenate(mixtures, 0)
    flat_store(flat_out, 3465, dot_tn(mixture, cot))
    flat_store(flat_out, 4617, column_sum(cot))
    attn = rounded(dot(mixture, proj_ref[...]) + vector(proj_bias_ref))
    stage[...] = dot_tn(order, coarse_ref[...] + attn)
    store_groups(out_ref, stage)


def flat_store(flat, start, matrix):
    height, width = matrix.shape
    step = width // 128
    for c in range(step):
        lanes = slice(c * 128, (c + 1) * 128)
        if height == 1:
            flat[start + c : start + c + 1, :] = matrix[:, lanes]
        else:
            flat[pl.ds(start + c, height, stride=step), :] = matrix[:, lanes]


def keep_square(square, matrix):
    height = matrix.shape[0]
    square[0, 0:height, :] = matrix[:, 0:128]
    square[1, 0:height, 0:64] = matrix[:, 128:192]


def every_other(square, start):
    take = pl.ds(start, 96, stride=2)
    return jnp.concatenate([square[0, take, :], square[1, take, :][:, 0:64]], 1)


def block_store(flat, start, blocks):
    for c, block in enumerate(blocks):
        if block.shape[0] == 1:
            flat[start + c : start + c + 1, :] = block
        else:
            flat[pl.ds(start + c, block.shape[0], stride=len(blocks)), :] = block


def fine_back_body(
    starts,
    rows,
    part_ref,
    own_part_ref,
    cot_ref,
    coarse_ref,
    merged_ref,
    fine_ref,
    hat_ref,
    normed_ref,
    mix_ref,
    q_ref,
    k_ref,
    v_ref,
    probs_a,
    probs_b,
    probs_c,
    qkv_ref,
    cgain_ref,
    merge_gain_ref,
    merge_ref,
    proj_ref,
    flat_c,
    table_q,
    fog_out,
    own_out,
    par_out,
    upo_out,
    upp_out,
    dno_out,
    dnp_out,
    pieces_out,
    tables_out,
    kgrad,
    vgrad,
    flat,
    tables,
    square,
):
    norm_grad = part_ref[...] + own_part_ref[...]
    hat, scale = norm_parts(coarse_ref[...])
    flat_store(flat, 3477, column_sum(norm_grad * hat))
    flat_store(flat, 3480, column_sum(norm_grad))
    coarse_grad = rounded(cot_ref[...] + norm_back(hat, scale, norm_grad, vector(cgain_ref)))
    quartet_sel = quartet_order()
    quartet = dot(quartet_sel, fine_ref[...])
    hats, scale = quartet_norm([quartet[p * COARSE : (p + 1) * COARSE] for p in range(4)])
    inners, gains, shifts = ([], [], [])
    merge_gain = vector(merge_gain_ref)
    for p in range(4):
        at = slice(p * C_F, (p + 1) * C_F)
        flat_store(flat, 1173 + 3 * p * C_F, dot_tn(merged_ref[p], coarse_grad))
        grad = dot_nt(coarse_grad, merge_ref[at, :])
        gains.append(column_sum(grad * hats[p]))
        shifts.append(column_sum(grad))
        inners.append(grad * merge_gain[:, at])
    block_store(flat, 1161, lane_blocks(gains))
    block_store(flat, 1167, lane_blocks(shifts))
    width = 4.0 * C_F
    first = sum(jnp.sum(inner, -1, keepdims=True) for inner in inners) / width
    second = sum(jnp.sum(i * h, -1, keepdims=True) for i, h in zip(inners, hats)) / width
    grads = jnp.concatenate([scale * (i - first - h * second) for i, h in zip(inners, hats)], 0)
    high = rounded(grads)
    attn_grad = dot_tn(quartet_sel, high)
    fog_out[...] = attn_grad + dot_tn(quartet_sel, grads - high)
    mixture_grad = rounded(dot_nt(attn_grad, proj_ref[...]))
    weight = dot_tn(mix_ref[...], attn_grad)
    corner = weight[0:1]
    keep_square(square, jnp.concatenate([weight, column_sum(attn_grad)], 0))
    block_store(flat, 873, lane_blocks([every_other(square, 1), every_other(square, 2)]))
    kinds = fine_kinds()
    places = {"a": (PART_A, probs_a), "b": (PART_B, probs_b), "c": (PART_C, probs_c)}
    query_grads = {}
    for zone in range(2):
        for name, (start, count), pieces in fine_windows(zone):
            rows_at, mask, _, _, toep, block = kinds[name]
            table_at, probs_ref = places[name]
            dq, dk, dv, table = attend_back(
                q_ref[start : start + count, :],
                gathered(k_ref, pieces),
                gathered(v_ref, pieces),
                rows_at,
                mask,
                probs_ref[zone],
                mixture_grad[start : start + count],
                toep,
                block,
            )
            query_grads[name, zone] = dq
            for c in range(3):
                at = table_at + (2 * c + zone) * block
                tables[at : at + block, :] = table[:, c * 128 : (c + 1) * 128]
            at = 0
            for source, begin, size in pieces:
                to = slice(SOURCES[source] + begin, SOURCES[source] + begin + size)
                kgrad[to, :] = rounded(dk[at : at + size])
                vgrad[to, :] = rounded(dv[at : at + size])
                at += size
    query_grad = jnp.concatenate([query_grads[name, zone] for name in "cab" for zone in range(2)], 0)
    part = dot_nt(kgrad[...], qkv_ref[:, C_F : 2 * C_F]) + dot_nt(vgrad[...], qkv_ref[:, 2 * C_F :])
    own = part[0:FINE] + dot_nt(query_grad, qkv_ref[:, 0:C_F])
    own_out[...] = own
    par_out[...] = part[FINE : 2 * FINE].astype(BF16)
    for place, out in enumerate((upo_out, upp_out, dno_out, dnp_out)):
        at = SOURCES[2 + place]
        out[...] = packed_side(part[at : at + SIDE]).astype(BF16)
    hat_grad = column_sum(own * hat_ref[0:FINE, :])
    hat_grad += column_sum(part[FINE:] * hat_ref[FINE:, :])
    block_store(
        flat, 0, lane_blocks([hat_grad, column_sum(own) + column_sum(part[FINE:])])
    )
    evens, odds, sums = ([], [], [])
    for norm, grad in (
        (normed_ref[0:FINE, :], query_grad),
        (normed_ref[...], kgrad[...]),
        (normed_ref[...], vgrad[...]),
    ):
        keep_square(square, dot_tn(norm, grad))
        evens.append(every_other(square, 0))
        odds.append(every_other(square, 1))
        sums.append(column_sum(grad))
    block_store(flat, 3, lane_blocks(evens + odds))
    block_store(flat, 867, lane_blocks(sums + [corner]))
    tables[240:PART_A, :] = jnp.zeros((PART_A - 240, 128), F32)
    tables[PART_END:, :] = jnp.zeros((TABLE_ROWS - PART_END, 128), F32)
    for c in range(3):
        at = PART_Q + 288 * c
        tables[at : at + 288, :] = table_q[:, c * 128 : (c + 1) * 128]
    split = 3483
    trows = TABLE_ROWS // len(starts)
    for place, start in starts:
        end = start + rows
        if start < split:
            size = min(end, split) - start
            value = flat[start : start + size, :]
            if end > split:
                value = jnp.concatenate([value, flat_c[0 : end - split, :]], 0)
        else:
            size = min(end, 8103) - start
            value = flat_c[start - split : start - split + size, :]
            if size < rows:
                value = jnp.concatenate([value, jnp.zeros((rows - size, 128), F32)], 0)
        chunk = pieces_out.shape[2]
        for y in range(pieces_out.shape[0]):
            pieces_out[y, place] = value[y * chunk : (y + 1) * chunk].astype(BF16)
        tables_out[place] = tables[place * trows : (place + 1) * trows, :].astype(BF16)


def final_body(
    x_ref,
    gain_ref,
    fog_ref,
    own_ref,
    par_ref,
    low_ref,
    high_ref,
    t_ref,
    token_out,
    fine_out,
    coarse_out,
    stage,
    grad,
):
    grad[...] = own_ref[...] + par_ref[...].astype(F32)
    grad[LOW : LOW + SIDE, :] += unpacked_side(low_ref[...].astype(F32))
    grad[TOP : TOP + SIDE, :] += unpacked_side(high_ref[...].astype(F32))
    hat, scale = norm_parts(x_ref[...].astype(F32))
    total = fog_ref[...] + norm_back(hat, scale, rounded(grad[...]), vector(gain_ref))
    stage[...] = dot_tn(fine_order(), total)
    store_groups(token_out, stage)

    def part(start, height):
        return jnp.concatenate(
            [t_ref[start + c * height : start + (c + 1) * height, :] for c in range(3)], 1
        )

    def natural(kind, block):
        total = None
        for zk in range(2):
            term = dot_tn(table_rows(kind, zk), dot_nt(block, table_lanes(zk)))
            total = term if total is None else total + term
        return total

    fine_out[0:288, :] = natural("a", part(PART_A, 144))
    fine_out[288:576, :] = natural("b", part(PART_B, 80)) + natural("c", part(PART_C, 80))
    coarse_out[...] = natural("q", part(PART_Q, 288))


def mesh_parts(lat, lon):
    cores = 2
    xs = 4 if lon % 8 == 0 else 1
    ys = 4 if lat % 4 == 0 else lat
    return (cores, xs, lon // (cores * xs), ys, lat // ys)


def piece_rows(total, lon, ys):
    longest = -(-(127 + total // lon) // 128)
    unit = 16 * ys
    return -(-longest // unit) * unit


def reduce_body(
    dims,
    norm_factor,
    g_ref,
    gt_ref,
    par_ref,
    upo_ref,
    upp_ref,
    dno_ref,
    dnp_ref,
    p_ref,
    t_ref,
    par_out,
    low_out,
    high_out,
    par_buf,
    up_buf,
    down_buf,
    up_sum,
    down_sum,
    low_buf,
    high_buf,
    core_buf,
    head_buf,
    tail_buf,
    y_buf,
    y_sum,
    x_buf,
    x_sum,
    z_buf,
    h_send,
    h_buf,
    share,
    tab_core,
    tab_x,
    tab_sum,
    tab_hand,
    tab_z,
    tab_all,
    send_sems,
    recv_sems,
):
    cores, xs, zs, ys, hs = dims
    half = xs * zs
    chunk = g_ref.shape[2]
    trows = gt_ref.shape[1]
    lat, lon = (lax.axis_index("lat"), lax.axis_index("lon"))
    core = lax.rem(lon, cores)
    x = lax.rem(lon // cores, xs)
    z = lon // (cores * xs)
    y = lax.rem(lat, ys)
    h = lat // ys
    lats = ys * hs

    def at(here, d, count):
        return lax.rem(here + d, count)

    def lon_of(core_to, x_to, z_to):
        return (z_to * xs + x_to) * cores + core_to

    other_core = (lat, lon_of(1 - core, x, z))
    x_peers = {d: (lat, lon_of(core, at(x, d, xs), z)) for d in range(1, xs)}
    y_peers = {d: (h * ys + at(y, d, ys), lon) for d in range(1, ys)}
    z_peers = {d: (lat, lon_of(core, x, at(z, d, zs))) for d in range(1, zs)}
    far = (at(h, 1, hs) * ys + y, lon)
    before, after = ((at(lat, lats - 1, lats), lon), (at(lat, 1, lats), lon))
    beside = (lat, partner_of(lon, cores * half))
    peers = [other_core, before, after, beside]
    peers += list(x_peers.values()) + list(y_peers.values()) + list(z_peers.values())
    if hs > 1:
        peers.append(far)
    meet(peers)
    pending = []

    def send(src, dst, peer):
        sem = len(pending)
        copy = start_copy(src, dst, send_sems.at[sem], recv_sems.at[sem], peer)
        pending.append(copy)
        return copy

    def arrived(copies):
        for copy in copies:
            copy.wait_recv()

    def add_into(target, terms, count):
        def step(i, carry):
            total = terms[0](i).astype(F32)
            for term in terms[1:]:
                total = total + term(i).astype(F32)
            target[i] = total.astype(BF16)
            return carry

        lax.fori_loop(0, count, step, 0)

    away = pl.ds((1 - core) * half, half)
    mine = core * half
    table_core = send(gt_ref.at[away], tab_core, other_core)
    edges = [
        send(upp_ref, up_buf, beside),
        send(dnp_ref, down_buf, beside),
        send(par_ref, par_buf, beside),
    ]
    order = {4: (2, 1, 3, 0), 2: (1, 0), 1: (0,)}[ys]
    crossing = {d: send(g_ref.at[at(y, d, ys), away], core_buf.at[d], other_core) for d in order}
    table_core.wait_recv()
    add_into(tab_core, [lambda i: tab_core[i], lambda i: gt_ref[mine + i]], half)
    table_x = [
        send(tab_core.at[pl.ds(at(x, d, xs) * zs, zs)], tab_x.at[d - 1], x_peers[d])
        for d in range(1, xs)
    ]
    cut = half // 2
    head, tail = (pl.ds(0, cut), pl.ds(cut, half - cut))
    gathered_y = []
    for d in order:
        crossing[d].wait_recv()
        row = at(y, d, ys)
        buf = core_buf.at[d]
        add_into(buf, [lambda i: buf[i], lambda i: g_ref[row, mine + i]], half)
        if ys == 4 and d == 2:
            over_right = send(core_buf.at[2, head], head_buf, y_peers[1])
            over_left = send(core_buf.at[2, tail], tail_buf, y_peers[3])
        if ys == 4 and d == 1:
            gathered_y.append(send(core_buf.at[1, tail], y_buf.at[0, tail], y_peers[1]))
        if ys == 4 and d == 3:
            gathered_y.append(send(core_buf.at[3, head], y_buf.at[1, head], y_peers[3]))
        if ys == 2 and d == 1:
            gathered_y.append(send(core_buf.at[1], y_buf.at[0], y_peers[1]))
    if ys == 4:
        over_right.wait_recv()
        right = core_buf.at[1]
        add_into(right, [lambda i: right[i], lambda i: head_buf[i]], cut)
        gathered_y.append(send(core_buf.at[1, head], y_buf.at[0, head], y_peers[1]))
        over_left.wait_recv()
        left = core_buf.at[3, tail]
        add_into(left, [lambda i: left[i], lambda i: tail_buf[i]], half - cut)
        gathered_y.append(send(core_buf.at[3, tail], y_buf.at[1, tail], y_peers[3]))

    arrived(table_x)
    base = x * zs
    terms = [lambda i: tab_core[base + i]]
    terms += [lambda i, d=d: tab_x[d - 1, i] for d in range(1, xs)]
    add_into(tab_sum, terms, zs)
    first_row = (core * xs + x) * zs * trows
    hand_sem = len(pending)
    handed = pltpu.make_async_remote_copy(
        src_ref=tab_sum,
        dst_ref=tab_hand,
        send_sem=send_sems.at[hand_sem],
        recv_sem=recv_sems.at[hand_sem],
        device_id=before,
        device_id_type=MESH,
    )
    arrived(edges[:2])
    up_sum[...] = (upo_ref[...].astype(F32) + up_buf[...].astype(F32)).astype(BF16)
    down_sum[...] = (dno_ref[...].astype(F32) + down_buf[...].astype(F32)).astype(BF16)

    @pl.when(first_row < PART_A)
    def _():
        handed.start()
        handed.wait()

        def choose(i, carry):
            row = first_row + i * trows + lax.broadcasted_iota(jnp.int32, (trows, 128), 0)
            tab_sum[i] = jnp.where(
                row < PART_A, tab_hand[i].astype(F32), tab_sum[i].astype(F32)
            ).astype(BF16)
            return carry

        lax.fori_loop(0, zs, choose, 0)

    pending.append(None)
    table_z = [
        send(tab_sum.at[at(z, d, zs)], tab_z.at[d - 1], z_peers[d]) for d in range(1, zs)
    ]

    arrived(gathered_y)
    terms = [lambda i: core_buf[0, i]]
    terms += [lambda i, d=d: y_buf[d, i] for d in range({4: 2, 2: 1, 1: 0}[ys])]
    add_into(y_sum, terms, half)
    along_x = [
        send(y_sum.at[pl.ds(at(x, d, xs) * zs, zs)], x_buf.at[d - 1], x_peers[d])
        for d in range(1, xs)
    ]
    edges.append(send(up_sum, low_buf, after))
    edges.append(send(down_sum, high_buf, before))

    arrived(table_z)
    total = tab_sum[z].astype(F32)
    for d in range(1, zs):
        total = total + tab_z[d - 1].astype(F32)
    tab_all[core, x, z] = (total * norm_factor).astype(BF16)
    own = tab_all.at[core, x, z]
    back_z = [send(own, own, z_peers[d]) for d in range(1, zs)]

    arrived(along_x)
    terms = [lambda i: y_sum[base + i]]
    terms += [lambda i, d=d: x_buf[d - 1, i] for d in range(1, xs)]
    add_into(x_sum, terms, zs)
    along_z = [send(x_sum.at[at(z, d, zs)], z_buf.at[d - 1], z_peers[d]) for d in range(1, zs)]

    arrived(back_z)
    own = tab_all.at[core, x]
    back_x = [send(own, own, x_peers[d]) for d in range(1, xs)]

    arrived(along_z)
    total = x_sum[z].astype(F32)
    for d in range(1, zs):
        total = total + z_buf[d - 1].astype(F32)
    if hs > 1:
        h_send[...] = total.astype(BF16)
        across = send(h_send, h_buf, far)
    arrived(back_x)
    own = tab_all.at[core]
    back_core = send(own, own, other_core)
    if hs > 1:
        across.wait_recv()
        total = h_send[...].astype(F32) + h_buf[...].astype(F32)
    rows = pl.ds(pl.multiple_of(y * chunk, 8), chunk)
    share[rows, :] = total * norm_factor
    back_y = [send(share.at[rows], share.at[rows], y_peers[d]) for d in range(1, ys)]
    arrived(edges[2:])
    par_out[...] = par_buf[...]
    low_out[...] = low_buf[...]
    high_out[...] = high_buf[...]
    back_core.wait_recv()
    t_ref[...] = tab_all[...]
    arrived(back_y)
    p_ref[...] = share[...]
    for copy in pending:
        if copy is not None:
            copy.wait_send()


def reduce_all(pieces, tables, edges, norm_factor, dims):
    cores, xs, zs, ys, hs = dims
    half = xs * zs
    chunk = pieces.shape[2]
    trows = tables.shape[1]
    sem = pltpu.SemaphoreType.DMA((64,))
    vmem = pl.BlockSpec(memory_space=pltpu.VMEM)
    side = (128, 128)
    all_tables = (cores, xs, zs, trows, 128)
    outs = [((ys * chunk, 128), F32), (all_tables, BF16), ((FINE, C_F), BF16)]
    outs += [(side, BF16), (side, BF16)]
    buffers = [
        (FINE, C_F),
        *[side] * 6,
        (ys, half, chunk, 128),
        (half // 2, chunk, 128),
        (half - half // 2, chunk, 128),
        (2, half, chunk, 128),
        (half, chunk, 128),
        (max(xs - 1, 1), zs, chunk, 128),
        (zs, chunk, 128),
        (max(zs - 1, 1), chunk, 128),
        (chunk, 128),
        (chunk, 128),
        None,
        (half, trows, 128),
        (max(xs - 1, 1), zs, trows, 128),
        (zs, trows, 128),
        (zs, trows, 128),
        (max(zs - 1, 1), trows, 128),
        all_tables,
    ]
    scratch = [
        pltpu.VMEM((ys * chunk, 128), F32) if shape is None else pltpu.VMEM(shape, BF16)
        for shape in buffers
    ]
    return pl.pallas_call(
        functools.partial(reduce_body, dims, norm_factor),
        out_shape=tuple(jax.ShapeDtypeStruct(shape, dtype) for shape, dtype in outs),
        in_specs=[vmem] * 7,
        out_specs=(vmem,) * 5,
        scratch_shapes=scratch + [sem, sem],
        compiler_params=pltpu.CompilerParams(
            collective_id=7, has_side_effects=True, vmem_limit_bytes=VMEM_BYTES
        ),
        cost_estimate=lasting(35),
        name="grad_reduce",
    )(pieces, tables, *edges)


def shards(
    tokens,
    fine_gain,
    fine_shift,
    fine_qkv,
    fine_qkv_bias,
    fine_proj,
    fine_proj_bias,
    fine_table,
    merge_gain,
    merge_shift,
    merge_weight,
    coarse_gain,
    coarse_shift,
    coarse_qkv,
    coarse_qkv_bias,
    coarse_proj,
    coarse_proj_bias,
    coarse_table,
    cotangent,
):
    lat_count, lon_count = (lax.axis_size("lat"), lax.axis_size("lon"))
    lat, lon = (lax.axis_index("lat"), lax.axis_index("lon"))
    norm_factor = 1.0 / math.sqrt(tokens.size // C_F * lat_count * lon_count / 4)
    fine_rows = fine_table.reshape(576, 138)
    coarse_rows = coarse_table.reshape(576, 138)
    cells = tokens[0].transpose(1, 2, 0, 3)
    cot_cells = cotangent[0].transpose(1, 2, 0, 3)

    group = min(8, lon_count)
    side = ((128, 128), BF16)
    own = ((FINE, C_F), BF16)
    table_part = ((group, PART_A // group, 128), BF16)
    x, low, high, table_send = call(
        prepare_body,
        [own, side, side, table_part],
        (cells, fine_rows),
        [pltpu.VMEM((288, C_F), F32)],
        "prepare",
        2,
    )
    halo = [own, side, side, side, side, table_part]
    par, upo, upp, dno, dnp, table_before = exchange_call(
        halo_body,
        halo,
        (x, low, high, table_send),
        [pltpu.VMEM(*s) for s in halo],
        (6, max(group - 1, 1)),
        1,
        "halo",
        10,
    )
    bias_a, bias_b, bias_c, bias_q = call(
        bias_body,
        [((2, 432, 144), F32), ((2, 240, 160), F32), ((2, 240, 160), F32), ((2, 432, 160), F32)],
        (fine_rows, table_before.reshape(PART_A, 128), coarse_rows),
        (),
        "bias_terms",
        4,
    )
    (
        hat,
        normed,
        q,
        k,
        v,
        probs_a,
        probs_b,
        probs_c,
        mixture,
        fine_out,
        merged,
        coarse,
        cnorm,
    ) = call(
        fine_forward_body,
        [
            ((ALL_ROWS, C_F), F32),
            ((ALL_ROWS, C_F), BF16),
            ((FINE, C_F), F32),
            ((ALL_ROWS, C_F), F32),
            ((ALL_ROWS, C_F), F32),
            ((2, 432, 144), F32),
            ((2, 240, 160), F32),
            ((2, 240, 160), F32),
            own,
            own,
            ((4, COARSE, C_F), BF16),
            ((COARSE, C_C), F32),
            ((COARSE, C_C), BF16),
        ],
        (
            x,
            par,
            upo,
            upp,
            dno,
            dnp,
            fine_gain,
            fine_shift,
            fine_qkv,
            fine_qkv_bias,
            fine_proj,
            fine_proj_bias,
            merge_gain,
            merge_shift,
            merge_weight,
            coarse_gain,
            coarse_shift,
            bias_a,
            bias_b,
            bias_c,
        ),
        (),
        "fine_forward",
        10,
    )
    gathered_to = [((4, COARSE, C_C), BF16)]
    (gathered_norm,) = exchange_call(
        group_body, gathered_to, (cnorm,), [pltpu.VMEM(*gathered_to[0])], (3,), 2, "coarse_gather", 5
    )
    coarse_out, parts, own_part, flat_c, table_q, cot = call(
        coarse_body,
        [
            ((6, 3, 4, C_C), BF16),
            ((4, COARSE, C_C), BF16),
            ((COARSE, C_C), F32),
            ((4620, 128), F32),
            ((288, 384), F32),
            ((COARSE, C_C), F32),
        ],
        (
            gathered_norm,
            cnorm,
            coarse,
            cot_cells,
            coarse_qkv,
            coarse_qkv_bias,
            coarse_proj,
            coarse_proj_bias,
            bias_q,
        ),
        [
            pltpu.VMEM((72, C_C), F32),
            pltpu.VMEM((4 * COARSE, C_C), F32),
            pltpu.VMEM((4 * COARSE, C_C), F32),
        ],
        "coarse_attention",
        7,
    )
    (norm_part,) = exchange_call(
        ungroup_body,
        [((COARSE, C_C), F32)],
        (parts,),
        [pltpu.VMEM((3, COARSE, C_C), BF16)],
        (3,),
        3,
        "coarse_scatter",
        5,
    )
    dims = mesh_parts(lat_count, lon_count)
    cores, xs, zs, ys, hs = dims
    segment = PARAMS // lon_count
    rows = piece_rows(PARAMS, lon_count, ys)
    starts = []
    for index in range(lon_count):
        core, x_at, z_at = (index % cores, index // cores % xs, index // (cores * xs))
        starts.append(((core * xs + x_at) * zs + z_at, index * segment // 128))
    trows = TABLE_ROWS // lon_count
    fine_out_grad, own_grad, *edges, pieces, table_pieces = call(
        functools.partial(fine_back_body, starts, rows),
        [
            ((FINE, C_F), F32),
            ((FINE, C_F), F32),
            own,
            side,
            side,
            side,
            side,
            ((ys, lon_count, rows // ys, 128), BF16),
            ((lon_count, trows, 128), BF16),
        ],
        (
            norm_part,
            own_part,
            cot,
            coarse,
            merged,
            fine_out,
            hat,
            normed,
            mixture,
            q,
            k,
            v,
            probs_a,
            probs_b,
            probs_c,
            fine_qkv,
            coarse_gain,
            merge_gain,
            merge_weight,
            fine_proj,
            flat_c,
            table_q,
        ),
        [
            pltpu.VMEM((ALL_ROWS, C_F), F32),
            pltpu.VMEM((ALL_ROWS, C_F), F32),
            pltpu.VMEM((3488, 128), F32),
            pltpu.VMEM((TABLE_ROWS, 128), F32),
            pltpu.VMEM((2, 200, 128), F32),
        ],
        "fine_backward",
        9,
    )
    owned, table_sum, par_back, low_back, high_back = reduce_all(
        pieces, table_pieces, edges, norm_factor, dims
    )
    shift = lax.rem(lon * segment, 128)
    param_grads = lax.dynamic_slice(owned.reshape(-1), (shift,), (segment,))
    token_grad, fine_total, coarse_total = call(
        final_body,
        [((12, 6, 4, C_F), BF16), ((576, 138), F32), ((576, 138), F32)],
        (
            x,
            fine_gain,
            fine_out_grad,
            own_grad,
            par_back,
            low_back,
            high_back,
            table_sum.reshape(TABLE_ROWS, 128),
        ),
        [pltpu.VMEM((288, C_F), F32), pltpu.VMEM((FINE, C_F), F32)],
        "final",
        2,
    )
    return (
        coarse_out.transpose(2, 0, 1, 3)[None],
        token_grad.transpose(2, 0, 1, 3)[None],
        param_grads,
        fine_total.reshape(2, -1),
        coarse_total.reshape(2, -1),
    )


def solution(mesh):
    tiles = P(None, None, "lat", "lon", None)
    whole = P()
    rows = P("lat", None)
    return jax.shard_map(
        shards,
        mesh=mesh,
        in_specs=(tiles,) + (whole,) * 6 + (rows,) + (whole,) * 9 + (rows, tiles),
        out_specs=(tiles, tiles, P("lon"), rows, rows),
        check_vma=False,
    )
```

```python
import functools
import math

import jax
import jax.numpy as jnp
from jax import lax
from jax.experimental import pallas as pl
from jax.experimental.pallas import tpu as pltpu
from jax.sharding import PartitionSpec as P

HEAD = 32
HEADS_F = 6
HEADS_C = 12
C_F = 192
C_C = 384
SPAN = 23
EPS = 1e-05
NEGATIVE = -1e30
MESH = pl.DeviceIdType.MESH
F32 = jnp.float32
BF16 = jnp.bfloat16
MIB = 1024 * 1024
VMEM_BYTES = 28 * MIB

LOW, MID, TOP = (0, 80, 224)
PARAMS = 1037184
TABLE_ROWS = 2048
FINE = 304
SIDE = 80
COARSE = 80
PART_C, PART_A, PART_B, PART_Q, PART_END = (0, 256, 688, 928, 1792)


def whole(x, n):
    return jnp.floor((x + 0.5) * (1.0 / n))


def rest(x, n):
    return x - n * whole(x, n)


def down_rows(n):
    return lax.broadcasted_iota(jnp.int32, (n, 1), 0).astype(F32)


def along_lanes(n):
    return lax.broadcasted_iota(jnp.int32, (1, n), 1).astype(F32)


def match(a, b):
    return jnp.where(a == b, 1.0, 0.0).astype(BF16)


def fine_row(zone, zq, row, col):
    low = LOW + zone * 40 + (zq * 3 + row) * 6 + col
    mid = MID + zone * 72 + (zq * 6 + row - 3) * 6 + col
    top = TOP + zone * 40 + (zq * 3 + row - 9) * 6 + col
    return jnp.where(row < 3, low, jnp.where(row < 9, mid, top))


def fine_order():
    at = down_rows(FINE)
    low, top = (at < MID, at >= TOP)
    edge = jnp.where(top, at - TOP, at)
    mid = at - MID
    in_edge = low | top
    part = rest(edge, 40)
    zone = jnp.where(in_edge, whole(edge, 40), whole(mid, 72))
    zq = jnp.where(in_edge, whole(part, 18), whole(rest(mid, 72), 36))
    row = jnp.where(
        in_edge,
        whole(rest(part, 18), 6) + jnp.where(top, 9.0, 0.0),
        3 + whole(rest(mid, 36), 6),
    )
    col = jnp.where(in_edge, rest(part, 6), rest(mid, 6))
    code = (row * 6 + col) * 4 + rest(2 * zone + zq + 1, 4)
    return match(jnp.where(in_edge & (part >= 36), -1.0, code), along_lanes(288))


def coarse_place(at):
    part = rest(at, 40)
    return (whole(at, 40), whole(part, 18), whole(rest(part, 18), 3), rest(part, 3), part < 36)


def coarse_order():
    zone, zq, row, col, valid = coarse_place(down_rows(COARSE))
    code = (row * 3 + col) * 4 + 2 * zone + zq
    return match(jnp.where(valid, code, -1.0), along_lanes(72))


def quartet_order():
    at = down_rows(4 * COARSE)
    p = whole(at, COARSE)
    zone, zq, row, col, valid = coarse_place(rest(at, COARSE))
    rolled = rest(2 * zone + zq + 3, 4)
    source = fine_row(
        whole(rolled, 2), rest(rolled, 2), 2 * row + rest(p, 2), 2 * col + whole(p, 2)
    )
    return match(jnp.where(valid, source, -1.0), along_lanes(FINE))


def head_rows(heads, lats, cols, tokens, block):
    at = down_rows(block * cols)
    part = rest(at, block)
    h = whole(part, 2 * lats)
    zq = whole(rest(part, 2 * lats), lats)
    code = (zq * lats + rest(part, lats)) * cols + whole(at, block)
    valid = part < heads * 2 * lats
    head = jnp.where(valid, h, -1.0)
    mask = match(head, whole(along_lanes(heads * HEAD), HEAD)).astype(F32)
    return (match(jnp.where(valid, code, -1.0), along_lanes(tokens)), mask, zq)


def pair_keys(size, half):
    u = along_lanes(size)
    if size == 144:
        source, part = (whole(u, 72), rest(u, 72))
        zk, ak, valid = (whole(part, 36), whole(rest(part, 36), 6), part >= 0)
    else:
        slot, part = (whole(u, 40), rest(u, 40))
        source = rest(slot, 2)
        zk = whole(part, 18)
        ak = 3 * whole(slot, 2) + whole(rest(part, 18), 6)
        valid = part < 36
    return (zk, ak, rest(part, 6) + 6 * jnp.abs(half - source), valid)


def group_keys():
    u = along_lanes(160)
    part = rest(u, 40)
    zk, ak = (whole(part, 18), whole(rest(part, 18), 3))
    return (zk, ak, rest(part, 3) + 3 * whole(u, 40), part < 36)


def toeplitz(keys, cols, shift):
    zk, ak, col, valid = keys
    at = down_rows(384)
    tail = at >= 256
    level = jnp.where(tail, whole(at - 256, 64), whole(at, 128))
    entry = jnp.where(tail, 128 + rest(at, 64), rest(at, 128))
    code = (level * 6 + whole(entry, SPAN)) * 64 + rest(entry, SPAN)
    code = jnp.where(entry < 138, code, -1.0)
    key_code = jnp.where(valid, (zk * 6 + ak) * 64 - col + shift + 11, -100.0)
    return [match(code, key_code + oq) for oq in range(cols)]


def table_lanes(zk):
    entry = down_rows(138)
    return match(
        jnp.where(entry < 128, zk * 128 + entry, 256 + zk * 64 + entry - 128), along_lanes(384)
    )


def table_rows(kind, zk):
    if kind == "q":
        at = down_rows(288)
        part = rest(at, 144)
        aq = rest(part, 6)
        lead = (whole(aq, 3) * 2 + whole(at, 144)) * HEADS_C + whole(part, 12)
        zq = whole(rest(part, 12), 6)
        return match(((lead * 2 + zq) * 2 + zk) * 3 + rest(aq, 3), along_lanes(576))
    if kind == "a":
        at, block, lats, first = (down_rows(144), 72, 6, 0)
    else:
        at, block, lats, first = (down_rows(80), 40, 3, 3 if kind == "c" else 0)
    part = rest(at, block)
    lead = whole(at, block) * HEADS_F + whole(part, 2 * lats)
    zq = whole(rest(part, 2 * lats), lats)
    code = ((lead * 2 + zq) * 2 + zk) * 6 + rest(part, lats) + first
    return match(jnp.where(part < 12 * lats, code, -1.0), along_lanes(288))


def dot(a, b):
    return jnp.dot(a.astype(BF16), b.astype(BF16), preferred_element_type=F32)


def dot_nt(a, b):
    return lax.dot_general(
        a.astype(BF16), b.astype(BF16), (((1,), (1,)), ((), ())), preferred_element_type=F32
    )


def dot_tn(a, b):
    return lax.dot_general(
        a.astype(BF16), b.astype(BF16), (((0,), (0,)), ((), ())), preferred_element_type=F32
    )


def rounded(value):
    return value.astype(BF16).astype(F32)


def norm_parts(volume):
    centre = volume - jnp.mean(volume, -1, keepdims=True)
    spread = jnp.mean(centre * centre, -1, keepdims=True)
    scale = lax.rsqrt(spread + EPS)
    return (centre * scale, scale)


def norm_back(hat, scale, grad, gain):
    inner = grad * gain
    return scale * (
        inner
        - jnp.mean(inner, -1, keepdims=True)
        - hat * jnp.mean(inner * hat, -1, keepdims=True)
    )


def column_sum(value):
    return jnp.sum(value, 0, keepdims=True)


def attend(queries, keys, values, rows, mask, bias):
    packed = dot(rows, queries) * mask
    scores = dot_nt(packed, keys) * HEAD ** (-0.5) + bias
    weights = jnp.exp(scores - jnp.max(scores, -1, keepdims=True))
    probs = weights / jnp.sum(weights, -1, keepdims=True)
    mixture = dot(probs, values) * mask
    return (probs, dot_tn(rows, mixture))


def attend_back(queries, keys, values, rows, mask, probs, mixture_grad, toep, block):
    factor = HEAD ** (-0.5)
    packed = dot(rows, queries) * mask
    grad = dot(rows, mixture_grad) * mask
    value_grad = dot_tn(probs, grad)
    prob_grad = dot_nt(grad, values)
    score_grad = probs * (prob_grad - jnp.sum(prob_grad * probs, -1, keepdims=True))
    query_grad = dot_tn(rows, dot(score_grad, keys) * factor * mask)
    key_grad = dot_tn(score_grad, packed) * factor
    table = None
    for oq, select in enumerate(toep):
        part = dot_nt(score_grad[oq * block : (oq + 1) * block], select)
        table = part if table is None else table + part
    return (query_grad, key_grad, value_grad, table)


def lasting(micros):
    return pl.CostEstimate(flops=int(micros * 2.0e9), bytes_accessed=int(micros * 3.69e6), transcendentals=int(micros * 1e6))


def call(body, outs, args, scratch, name, micros, in_place=(), limit=VMEM_BYTES):
    vmem = pl.BlockSpec(memory_space=pltpu.VMEM)
    away = pl.BlockSpec(memory_space=pltpu.HBM)
    return pl.pallas_call(
        body,
        out_shape=tuple(jax.ShapeDtypeStruct(shape, dtype) for shape, dtype in outs),
        in_specs=[away if at in in_place else vmem for at in range(len(args))],
        out_specs=(vmem,) * len(outs),
        scratch_shapes=list(scratch),
        compiler_params=pltpu.CompilerParams(vmem_limit_bytes=limit),
        cost_estimate=lasting(micros),
        name=name,
    )(*args)


def vector(ref):
    return ref[...].reshape(1, -1)


def query_half():
    return 1 - lax.rem(lax.axis_index("lon"), 2)


def packed_side(value):
    tail = jnp.concatenate([value[0:40, 128:192], value[40:80, 128:192]], 1)
    return jnp.concatenate([value[:, 0:128], tail, jnp.zeros((8, 128), value.dtype)], 0)


def unpacked_side(block):
    tail = jnp.concatenate([block[80:120, 0:64], block[80:120, 64:128]], 0)
    return jnp.concatenate([block[0:80, :], tail], 1)


def lane_blocks(pieces):
    blocks = []
    for a, b in zip(pieces[::2], pieces[1::2]):
        blocks += [a[:, 0:128], jnp.concatenate([a[:, 128:192], b[:, 0:64]], 1), b[:, 64:192]]
    return blocks


def partner_of(lon, count):
    odd = lax.rem(lon, 2)
    return lax.rem(lon + 2 * odd - 1 + count, count)


def ring_positions():
    lat_count, lon_count = (lax.axis_size("lat"), lax.axis_size("lon"))
    lat, lon = (lax.axis_index("lat"), lax.axis_index("lon"))
    up = lax.rem(lat + 1, lat_count)
    down = lax.rem(lat + lat_count - 1, lat_count)
    return (lat, lon, up, down, partner_of(lon, lon_count))


def meet(peers):
    barrier = pltpu.get_barrier_semaphore()
    for peer in peers:
        pl.semaphore_signal(barrier, inc=1, device_id=peer, device_id_type=MESH)
    pl.semaphore_wait(barrier, len(peers))


def start_copy(src, dst, send_sem, recv_sem, peer):
    copy = pltpu.make_async_remote_copy(
        src_ref=src,
        dst_ref=dst,
        send_sem=send_sem,
        recv_sem=recv_sem,
        device_id=peer,
        device_id_type=MESH,
    )
    copy.start()
    return copy


def exchange(sends, send_sems, recv_sems):
    copies = []
    for at, (src, dst, peer) in enumerate(sends):
        copies.append(start_copy(src, dst, send_sems.at[at], recv_sems.at[at], peer))
    for copy in copies:
        copy.wait_recv()
    for copy in copies:
        copy.wait_send()


def exchange_call(body, outs, args, scratch, counts, collective_id, name, micros):
    vmem = pl.BlockSpec(memory_space=pltpu.VMEM)
    sem = pltpu.SemaphoreType.DMA
    return pl.pallas_call(
        body,
        out_shape=tuple(jax.ShapeDtypeStruct(shape, dtype) for shape, dtype in outs),
        in_specs=[vmem] * len(args),
        out_specs=(vmem,) * len(outs),
        scratch_shapes=list(scratch) + [sem((count,)) for count in counts for _ in range(2)],
        compiler_params=pltpu.CompilerParams(
            collective_id=collective_id, has_side_effects=True, vmem_limit_bytes=VMEM_BYTES
        ),
        cost_estimate=lasting(micros),
        name=name,
    )(*args)


def halo_body(x_ref, low_ref, high_ref, tab_ref, *refs):
    outs, bufs, (ss, rs, ts, tr) = (refs[:6], refs[6:12], refs[12:])
    par, upo, upp, dno, dnp, tab = bufs
    lat, lon, up, down, partner = ring_positions()
    size = tab.shape[0]
    rank = lax.rem(lon, size)
    others = [lax.rem(rank + d, size) for d in range(1, size)]
    near = [(lat, lon - rank + other) for other in others]
    beside = (lat, partner)
    meet([(up, lon), (down, lon), beside] + near)
    low_copy = start_copy(low_ref, upo, ss.at[1], rs.at[1], (down, lon))
    high_copy = start_copy(high_ref, dno, ss.at[2], rs.at[2], (up, lon))
    table_copy = start_copy(tab_ref.at[rank], tab.at[rank], ss.at[3], rs.at[3], (up, lon))
    x_copy = start_copy(x_ref, par, ss.at[0], rs.at[0], beside)
    copies = [x_copy, low_copy, high_copy, table_copy]
    low_copy.wait_recv()
    relays = [start_copy(upo, upp, ss.at[4], rs.at[4], beside)]
    high_copy.wait_recv()
    relays.append(start_copy(dno, dnp, ss.at[5], rs.at[5], beside))
    table_copy.wait_recv()
    for d, peer in enumerate(near):
        relays.append(start_copy(tab.at[rank], tab.at[rank], ts.at[d], tr.at[d], peer))
    x_copy.wait_recv()
    for copy in relays:
        copy.wait_recv()
    for copy in copies + relays:
        copy.wait_send()
    for out, buf in zip(outs, bufs):
        out[...] = buf[...]


def group_body(own_ref, out_ref, buf, ss, rs):
    lat, lon = (lax.axis_index("lat"), lax.axis_index("lon"))
    place = lax.rem(lon, 4)
    others = [lax.rem(place + d, 4) for d in range(1, 4)]
    peers = [(lat, lon - place + other) for other in others]
    meet(peers)
    buf[place] = own_ref[...]
    exchange([(own_ref, buf.at[place], peer) for peer in peers], ss, rs)
    out_ref[...] = buf[...]


def ungroup_body(parts_ref, out_ref, buf, ss, rs):
    lat, lon = (lax.axis_index("lat"), lax.axis_index("lon"))
    place = lax.rem(lon, 4)
    others = [lax.rem(place + d, 4) for d in range(1, 4)]
    peers = [(lat, lon - place + other) for other in others]
    meet(peers)
    exchange(
        [(parts_ref.at[other], buf.at[d], peers[d]) for d, other in enumerate(others)], ss, rs
    )
    total = parts_ref[place].astype(F32)
    for d in range(3):
        total = total + buf[d].astype(F32)
    out_ref[...] = total


def spread(kind, table):
    total = None
    for zk in range(2):
        part = dot(dot(table_rows(kind, zk), table), table_lanes(zk))
        total = part if total is None else total + part
    return total


def bias_rows(table, toep, zone, block):
    rows = table[zone * block : (zone + 1) * block]
    return jnp.concatenate([dot(rows, select) for select in toep], 0)


def banned(keys, zq, zone):
    ban = jnp.where(keys[3], 0.0, NEGATIVE)
    if zone == 1:
        ban = ban + jnp.where(zq == keys[0], 0.0, NEGATIVE)
    return ban


def fetch_groups(stage, ref):
    rows, cols = ref.shape[:2]
    for row in range(rows):
        for col in range(cols):
            at = (row * cols + col) * 4
            stage[at : at + 4, :] = ref[row, col].astype(F32)


def store_groups(ref, stage):
    rows, cols = ref.shape[:2]
    for row in range(rows):
        for col in range(cols):
            at = (row * cols + col) * 4
            ref[row, col] = stage[at : at + 4, :].astype(BF16)


def prepare_body(x_ref, tf_ref, own_out, low_out, high_out, tab_out, stage):
    fetch_groups(stage, x_ref)
    tokens = dot(fine_order(), stage[...])
    own_out[...] = tokens.astype(BF16)
    low_out[...] = packed_side(tokens[LOW : LOW + SIDE]).astype(BF16)
    high_out[...] = packed_side(tokens[TOP : TOP + SIDE]).astype(BF16)
    table = spread("c", tf_ref[288:576, :])
    pieces = [table[:, c * 128 : (c + 1) * 128] for c in range(3)]
    block = jnp.concatenate(pieces + [jnp.zeros((16, 128), F32)], 0).astype(BF16)
    size = tab_out.shape[1]
    for place in range(tab_out.shape[0]):
        tab_out[place] = block[place * size : (place + 1) * size, :]


def fine_kinds():
    half = query_half().astype(F32)
    rows_a, mask_a, zq_a = head_rows(HEADS_F, 6, 6, 72, 72)
    rows_b, mask_b, zq_b = head_rows(HEADS_F, 3, 6, 40, 40)
    keys_a, keys_b = (pair_keys(144, half), pair_keys(160, half))
    toep_a, toep_b = (toeplitz(keys_a, 6, 6 * half), toeplitz(keys_b, 6, 6 * half))
    mid = (rows_a, mask_a, zq_a, keys_a, toep_a, 72)
    edge = (rows_b, mask_b, zq_b, keys_b, toep_b, 40)
    return {"a": mid, "b": edge, "c": edge}


def bias_body(tf_ref, tp_ref, tc_ref, out_a, out_b, out_c, out_q):
    tables = {
        "a": spread("a", tf_ref[0:288, :]),
        "b": spread("b", tf_ref[288:576, :]),
        "c": jnp.concatenate([tp_ref[c * 80 : (c + 1) * 80, :].astype(F32) for c in range(3)], 1),
    }
    lat = lax.axis_index("lat")
    late = along_lanes(160) >= 80
    edges = {
        "a": 0.0,
        "b": jnp.where(late & (lat == lax.axis_size("lat") - 1), NEGATIVE, 0.0),
        "c": jnp.where(jnp.logical_not(late) & (lat == 0), NEGATIVE, 0.0),
    }
    kinds = fine_kinds()
    for name, out in (("a", out_a), ("b", out_b), ("c", out_c)):
        _, _, zq, keys, toep, block = kinds[name]
        for zone in range(2):
            terms = bias_rows(tables[name], toep, zone, block)
            out[zone] = terms + banned(keys, zq, zone) + edges[name]
    _, _, zq = head_rows(HEADS_C, 6, 3, 40, 144)
    cells = group_keys()
    toep = toeplitz(cells, 3, 3 * lax.rem(lax.axis_index("lon"), 4).astype(F32))
    table = spread("q", tc_ref[...])
    for zone in range(2):
        out_q[zone] = bias_rows(table, toep, zone, 144) + banned(cells, zq, 0)


def fine_windows(zone):
    edge = zone * 40
    return (
        ("a", (MID + zone * 72, 72), [(0, MID + zone * 72, 72), (1, MID + zone * 72, 72)]),
        ("b", (TOP + edge, 40), [(0, TOP + edge, 40), (1, TOP + edge, 40), (2, edge, 40), (3, edge, 40)]),
        ("c", (LOW + edge, 40), [(4, edge, 40), (5, edge, 40), (0, LOW + edge, 40), (1, LOW + edge, 40)]),
    )


SOURCES = (0, FINE, 2 * FINE, 2 * FINE + SIDE, 2 * FINE + 2 * SIDE, 2 * FINE + 3 * SIDE)
ALL_ROWS = 2 * FINE + 4 * SIDE


def gathered(ref, pieces):
    return jnp.concatenate(
        [ref[SOURCES[source] + start : SOURCES[source] + start + count, :] for source, start, count in pieces],
        0,
    )


def fine_forward_body(
    own_ref,
    par_ref,
    upo_ref,
    upp_ref,
    dno_ref,
    dnp_ref,
    gain_ref,
    shift_ref,
    qkv_ref,
    qkv_bias_ref,
    proj_ref,
    proj_bias_ref,
    merge_gain_ref,
    merge_shift_ref,
    merge_ref,
    coarse_gain_ref,
    coarse_shift_ref,
    bias_a,
    bias_b,
    bias_c,
    hat_out,
    normed,
    q_out,
    k_out,
    v_out,
    probs_a,
    probs_b,
    probs_c,
    mix_out,
    fine_out,
    merged_out,
    coarse_out,
    cnorm_out,
):
    gain, shift = (vector(gain_ref), vector(shift_ref))
    own = own_ref[...].astype(F32)
    for place, tokens in enumerate(
        [own, par_ref[...].astype(F32)]
        + [unpacked_side(ref[...].astype(F32)) for ref in (upo_ref, upp_ref, dno_ref, dnp_ref)]
    ):
        hat, _ = norm_parts(tokens)
        at = slice(SOURCES[place], SOURCES[place] + tokens.shape[0])
        hat_out[at, :] = hat
        normed[at, :] = (hat * gain + shift).astype(BF16)
    bias = vector(qkv_bias_ref)
    q_out[...] = rounded(dot(normed[0:FINE, :], qkv_ref[:, 0:C_F]) + bias[:, 0:C_F])
    k_out[...] = rounded(dot(normed[...], qkv_ref[:, C_F : 2 * C_F]) + bias[:, C_F : 2 * C_F])
    v_out[...] = rounded(dot(normed[...], qkv_ref[:, 2 * C_F :]) + bias[:, 2 * C_F :])
    kinds = fine_kinds()
    probs_refs = {"a": (bias_a, probs_a), "b": (bias_b, probs_b), "c": (bias_c, probs_c)}
    mixtures = {}
    for zone in range(2):
        for name, (start, count), pieces in fine_windows(zone):
            rows, mask = kinds[name][:2]
            bias_ref, probs_ref = probs_refs[name]
            probs, mixture = attend(
                q_out[start : start + count, :],
                gathered(k_out, pieces),
                gathered(v_out, pieces),
                rows,
                mask,
                bias_ref[zone],
            )
            probs_ref[zone] = probs
            mixtures[name, zone] = mixture
    mixture = jnp.concatenate([mixtures[name, zone] for name in "cab" for zone in range(2)], 0)
    mix_out[...] = mixture.astype(BF16)
    attn = rounded(dot(mixture, proj_ref[...]) + vector(proj_bias_ref))
    fine = rounded(own + attn)
    fine_out[...] = fine.astype(BF16)
    quartet = dot(quartet_order(), fine)
    parts = [quartet[p * COARSE : (p + 1) * COARSE] for p in range(4)]
    hats, _ = quartet_norm(parts)
    coarse = None
    gain, shift = (vector(merge_gain_ref), vector(merge_shift_ref))
    for p in range(4):
        at = slice(p * C_F, (p + 1) * C_F)
        value = (hats[p] * gain[:, at] + shift[:, at]).astype(BF16)
        merged_out[p] = value
        part = dot(value, merge_ref[p * C_F : (p + 1) * C_F, :])
        coarse = part if coarse is None else coarse + part
    coarse = rounded(coarse)
    coarse_out[...] = coarse
    hat, _ = norm_parts(coarse)
    cnorm_out[...] = (hat * vector(coarse_gain_ref) + vector(coarse_shift_ref)).astype(BF16)


def quartet_norm(parts):
    width = 4.0 * C_F
    mean = sum(jnp.sum(part, -1, keepdims=True) for part in parts) / width
    centres = [part - mean for part in parts]
    spread = sum(jnp.sum(c * c, -1, keepdims=True) for c in centres) / width
    scale = lax.rsqrt(spread + EPS)
    return ([c * scale for c in centres], scale)


def coarse_body(
    group_ref,
    own_ref,
    coarse_ref,
    cot_ref,
    qkv_ref,
    qkv_bias_ref,
    proj_ref,
    proj_bias_ref,
    bias_ref,
    out_ref,
    parts_out,
    own_out,
    flat_out,
    table_out,
    cot_out,
    stage,
    keys,
    values,
):
    fetch_groups(stage, cot_ref)
    order = coarse_order()
    cot = dot(order, stage[...])
    cot_out[...] = cot
    bias = vector(qkv_bias_ref)
    wide = [slice(i * C_C, (i + 1) * C_C) for i in range(3)]
    queries = rounded(dot(own_ref[...], qkv_ref[:, wide[0]]) + bias[:, wide[0]])
    group = jnp.concatenate([group_ref[g] for g in range(4)], 0)
    keys[...] = rounded(dot(group, qkv_ref[:, wide[1]]) + bias[:, wide[1]])
    values[...] = rounded(dot(group, qkv_ref[:, wide[2]]) + bias[:, wide[2]])
    mixture_grad = rounded(dot_nt(cot, proj_ref[...]))
    rows, mask, _ = head_rows(HEADS_C, 6, 3, 40, 144)
    toep = toeplitz(group_keys(), 3, 3 * lax.rem(lax.axis_index("lon"), 4).astype(F32))
    mixtures, query_grads, grads = ([], [], [])
    for zone in range(2):
        here = slice(zone * 40, (zone + 1) * 40)
        at = [slice(g * COARSE + zone * 40, g * COARSE + zone * 40 + 40) for g in range(4)]
        k = jnp.concatenate([keys[there, :] for there in at], 0)
        v = jnp.concatenate([values[there, :] for there in at], 0)
        probs, mixture = attend(queries[here], k, v, rows, mask, bias_ref[zone])
        dq, dk, dv, table = attend_back(
            queries[here], k, v, rows, mask, probs, mixture_grad[here], toep, 144
        )
        table_out[zone * 144 : (zone + 1) * 144, :] = table
        mixtures.append(mixture)
        query_grads.append(dq)
        grads.append((dk, dv))
    key_grad, value_grad = (
        rounded(
            jnp.concatenate(
                [grads[zone][i][g * 40 : (g + 1) * 40] for g in range(4) for zone in range(2)], 0
            )
        )
        for i in range(2)
    )
    query_grad = jnp.concatenate(query_grads, 0)
    part = dot_nt(key_grad, qkv_ref[:, wide[1]]) + dot_nt(value_grad, qkv_ref[:, wide[2]])
    for g in range(4):
        parts_out[g] = part[g * COARSE : (g + 1) * COARSE].astype(BF16)
    own_out[...] = dot_nt(query_grad, qkv_ref[:, wide[0]])
    for i, (norm, grad) in enumerate(
        ((own_ref[...], query_grad), (group, key_grad), (group, value_grad))
    ):
        weight = dot_tn(norm, grad)
        sums = column_sum(grad)
        for c in range(3):
            lanes = slice(c * 128, (c + 1) * 128)
            flat_out[pl.ds(3 * i + c, C_C, stride=9), :] = weight[:, lanes]
            flat_out[3456 + 3 * i + c : 3457 + 3 * i + c, :] = sums[:, lanes]
    mixture = jnp.concatenate(mixtures, 0)
    flat_store(flat_out, 3465, dot_tn(mixture, cot))
    flat_store(flat_out, 4617, column_sum(cot))
    attn = rounded(dot(mixture, proj_ref[...]) + vector(proj_bias_ref))
    stage[...] = dot_tn(order, coarse_ref[...] + attn)
    store_groups(out_ref, stage)


def flat_store(flat, start, matrix):
    height, width = matrix.shape
    step = width // 128
    for c in range(step):
        lanes = slice(c * 128, (c + 1) * 128)
        if height == 1:
            flat[start + c : start + c + 1, :] = matrix[:, lanes]
        else:
            flat[pl.ds(start + c, height, stride=step), :] = matrix[:, lanes]


def keep_square(square, matrix):
    height = matrix.shape[0]
    square[0, 0:height, :] = matrix[:, 0:128]
    square[1, 0:height, 0:64] = matrix[:, 128:192]


def every_other(square, start):
    take = pl.ds(start, 96, stride=2)
    return jnp.concatenate([square[0, take, :], square[1, take, :][:, 0:64]], 1)


def block_store(flat, start, blocks):
    for c, block in enumerate(blocks):
        if block.shape[0] == 1:
            flat[start + c : start + c + 1, :] = block
        else:
            flat[pl.ds(start + c, block.shape[0], stride=len(blocks)), :] = block


def fine_back_body(
    starts,
    rows,
    part_ref,
    own_part_ref,
    cot_ref,
    coarse_ref,
    merged_ref,
    fine_ref,
    hat_ref,
    normed_ref,
    mix_ref,
    q_ref,
    k_ref,
    v_ref,
    probs_a,
    probs_b,
    probs_c,
    qkv_ref,
    cgain_ref,
    merge_gain_ref,
    merge_ref,
    proj_ref,
    flat_c,
    table_q,
    fog_out,
    own_out,
    par_out,
    upo_out,
    upp_out,
    dno_out,
    dnp_out,
    pieces_out,
    tables_out,
    kgrad,
    vgrad,
    flat,
    tables,
    square,
):
    norm_grad = part_ref[...] + own_part_ref[...]
    hat, scale = norm_parts(coarse_ref[...])
    flat_store(flat, 3477, column_sum(norm_grad * hat))
    flat_store(flat, 3480, column_sum(norm_grad))
    coarse_grad = rounded(cot_ref[...] + norm_back(hat, scale, norm_grad, vector(cgain_ref)))
    quartet_sel = quartet_order()
    quartet = dot(quartet_sel, fine_ref[...])
    hats, scale = quartet_norm([quartet[p * COARSE : (p + 1) * COARSE] for p in range(4)])
    inners, gains, shifts = ([], [], [])
    merge_gain = vector(merge_gain_ref)
    for p in range(4):
        at = slice(p * C_F, (p + 1) * C_F)
        flat_store(flat, 1173 + 3 * p * C_F, dot_tn(merged_ref[p], coarse_grad))
        grad = dot_nt(coarse_grad, merge_ref[at, :])
        gains.append(column_sum(grad * hats[p]))
        shifts.append(column_sum(grad))
        inners.append(grad * merge_gain[:, at])
    block_store(flat, 1161, lane_blocks(gains))
    block_store(flat, 1167, lane_blocks(shifts))
    width = 4.0 * C_F
    first = sum(jnp.sum(inner, -1, keepdims=True) for inner in inners) / width
    second = sum(jnp.sum(i * h, -1, keepdims=True) for i, h in zip(inners, hats)) / width
    grads = jnp.concatenate([scale * (i - first - h * second) for i, h in zip(inners, hats)], 0)
    high = rounded(grads)
    attn_grad = dot_tn(quartet_sel, high)
    fog_out[...] = attn_grad + dot_tn(quartet_sel, grads - high)
    mixture_grad = rounded(dot_nt(attn_grad, proj_ref[...]))
    weight = dot_tn(mix_ref[...], attn_grad)
    corner = weight[0:1]
    keep_square(square, jnp.concatenate([weight, column_sum(attn_grad)], 0))
    block_store(flat, 873, lane_blocks([every_other(square, 1), every_other(square, 2)]))
    kinds = fine_kinds()
    places = {"a": (PART_A, probs_a), "b": (PART_B, probs_b), "c": (PART_C, probs_c)}
    query_grads = {}
    for zone in range(2):
        for name, (start, count), pieces in fine_windows(zone):
            rows_at, mask, _, _, toep, block = kinds[name]
            table_at, probs_ref = places[name]
            dq, dk, dv, table = attend_back(
                q_ref[start : start + count, :],
                gathered(k_ref, pieces),
                gathered(v_ref, pieces),
                rows_at,
                mask,
                probs_ref[zone],
                mixture_grad[start : start + count],
                toep,
                block,
            )
            query_grads[name, zone] = dq
            for c in range(3):
                at = table_at + (2 * c + zone) * block
                tables[at : at + block, :] = table[:, c * 128 : (c + 1) * 128]
            at = 0
            for source, begin, size in pieces:
                to = slice(SOURCES[source] + begin, SOURCES[source] + begin + size)
                kgrad[to, :] = rounded(dk[at : at + size])
                vgrad[to, :] = rounded(dv[at : at + size])
                at += size
    query_grad = jnp.concatenate([query_grads[name, zone] for name in "cab" for zone in range(2)], 0)
    part = dot_nt(kgrad[...], qkv_ref[:, C_F : 2 * C_F]) + dot_nt(vgrad[...], qkv_ref[:, 2 * C_F :])
    own = part[0:FINE] + dot_nt(query_grad, qkv_ref[:, 0:C_F])
    own_out[...] = own
    par_out[...] = part[FINE : 2 * FINE].astype(BF16)
    for place, out in enumerate((upo_out, upp_out, dno_out, dnp_out)):
        at = SOURCES[2 + place]
        out[...] = packed_side(part[at : at + SIDE]).astype(BF16)
    hat_grad = column_sum(own * hat_ref[0:FINE, :])
    hat_grad += column_sum(part[FINE:] * hat_ref[FINE:, :])
    block_store(
        flat, 0, lane_blocks([hat_grad, column_sum(own) + column_sum(part[FINE:])])
    )
    evens, odds, sums = ([], [], [])
    for norm, grad in (
        (normed_ref[0:FINE, :], query_grad),
        (normed_ref[...], kgrad[...]),
        (normed_ref[...], vgrad[...]),
    ):
        keep_square(square, dot_tn(norm, grad))
        evens.append(every_other(square, 0))
        odds.append(every_other(square, 1))
        sums.append(column_sum(grad))
    block_store(flat, 3, lane_blocks(evens + odds))
    block_store(flat, 867, lane_blocks(sums + [corner]))
    tables[240:PART_A, :] = jnp.zeros((PART_A - 240, 128), F32)
    tables[PART_END:, :] = jnp.zeros((TABLE_ROWS - PART_END, 128), F32)
    for c in range(3):
        at = PART_Q + 288 * c
        tables[at : at + 288, :] = table_q[:, c * 128 : (c + 1) * 128]
    split = 3483
    trows = TABLE_ROWS // len(starts)
    for place, start in starts:
        end = start + rows
        if start < split:
            size = min(end, split) - start
            value = flat[start : start + size, :]
            if end > split:
                value = jnp.concatenate([value, flat_c[0 : end - split, :]], 0)
        else:
            size = min(end, 8103) - start
            value = flat_c[start - split : start - split + size, :]
            if size < rows:
                value = jnp.concatenate([value, jnp.zeros((rows - size, 128), F32)], 0)
        chunk = pieces_out.shape[2]
        for y in range(pieces_out.shape[0]):
            pieces_out[y, place] = value[y * chunk : (y + 1) * chunk].astype(BF16)
        tables_out[place] = tables[place * trows : (place + 1) * trows, :].astype(BF16)


def final_body(
    x_ref,
    gain_ref,
    fog_ref,
    own_ref,
    par_ref,
    low_ref,
    high_ref,
    t_ref,
    token_out,
    fine_out,
    coarse_out,
    stage,
    grad,
):
    grad[...] = own_ref[...] + par_ref[...].astype(F32)
    grad[LOW : LOW + SIDE, :] += unpacked_side(low_ref[...].astype(F32))
    grad[TOP : TOP + SIDE, :] += unpacked_side(high_ref[...].astype(F32))
    hat, scale = norm_parts(x_ref[...].astype(F32))
    total = fog_ref[...] + norm_back(hat, scale, rounded(grad[...]), vector(gain_ref))
    stage[...] = dot_tn(fine_order(), total)
    store_groups(token_out, stage)

    def part(start, height):
        return jnp.concatenate(
            [t_ref[start + c * height : start + (c + 1) * height, :] for c in range(3)], 1
        )

    def natural(kind, block):
        total = None
        for zk in range(2):
            term = dot_tn(table_rows(kind, zk), dot_nt(block, table_lanes(zk)))
            total = term if total is None else total + term
        return total

    fine_out[0:288, :] = natural("a", part(PART_A, 144))
    fine_out[288:576, :] = natural("b", part(PART_B, 80)) + natural("c", part(PART_C, 80))
    coarse_out[...] = natural("q", part(PART_Q, 288))


def mesh_parts(lat, lon):
    cores = 2
    xs = 4 if lon % 8 == 0 else 1
    ys = 4 if lat % 4 == 0 else lat
    return (cores, xs, lon // (cores * xs), ys, lat // ys)


def piece_rows(total, lon, ys):
    longest = -(-(127 + total // lon) // 128)
    unit = 16 * ys
    return -(-longest // unit) * unit


def reduce_body(
    dims,
    norm_factor,
    g_ref,
    gt_ref,
    par_ref,
    upo_ref,
    upp_ref,
    dno_ref,
    dnp_ref,
    p_ref,
    t_ref,
    par_out,
    low_out,
    high_out,
    par_buf,
    up_buf,
    down_buf,
    up_sum,
    down_sum,
    low_buf,
    high_buf,
    core_buf,
    head_buf,
    tail_buf,
    y_buf,
    y_sum,
    x_buf,
    x_sum,
    z_buf,
    h_send,
    h_buf,
    share,
    tab_core,
    tab_x,
    tab_sum,
    tab_own,
    tab_hand,
    tab_z,
    tab_all,
    send_sems,
    recv_sems,
):
    cores, xs, zs, ys, hs = dims
    half = xs * zs
    chunk = g_ref.shape[2]
    trows = gt_ref.shape[1]
    lat, lon = (lax.axis_index("lat"), lax.axis_index("lon"))
    core = lax.rem(lon, cores)
    x = lax.rem(lon // cores, xs)
    z = lon // (cores * xs)
    y = lax.rem(lat, ys)
    h = lat // ys
    lats = ys * hs

    def at(here, d, count):
        return lax.rem(here + d, count)

    def lon_of(core_to, x_to, z_to):
        return (z_to * xs + x_to) * cores + core_to

    other_core = (lat, lon_of(1 - core, x, z))
    x_peers = {d: (lat, lon_of(core, at(x, d, xs), z)) for d in range(1, xs)}
    y_peers = {d: (h * ys + at(y, d, ys), lon) for d in range(1, ys)}
    z_peers = {d: (lat, lon_of(core, x, at(z, d, zs))) for d in range(1, zs)}
    far = (at(h, 1, hs) * ys + y, lon)
    before, after = ((at(lat, lats - 1, lats), lon), (at(lat, 1, lats), lon))
    beside = (lat, partner_of(lon, cores * half))
    peers = [before, after] + ([far] if hs > 1 else [])
    peers += list(z_peers.values())[::-1] + list(y_peers.values()) + list(x_peers.values())
    peers += [beside, other_core]
    meet(peers)
    pending = []

    def send(src, dst, peer):
        sem = len(pending)
        copy = start_copy(src, dst, send_sems.at[sem], recv_sems.at[sem], peer)
        pending.append(copy)
        return copy

    def arrived(copies):
        for copy in copies:
            copy.wait_recv()

    def add_into(target, terms, count):
        def step(i, carry):
            total = terms[0](i).astype(F32)
            for term in terms[1:]:
                total = total + term(i).astype(F32)
            target[i] = total.astype(BF16)
            return carry

        lax.fori_loop(0, count, step, 0)

    away = pl.ds((1 - core) * half, half)
    mine = core * half
    table_core = send(gt_ref.at[away], tab_core, other_core)
    edges = [
        send(upp_ref, up_buf, beside),
        send(dnp_ref, down_buf, beside),
        send(par_ref, par_buf, beside),
    ]
    order = {4: (2, 1, 3, 0), 2: (1, 0), 1: (0,)}[ys]
    crossing = {d: send(g_ref.at[at(y, d, ys), away], core_buf.at[d], other_core) for d in order}
    table_core.wait_recv()
    add_into(tab_core, [lambda i: tab_core[i], lambda i: gt_ref[mine + i]], half)
    table_x = [
        send(tab_core.at[pl.ds(at(x, d, xs) * zs, zs)], tab_x.at[d - 1], x_peers[d])
        for d in range(1, xs)
    ]
    cut = half // 2
    head, tail = (pl.ds(0, cut), pl.ds(cut, half - cut))
    gathered_y = []
    for d in order:
        crossing[d].wait_recv()
        row = at(y, d, ys)
        buf = core_buf.at[d]
        add_into(buf, [lambda i: buf[i], lambda i: g_ref[row, mine + i]], half)
        if ys == 4 and d == 2:
            over_right = send(core_buf.at[2, head], head_buf, y_peers[1])
            over_left = send(core_buf.at[2, tail], tail_buf, y_peers[3])
        if ys == 4 and d == 1:
            gathered_y.append(send(core_buf.at[1, tail], y_buf.at[0, tail], y_peers[1]))
        if ys == 4 and d == 3:
            gathered_y.append(send(core_buf.at[3, head], y_buf.at[1, head], y_peers[3]))
        if ys == 2 and d == 1:
            gathered_y.append(send(core_buf.at[1], y_buf.at[0], y_peers[1]))
    if ys == 4:
        over_right.wait_recv()
        right = core_buf.at[1]
        add_into(right, [lambda i: right[i], lambda i: head_buf[i]], cut)
        gathered_y.append(send(core_buf.at[1, head], y_buf.at[0, head], y_peers[1]))
        over_left.wait_recv()
        left = core_buf.at[3, tail]
        add_into(left, [lambda i: left[i], lambda i: tail_buf[i]], half - cut)
        gathered_y.append(send(core_buf.at[3, tail], y_buf.at[1, tail], y_peers[3]))

    arrived(edges[:2])
    up_sum[...] = (upo_ref[...].astype(F32) + up_buf[...].astype(F32)).astype(BF16)
    down_sum[...] = (dno_ref[...].astype(F32) + down_buf[...].astype(F32)).astype(BF16)
    edges.append(send(up_sum, low_buf, after))
    edges.append(send(down_sum, high_buf, before))
    arrived(table_x)
    base = x * zs
    terms = [lambda i: tab_core[base + i]]
    terms += [lambda i, d=d: tab_x[d - 1, i] for d in range(1, xs)]
    add_into(tab_sum, terms, zs)
    table_z = [
        send(tab_sum.at[at(z, d, zs)], tab_z.at[d - 1], z_peers[d]) for d in range(1, zs)
    ]

    arrived(gathered_y)
    terms = [lambda i: core_buf[0, i]]
    terms += [lambda i, d=d: y_buf[d, i] for d in range({4: 2, 2: 1, 1: 0}[ys])]
    add_into(y_sum, terms, half)
    along_x = [
        send(y_sum.at[pl.ds(at(x, d, xs) * zs, zs)], x_buf.at[d - 1], x_peers[d])
        for d in range(1, xs)
    ]

    arrived(table_z)
    total = tab_sum[z].astype(F32)
    for d in range(1, zs):
        total = total + tab_z[d - 1].astype(F32)
    own = tab_all.at[core, x, z]
    tab_own[...] = (total * norm_factor).astype(BF16)
    tab_all[core, x, z] = tab_own[...]
    first_row = ((core * xs + x) * zs + z) * trows

    def prepared(src, dst, peer):
        sem = len(pending)
        copy = pltpu.make_async_remote_copy(
            src_ref=src,
            dst_ref=dst,
            send_sem=send_sems.at[sem],
            recv_sem=recv_sems.at[sem],
            device_id=peer,
            device_id_type=MESH,
        )
        pending.append(copy)
        return copy

    handed = prepared(tab_own, tab_hand, before)
    pending.pop()
    pending.append(None)
    back_z = [prepared(own, own, z_peers[d]) for d in range(1, zs)]

    @pl.when(first_row < PART_A)
    def _():
        handed.start()

    @pl.when(first_row >= PART_A)
    def _():
        for copy in back_z:
            copy.start()

    arrived(along_x)
    terms = [lambda i: y_sum[base + i]]
    terms += [lambda i, d=d: x_buf[d - 1, i] for d in range(1, xs)]
    add_into(x_sum, terms, zs)
    along_z = [send(x_sum.at[at(z, d, zs)], z_buf.at[d - 1], z_peers[d]) for d in range(1, zs)]

    @pl.when(first_row < PART_A)
    def _():
        handed.wait()
        row = first_row + lax.broadcasted_iota(jnp.int32, (trows, 128), 0)
        tab_all[core, x, z] = jnp.where(
            row < PART_A, tab_hand[...].astype(F32), tab_own[...].astype(F32)
        ).astype(BF16)
        for copy in back_z:
            copy.start()

    arrived(along_z)
    total = x_sum[z].astype(F32)
    for d in range(1, zs):
        total = total + z_buf[d - 1].astype(F32)
    if hs > 1:
        h_send[...] = total.astype(BF16)
        across = send(h_send, h_buf, far)
    arrived(back_z)
    own = tab_all.at[core, x]
    back_x = [send(own, own, x_peers[d]) for d in range(1, xs)]
    if hs > 1:
        across.wait_recv()
        total = h_send[...].astype(F32) + h_buf[...].astype(F32)
    rows = pl.ds(pl.multiple_of(y * chunk, 8), chunk)
    share[rows, :] = total * norm_factor
    back_y = [send(share.at[rows], share.at[rows], y_peers[d]) for d in range(1, ys)]
    arrived(back_x)
    own = tab_all.at[core]
    back_core = send(own, own, other_core)
    arrived(edges[2:])
    par_out[...] = par_buf[...]
    low_out[...] = low_buf[...]
    high_out[...] = high_buf[...]
    arrived(back_y)
    p_ref[...] = share[...]
    back_core.wait_recv()
    t_ref[...] = tab_all[...]
    for copy in pending:
        if copy is not None:
            copy.wait_send()


def reduce_all(pieces, tables, edges, norm_factor, dims):
    cores, xs, zs, ys, hs = dims
    half = xs * zs
    chunk = pieces.shape[2]
    trows = tables.shape[1]
    sem = pltpu.SemaphoreType.DMA((64,))
    vmem = pl.BlockSpec(memory_space=pltpu.VMEM)
    side = (128, 128)
    all_tables = (cores, xs, zs, trows, 128)
    outs = [((ys * chunk, 128), F32), (all_tables, BF16), ((FINE, C_F), BF16)]
    outs += [(side, BF16), (side, BF16)]
    buffers = [
        (FINE, C_F),
        *[side] * 6,
        (ys, half, chunk, 128),
        (half // 2, chunk, 128),
        (half - half // 2, chunk, 128),
        (2, half, chunk, 128),
        (half, chunk, 128),
        (max(xs - 1, 1), zs, chunk, 128),
        (zs, chunk, 128),
        (max(zs - 1, 1), chunk, 128),
        (chunk, 128),
        (chunk, 128),
        None,
        (half, trows, 128),
        (max(xs - 1, 1), zs, trows, 128),
        (zs, trows, 128),
        (trows, 128),
        (trows, 128),
        (max(zs - 1, 1), trows, 128),
        all_tables,
    ]
    scratch = [
        pltpu.VMEM((ys * chunk, 128), F32) if shape is None else pltpu.VMEM(shape, BF16)
        for shape in buffers
    ]
    return pl.pallas_call(
        functools.partial(reduce_body, dims, norm_factor),
        out_shape=tuple(jax.ShapeDtypeStruct(shape, dtype) for shape, dtype in outs),
        in_specs=[vmem] * 7,
        out_specs=(vmem,) * 5,
        scratch_shapes=scratch + [sem, sem],
        compiler_params=pltpu.CompilerParams(
            collective_id=7, has_side_effects=True, vmem_limit_bytes=VMEM_BYTES
        ),
        cost_estimate=lasting(35),
        name="grad_reduce",
    )(pieces, tables, *edges)


def shards(
    tokens,
    fine_gain,
    fine_shift,
    fine_qkv,
    fine_qkv_bias,
    fine_proj,
    fine_proj_bias,
    fine_table,
    merge_gain,
    merge_shift,
    merge_weight,
    coarse_gain,
    coarse_shift,
    coarse_qkv,
    coarse_qkv_bias,
    coarse_proj,
    coarse_proj_bias,
    coarse_table,
    cotangent,
):
    lat_count, lon_count = (lax.axis_size("lat"), lax.axis_size("lon"))
    lat, lon = (lax.axis_index("lat"), lax.axis_index("lon"))
    norm_factor = 1.0 / math.sqrt(tokens.size // C_F * lat_count * lon_count / 4)
    fine_rows = fine_table.reshape(576, 138)
    coarse_rows = coarse_table.reshape(576, 138)
    cells = tokens[0].transpose(1, 2, 0, 3)
    cot_cells = cotangent[0].transpose(1, 2, 0, 3)

    group = min(8, lon_count)
    side = ((128, 128), BF16)
    own = ((FINE, C_F), BF16)
    table_part = ((group, PART_A // group, 128), BF16)
    x, low, high, table_send = call(
        prepare_body,
        [own, side, side, table_part],
        (cells, fine_rows),
        [pltpu.VMEM((288, C_F), F32)],
        "prepare",
        2,
    )
    halo = [own, side, side, side, side, table_part]
    par, upo, upp, dno, dnp, table_before = exchange_call(
        halo_body,
        halo,
        (x, low, high, table_send),
        [pltpu.VMEM(*s) for s in halo],
        (6, max(group - 1, 1)),
        1,
        "halo",
        10,
    )
    bias_a, bias_b, bias_c, bias_q = call(
        bias_body,
        [((2, 432, 144), F32), ((2, 240, 160), F32), ((2, 240, 160), F32), ((2, 432, 160), F32)],
        (fine_rows, table_before.reshape(PART_A, 128), coarse_rows),
        (),
        "bias_terms",
        4,
    )
    (
        hat,
        normed,
        q,
        k,
        v,
        probs_a,
        probs_b,
        probs_c,
        mixture,
        fine_out,
        merged,
        coarse,
        cnorm,
    ) = call(
        fine_forward_body,
        [
            ((ALL_ROWS, C_F), F32),
            ((ALL_ROWS, C_F), BF16),
            ((FINE, C_F), F32),
            ((ALL_ROWS, C_F), F32),
            ((ALL_ROWS, C_F), F32),
            ((2, 432, 144), F32),
            ((2, 240, 160), F32),
            ((2, 240, 160), F32),
            own,
            own,
            ((4, COARSE, C_F), BF16),
            ((COARSE, C_C), F32),
            ((COARSE, C_C), BF16),
        ],
        (
            x,
            par,
            upo,
            upp,
            dno,
            dnp,
            fine_gain,
            fine_shift,
            fine_qkv,
            fine_qkv_bias,
            fine_proj,
            fine_proj_bias,
            merge_gain,
            merge_shift,
            merge_weight,
            coarse_gain,
            coarse_shift,
            bias_a,
            bias_b,
            bias_c,
        ),
        (),
        "fine_forward",
        10,
    )
    gathered_to = [((4, COARSE, C_C), BF16)]
    (gathered_norm,) = exchange_call(
        group_body, gathered_to, (cnorm,), [pltpu.VMEM(*gathered_to[0])], (3,), 2, "coarse_gather", 5
    )
    coarse_out, parts, own_part, flat_c, table_q, cot = call(
        coarse_body,
        [
            ((6, 3, 4, C_C), BF16),
            ((4, COARSE, C_C), BF16),
            ((COARSE, C_C), F32),
            ((4620, 128), F32),
            ((288, 384), F32),
            ((COARSE, C_C), F32),
        ],
        (
            gathered_norm,
            cnorm,
            coarse,
            cot_cells,
            coarse_qkv,
            coarse_qkv_bias,
            coarse_proj,
            coarse_proj_bias,
            bias_q,
        ),
        [
            pltpu.VMEM((72, C_C), F32),
            pltpu.VMEM((4 * COARSE, C_C), F32),
            pltpu.VMEM((4 * COARSE, C_C), F32),
        ],
        "coarse_attention",
        7,
    )
    (norm_part,) = exchange_call(
        ungroup_body,
        [((COARSE, C_C), F32)],
        (parts,),
        [pltpu.VMEM((3, COARSE, C_C), BF16)],
        (3,),
        3,
        "coarse_scatter",
        5,
    )
    dims = mesh_parts(lat_count, lon_count)
    cores, xs, zs, ys, hs = dims
    segment = PARAMS // lon_count
    rows = piece_rows(PARAMS, lon_count, ys)
    starts = []
    for index in range(lon_count):
        core, x_at, z_at = (index % cores, index // cores % xs, index // (cores * xs))
        starts.append(((core * xs + x_at) * zs + z_at, index * segment // 128))
    trows = TABLE_ROWS // lon_count
    fine_out_grad, own_grad, *edges, pieces, table_pieces = call(
        functools.partial(fine_back_body, starts, rows),
        [
            ((FINE, C_F), F32),
            ((FINE, C_F), F32),
            own,
            side,
            side,
            side,
            side,
            ((ys, lon_count, rows // ys, 128), BF16),
            ((lon_count, trows, 128), BF16),
        ],
        (
            norm_part,
            own_part,
            cot,
            coarse,
            merged,
            fine_out,
            hat,
            normed,
            mixture,
            q,
            k,
            v,
            probs_a,
            probs_b,
            probs_c,
            fine_qkv,
            coarse_gain,
            merge_gain,
            merge_weight,
            fine_proj,
            flat_c,
            table_q,
        ),
        [
            pltpu.VMEM((ALL_ROWS, C_F), F32),
            pltpu.VMEM((ALL_ROWS, C_F), F32),
            pltpu.VMEM((3488, 128), F32),
            pltpu.VMEM((TABLE_ROWS, 128), F32),
            pltpu.VMEM((2, 200, 128), F32),
        ],
        "fine_backward",
        9,
    )
    owned, table_sum, par_back, low_back, high_back = reduce_all(
        pieces, table_pieces, edges, norm_factor, dims
    )
    shift = lax.rem(lon * segment, 128)
    param_grads = lax.dynamic_slice(owned.reshape(-1), (shift,), (segment,))
    token_grad, fine_total, coarse_total = call(
        final_body,
        [((12, 6, 4, C_F), BF16), ((576, 138), F32), ((576, 138), F32)],
        (
            x,
            fine_gain,
            fine_out_grad,
            own_grad,
            par_back,
            low_back,
            high_back,
            table_sum.reshape(TABLE_ROWS, 128),
        ),
        [pltpu.VMEM((288, C_F), F32), pltpu.VMEM((FINE, C_F), F32)],
        "final",
        2,
    )
    return (
        coarse_out.transpose(2, 0, 1, 3)[None],
        token_grad.transpose(2, 0, 1, 3)[None],
        param_grads,
        fine_total.reshape(2, -1),
        coarse_total.reshape(2, -1),
    )


def solution(mesh):
    tiles = P(None, None, "lat", "lon", None)
    whole = P()
    rows = P("lat", None)
    return jax.shard_map(
        shards,
        mesh=mesh,
        in_specs=(tiles,) + (whole,) * 6 + (rows,) + (whole,) * 9 + (rows, tiles),
        out_specs=(tiles, tiles, P("lon"), rows, rows),
        check_vma=False,
    )
```

```python
import functools
import math

import jax
import jax.numpy as jnp
from jax import lax
from jax.experimental import pallas as pl
from jax.experimental.pallas import tpu as pltpu
from jax.sharding import PartitionSpec as P

HEAD = 32
HEADS_F = 6
HEADS_C = 12
C_F = 192
C_C = 384
SPAN = 23
EPS = 1e-05
NEGATIVE = -1e30
MESH = pl.DeviceIdType.MESH
F32 = jnp.float32
BF16 = jnp.bfloat16
MIB = 1024 * 1024
VMEM_BYTES = 28 * MIB

LOW, MID, TOP = (0, 80, 224)
PARAMS = 1037184
TABLE_ROWS = 2048
FINE = 304
SIDE = 80
COARSE = 80
PART_C, PART_A, PART_B, PART_Q, PART_END = (0, 256, 688, 928, 1792)


def whole(x, n):
    return jnp.floor((x + 0.5) * (1.0 / n))


def rest(x, n):
    return x - n * whole(x, n)


def down_rows(n):
    return lax.broadcasted_iota(jnp.int32, (n, 1), 0).astype(F32)


def along_lanes(n):
    return lax.broadcasted_iota(jnp.int32, (1, n), 1).astype(F32)


def index_and_other(n, m, flip):
    return (along_lanes(n), down_rows(m)) if flip else (down_rows(n), along_lanes(m))


def match(a, b):
    return jnp.where(a == b, 1.0, 0.0).astype(BF16)


def fine_row(zone, zq, row, col):
    low = LOW + zone * 40 + (zq * 3 + row) * 6 + col
    mid = MID + zone * 72 + (zq * 6 + row - 3) * 6 + col
    top = TOP + zone * 40 + (zq * 3 + row - 9) * 6 + col
    return jnp.where(row < 3, low, jnp.where(row < 9, mid, top))


def fine_order(flip=False):
    at, cells = index_and_other(FINE, 288, flip)
    low, top = (at < MID, at >= TOP)
    edge = jnp.where(top, at - TOP, at)
    mid = at - MID
    in_edge = low | top
    part = rest(edge, 40)
    zone = jnp.where(in_edge, whole(edge, 40), whole(mid, 72))
    zq = jnp.where(in_edge, whole(part, 18), whole(rest(mid, 72), 36))
    row = jnp.where(
        in_edge,
        whole(rest(part, 18), 6) + jnp.where(top, 9.0, 0.0),
        3 + whole(rest(mid, 36), 6),
    )
    col = jnp.where(in_edge, rest(part, 6), rest(mid, 6))
    code = (row * 6 + col) * 4 + rest(2 * zone + zq + 1, 4)
    return match(jnp.where(in_edge & (part >= 36), -1.0, code), cells)


def coarse_place(at):
    part = rest(at, 40)
    return (whole(at, 40), whole(part, 18), whole(rest(part, 18), 3), rest(part, 3), part < 36)


def coarse_order(flip=False):
    at, cells = index_and_other(COARSE, 72, flip)
    zone, zq, row, col, valid = coarse_place(at)
    code = (row * 3 + col) * 4 + 2 * zone + zq
    return match(jnp.where(valid, code, -1.0), cells)


def quartet_order(flip=False):
    at, tokens = index_and_other(4 * COARSE, FINE, flip)
    p = whole(at, COARSE)
    zone, zq, row, col, valid = coarse_place(rest(at, COARSE))
    rolled = rest(2 * zone + zq + 3, 4)
    source = fine_row(
        whole(rolled, 2), rest(rolled, 2), 2 * row + rest(p, 2), 2 * col + whole(p, 2)
    )
    return match(jnp.where(valid, source, -1.0), tokens)


def head_rows(heads, lats, cols, tokens, block):
    def parts(at):
        part = rest(at, block)
        zq = whole(rest(part, 2 * lats), lats)
        code = (zq * lats + rest(part, lats)) * cols + whole(at, block)
        valid = part < heads * 2 * lats
        return (jnp.where(valid, whole(part, 2 * lats), -1.0), zq, jnp.where(valid, code, -1.0))

    rows = block * cols
    h, zq, code = parts(down_rows(rows))
    mask = match(h, whole(along_lanes(heads * HEAD), HEAD)).astype(F32)
    back = match(parts(along_lanes(rows))[2], down_rows(tokens))
    return ((match(code, along_lanes(tokens)), back), mask, zq)


def pair_keys(size, half):
    u = along_lanes(size)
    if size == 144:
        source, part = (whole(u, 72), rest(u, 72))
        zk, ak, valid = (whole(part, 36), whole(rest(part, 36), 6), part >= 0)
    else:
        slot, part = (whole(u, 40), rest(u, 40))
        source = rest(slot, 2)
        zk = whole(part, 18)
        ak = 3 * whole(slot, 2) + whole(rest(part, 18), 6)
        valid = part < 36
    return (zk, ak, rest(part, 6) + 6 * jnp.abs(half - source), valid)


def group_keys():
    u = along_lanes(160)
    part = rest(u, 40)
    zk, ak = (whole(part, 18), whole(rest(part, 18), 3))
    return (zk, ak, rest(part, 3) + 3 * whole(u, 40), part < 36)


def toeplitz(keys, cols, shift):
    zk, ak, col, valid = keys
    at = down_rows(384)
    tail = at >= 256
    level = jnp.where(tail, whole(at - 256, 64), whole(at, 128))
    entry = jnp.where(tail, 128 + rest(at, 64), rest(at, 128))
    code = (level * 6 + whole(entry, SPAN)) * 64 + rest(entry, SPAN)
    code = jnp.where(entry < 138, code, -1.0)
    key_code = jnp.where(valid, (zk * 6 + ak) * 64 - col + shift + 11, -100.0)
    return [match(code, key_code + oq) for oq in range(cols)]


def table_lanes(zk):
    entry = down_rows(138)
    return match(
        jnp.where(entry < 128, zk * 128 + entry, 256 + zk * 64 + entry - 128), along_lanes(384)
    )


def table_rows(kind, zk, flip=False):
    if kind == "q":
        at, source = index_and_other(288, 576, flip)
        part = rest(at, 144)
        aq = rest(part, 6)
        lead = (whole(aq, 3) * 2 + whole(at, 144)) * HEADS_C + whole(part, 12)
        zq = whole(rest(part, 12), 6)
        return match(((lead * 2 + zq) * 2 + zk) * 3 + rest(aq, 3), source)
    if kind == "a":
        count, block, lats, first = (144, 72, 6, 0)
    else:
        count, block, lats, first = (80, 40, 3, 3 if kind == "c" else 0)
    at, source = index_and_other(count, 288, flip)
    part = rest(at, block)
    lead = whole(at, block) * HEADS_F + whole(part, 2 * lats)
    zq = whole(rest(part, 2 * lats), lats)
    code = ((lead * 2 + zq) * 2 + zk) * 6 + rest(part, lats) + first
    return match(jnp.where(part < 12 * lats, code, -1.0), source)


def dot(a, b):
    return jnp.dot(a.astype(BF16), b.astype(BF16), preferred_element_type=F32)


def dot_nt(a, b):
    return lax.dot_general(
        a.astype(BF16), b.astype(BF16), (((1,), (1,)), ((), ())), preferred_element_type=F32
    )


def dot_tn(a, b):
    return lax.dot_general(
        a.astype(BF16), b.astype(BF16), (((0,), (0,)), ((), ())), preferred_element_type=F32
    )


def rounded(value):
    return value.astype(BF16).astype(F32)


def norm_parts(volume):
    centre = volume - jnp.mean(volume, -1, keepdims=True)
    spread = jnp.mean(centre * centre, -1, keepdims=True)
    scale = lax.rsqrt(spread + EPS)
    return (centre * scale, scale)


def norm_back(hat, scale, grad, gain):
    inner = grad * gain
    return scale * (
        inner
        - jnp.mean(inner, -1, keepdims=True)
        - hat * jnp.mean(inner * hat, -1, keepdims=True)
    )


def column_sum(value):
    return jnp.sum(value, 0, keepdims=True)


def attend(queries, keys, values, rows, mask, bias):
    spread_out, back = rows
    packed = dot(spread_out, queries) * mask
    scores = dot_nt(packed, keys) * HEAD ** (-0.5) + bias
    weights = jnp.exp(scores - jnp.max(scores, -1, keepdims=True))
    probs = weights / jnp.sum(weights, -1, keepdims=True)
    mixture = dot(probs, values) * mask
    return (probs, dot(back, mixture))


def attend_back(queries, keys, values, rows, mask, probs, mixture_grad, toep, block):
    factor = HEAD ** (-0.5)
    spread_out, back = rows
    packed = dot(spread_out, queries) * mask
    grad = dot(spread_out, mixture_grad) * mask
    value_grad = dot_tn(probs, grad)
    prob_grad = dot_nt(grad, values)
    score_grad = probs * (prob_grad - jnp.sum(prob_grad * probs, -1, keepdims=True))
    query_grad = dot(back, dot(score_grad, keys) * factor * mask)
    key_grad = dot_tn(score_grad, packed) * factor
    table = None
    for oq, select in enumerate(toep):
        part = dot_nt(score_grad[oq * block : (oq + 1) * block], select)
        table = part if table is None else table + part
    return (query_grad, key_grad, value_grad, table)


def lasting(micros):
    return pl.CostEstimate(flops=int(micros * 2.0e9), bytes_accessed=int(micros * 3.69e6), transcendentals=int(micros * 1e6))


def call(body, outs, args, scratch, name, micros, in_place=(), limit=VMEM_BYTES):
    vmem = pl.BlockSpec(memory_space=pltpu.VMEM)
    away = pl.BlockSpec(memory_space=pltpu.HBM)
    return pl.pallas_call(
        body,
        out_shape=tuple(jax.ShapeDtypeStruct(shape, dtype) for shape, dtype in outs),
        in_specs=[away if at in in_place else vmem for at in range(len(args))],
        out_specs=(vmem,) * len(outs),
        scratch_shapes=list(scratch),
        compiler_params=pltpu.CompilerParams(vmem_limit_bytes=limit),
        cost_estimate=lasting(micros),
        name=name,
    )(*args)


def vector(ref):
    return ref[...].reshape(1, -1)


def query_half():
    return 1 - lax.rem(lax.axis_index("lon"), 2)


def packed_side(value):
    tail = jnp.concatenate([value[0:40, 128:192], value[40:80, 128:192]], 1)
    return jnp.concatenate([value[:, 0:128], tail, jnp.zeros((8, 128), value.dtype)], 0)


def unpacked_side(block):
    tail = jnp.concatenate([block[80:120, 0:64], block[80:120, 64:128]], 0)
    return jnp.concatenate([block[0:80, :], tail], 1)


def lane_blocks(pieces):
    blocks = []
    for a, b in zip(pieces[::2], pieces[1::2]):
        blocks += [a[:, 0:128], jnp.concatenate([a[:, 128:192], b[:, 0:64]], 1), b[:, 64:192]]
    return blocks


def partner_of(lon, count):
    odd = lax.rem(lon, 2)
    return lax.rem(lon + 2 * odd - 1 + count, count)


def ring_positions():
    lat_count, lon_count = (lax.axis_size("lat"), lax.axis_size("lon"))
    lat, lon = (lax.axis_index("lat"), lax.axis_index("lon"))
    up = lax.rem(lat + 1, lat_count)
    down = lax.rem(lat + lat_count - 1, lat_count)
    return (lat, lon, up, down, partner_of(lon, lon_count))


def meet(peers):
    barrier = pltpu.get_barrier_semaphore()
    for peer in peers:
        pl.semaphore_signal(barrier, inc=1, device_id=peer, device_id_type=MESH)
    pl.semaphore_wait(barrier, len(peers))


def start_copy(src, dst, send_sem, recv_sem, peer):
    copy = pltpu.make_async_remote_copy(
        src_ref=src,
        dst_ref=dst,
        send_sem=send_sem,
        recv_sem=recv_sem,
        device_id=peer,
        device_id_type=MESH,
    )
    copy.start()
    return copy


def exchange(sends, send_sems, recv_sems):
    copies = []
    for at, (src, dst, peer) in enumerate(sends):
        copies.append(start_copy(src, dst, send_sems.at[at], recv_sems.at[at], peer))
    for copy in copies:
        copy.wait_recv()
    for copy in copies:
        copy.wait_send()


def exchange_call(body, outs, args, scratch, counts, collective_id, name, micros):
    vmem = pl.BlockSpec(memory_space=pltpu.VMEM)
    sem = pltpu.SemaphoreType.DMA
    return pl.pallas_call(
        body,
        out_shape=tuple(jax.ShapeDtypeStruct(shape, dtype) for shape, dtype in outs),
        in_specs=[vmem] * len(args),
        out_specs=(vmem,) * len(outs),
        scratch_shapes=list(scratch) + [sem((count,)) for count in counts for _ in range(2)],
        compiler_params=pltpu.CompilerParams(
            collective_id=collective_id, has_side_effects=True, vmem_limit_bytes=VMEM_BYTES
        ),
        cost_estimate=lasting(micros),
        name=name,
    )(*args)


def halo_body(x_ref, low_ref, high_ref, tab_ref, tf_ref, tc_ref, *refs):
    outs, biases, bufs, (ss, rs, ts, tr) = (refs[:5], refs[5:9], refs[9:15], refs[15:])
    par, upo, upp, dno, dnp, tab = bufs
    lat, lon, up, down, partner = ring_positions()
    size = tab.shape[0]
    rank = lax.rem(lon, size)
    others = [lax.rem(rank + d, size) for d in range(1, size)]
    near = [(lat, lon - rank + other) for other in others]
    beside = (lat, partner)
    meet([(up, lon), (down, lon), beside] + near)
    low_copy = start_copy(low_ref, upo, ss.at[1], rs.at[1], (down, lon))
    high_copy = start_copy(high_ref, dno, ss.at[2], rs.at[2], (up, lon))
    table_copy = start_copy(tab_ref.at[rank], tab.at[rank], ss.at[3], rs.at[3], (up, lon))
    x_copy = start_copy(x_ref, par, ss.at[0], rs.at[0], beside)
    copies = [x_copy, low_copy, high_copy, table_copy]
    kinds = fine_kinds()
    store_bias("a", spread("a", tf_ref[0:288, :]), kinds["a"], biases[0])
    store_bias("b", spread("b", tf_ref[288:576, :]), kinds["b"], biases[1])
    store_bias("q", spread("q", tc_ref[...]), coarse_kind(), biases[3])
    low_copy.wait_recv()
    relays = [start_copy(upo, upp, ss.at[4], rs.at[4], beside)]
    high_copy.wait_recv()
    relays.append(start_copy(dno, dnp, ss.at[5], rs.at[5], beside))
    table_copy.wait_recv()
    for d, peer in enumerate(near):
        relays.append(start_copy(tab.at[rank], tab.at[rank], ts.at[d], tr.at[d], peer))
    x_copy.wait_recv()
    for copy in relays:
        copy.wait_recv()
    table = jnp.concatenate([tab[place].astype(F32) for place in range(size)], 0)
    table = jnp.concatenate([table[c * 80 : (c + 1) * 80] for c in range(3)], 1)
    store_bias("c", table, kinds["c"], biases[2])
    for copy in copies + relays:
        copy.wait_send()
    for out, buf in zip(outs, bufs):
        out[...] = buf[...]


def group_body(own_ref, out_ref, buf, ss, rs):
    lat, lon = (lax.axis_index("lat"), lax.axis_index("lon"))
    place = lax.rem(lon, 4)
    others = [lax.rem(place + d, 4) for d in range(1, 4)]
    peers = [(lat, lon - place + other) for other in others]
    meet(peers)
    buf[place] = own_ref[...]
    exchange([(own_ref, buf.at[place], peer) for peer in peers], ss, rs)
    out_ref[...] = buf[...]


def ungroup_body(parts_ref, out_ref, buf, ss, rs):
    lat, lon = (lax.axis_index("lat"), lax.axis_index("lon"))
    place = lax.rem(lon, 4)
    others = [lax.rem(place + d, 4) for d in range(1, 4)]
    peers = [(lat, lon - place + other) for other in others]
    meet(peers)
    exchange(
        [(parts_ref.at[other], buf.at[d], peers[d]) for d, other in enumerate(others)], ss, rs
    )
    total = parts_ref[place].astype(F32)
    for d in range(3):
        total = total + buf[d].astype(F32)
    out_ref[...] = total


def spread(kind, table):
    total = None
    for zk in range(2):
        part = dot(dot(table_rows(kind, zk), table), table_lanes(zk))
        total = part if total is None else total + part
    return total


def bias_rows(table, toep, zone, block):
    rows = table[zone * block : (zone + 1) * block]
    return jnp.concatenate([dot(rows, select) for select in toep], 0)


def banned(keys, zq, zone):
    ban = jnp.where(keys[3], 0.0, NEGATIVE)
    if zone == 1:
        ban = ban + jnp.where(zq == keys[0], 0.0, NEGATIVE)
    return ban


def fetch_groups(stage, ref):
    rows, cols = ref.shape[:2]
    for row in range(rows):
        for col in range(cols):
            at = (row * cols + col) * 4
            stage[at : at + 4, :] = ref[row, col].astype(F32)


def store_groups(ref, stage):
    rows, cols = ref.shape[:2]
    for row in range(rows):
        for col in range(cols):
            at = (row * cols + col) * 4
            ref[row, col] = stage[at : at + 4, :].astype(BF16)


def prepare_body(x_ref, tf_ref, own_out, low_out, high_out, tab_out, stage):
    fetch_groups(stage, x_ref)
    tokens = dot(fine_order(), stage[...])
    own_out[...] = tokens.astype(BF16)
    low_out[...] = packed_side(tokens[LOW : LOW + SIDE]).astype(BF16)
    high_out[...] = packed_side(tokens[TOP : TOP + SIDE]).astype(BF16)
    table = spread("c", tf_ref[288:576, :])
    pieces = [table[:, c * 128 : (c + 1) * 128] for c in range(3)]
    block = jnp.concatenate(pieces + [jnp.zeros((16, 128), F32)], 0).astype(BF16)
    size = tab_out.shape[1]
    for place in range(tab_out.shape[0]):
        tab_out[place] = block[place * size : (place + 1) * size, :]


def fine_kinds():
    half = query_half().astype(F32)
    rows_a, mask_a, zq_a = head_rows(HEADS_F, 6, 6, 72, 72)
    rows_b, mask_b, zq_b = head_rows(HEADS_F, 3, 6, 40, 40)
    keys_a, keys_b = (pair_keys(144, half), pair_keys(160, half))
    toep_a, toep_b = (toeplitz(keys_a, 6, 6 * half), toeplitz(keys_b, 6, 6 * half))
    mid = (rows_a, mask_a, zq_a, keys_a, toep_a, 72)
    edge = (rows_b, mask_b, zq_b, keys_b, toep_b, 40)
    return {"a": mid, "b": edge, "c": edge}


def store_bias(name, table, kind, out):
    _, _, zq, keys, toep, block = kind
    lat = lax.axis_index("lat")
    late = along_lanes(160) >= 80
    edge = {
        "a": 0.0,
        "b": jnp.where(late & (lat == lax.axis_size("lat") - 1), NEGATIVE, 0.0),
        "c": jnp.where(jnp.logical_not(late) & (lat == 0), NEGATIVE, 0.0),
        "q": 0.0,
    }[name]
    for zone in range(2):
        terms = bias_rows(table, toep, zone, block)
        out[zone] = terms + banned(keys, zq, 0 if name == "q" else zone) + edge


def coarse_kind():
    rows, mask, zq = head_rows(HEADS_C, 6, 3, 40, 144)
    keys = group_keys()
    toep = toeplitz(keys, 3, 3 * lax.rem(lax.axis_index("lon"), 4).astype(F32))
    return (rows, mask, zq, keys, toep, 144)


def fine_windows(zone):
    edge = zone * 40
    return (
        ("a", (MID + zone * 72, 72), [(0, MID + zone * 72, 72), (1, MID + zone * 72, 72)]),
        ("b", (TOP + edge, 40), [(0, TOP + edge, 40), (1, TOP + edge, 40), (2, edge, 40), (3, edge, 40)]),
        ("c", (LOW + edge, 40), [(4, edge, 40), (5, edge, 40), (0, LOW + edge, 40), (1, LOW + edge, 40)]),
    )


SOURCES = (0, FINE, 2 * FINE, 2 * FINE + SIDE, 2 * FINE + 2 * SIDE, 2 * FINE + 3 * SIDE)
ALL_ROWS = 2 * FINE + 4 * SIDE


def gathered(ref, pieces):
    return jnp.concatenate(
        [ref[SOURCES[source] + start : SOURCES[source] + start + count, :] for source, start, count in pieces],
        0,
    )


def fine_forward_body(
    own_ref,
    par_ref,
    upo_ref,
    upp_ref,
    dno_ref,
    dnp_ref,
    gain_ref,
    shift_ref,
    qkv_ref,
    qkv_bias_ref,
    proj_ref,
    proj_bias_ref,
    merge_gain_ref,
    merge_shift_ref,
    merge_ref,
    coarse_gain_ref,
    coarse_shift_ref,
    bias_a,
    bias_b,
    bias_c,
    hat_out,
    normed,
    q_out,
    k_out,
    v_out,
    probs_a,
    probs_b,
    probs_c,
    mix_out,
    fine_out,
    merged_out,
    coarse_out,
    cnorm_out,
):
    gain, shift = (vector(gain_ref), vector(shift_ref))
    own = own_ref[...].astype(F32)
    for place, tokens in enumerate(
        [own, par_ref[...].astype(F32)]
        + [unpacked_side(ref[...].astype(F32)) for ref in (upo_ref, upp_ref, dno_ref, dnp_ref)]
    ):
        hat, _ = norm_parts(tokens)
        at = slice(SOURCES[place], SOURCES[place] + tokens.shape[0])
        hat_out[at, :] = hat
        normed[at, :] = (hat * gain + shift).astype(BF16)
    bias = vector(qkv_bias_ref)
    q_out[...] = rounded(dot(normed[0:FINE, :], qkv_ref[:, 0:C_F]) + bias[:, 0:C_F])
    k_out[...] = rounded(dot(normed[...], qkv_ref[:, C_F : 2 * C_F]) + bias[:, C_F : 2 * C_F])
    v_out[...] = rounded(dot(normed[...], qkv_ref[:, 2 * C_F :]) + bias[:, 2 * C_F :])
    kinds = fine_kinds()
    probs_refs = {"a": (bias_a, probs_a), "b": (bias_b, probs_b), "c": (bias_c, probs_c)}
    mixtures = {}
    for zone in range(2):
        for name, (start, count), pieces in fine_windows(zone):
            rows, mask = kinds[name][:2]
            bias_ref, probs_ref = probs_refs[name]
            probs, mixture = attend(
                q_out[start : start + count, :],
                gathered(k_out, pieces),
                gathered(v_out, pieces),
                rows,
                mask,
                bias_ref[zone],
            )
            probs_ref[zone] = probs
            mixtures[name, zone] = mixture
    mixture = jnp.concatenate([mixtures[name, zone] for name in "cab" for zone in range(2)], 0)
    mix_out[...] = mixture.astype(BF16)
    attn = rounded(dot(mixture, proj_ref[...]) + vector(proj_bias_ref))
    fine = rounded(own + attn)
    fine_out[...] = fine.astype(BF16)
    quartet = dot(quartet_order(), fine)
    parts = [quartet[p * COARSE : (p + 1) * COARSE] for p in range(4)]
    hats, _ = quartet_norm(parts)
    coarse = None
    gain, shift = (vector(merge_gain_ref), vector(merge_shift_ref))
    for p in range(4):
        at = slice(p * C_F, (p + 1) * C_F)
        value = (hats[p] * gain[:, at] + shift[:, at]).astype(BF16)
        merged_out[p] = value
        part = dot(value, merge_ref[p * C_F : (p + 1) * C_F, :])
        coarse = part if coarse is None else coarse + part
    coarse = rounded(coarse)
    coarse_out[...] = coarse
    hat, _ = norm_parts(coarse)
    cnorm_out[...] = (hat * vector(coarse_gain_ref) + vector(coarse_shift_ref)).astype(BF16)


def quartet_norm(parts):
    width = 4.0 * C_F
    mean = sum(jnp.sum(part, -1, keepdims=True) for part in parts) / width
    centres = [part - mean for part in parts]
    spread = sum(jnp.sum(c * c, -1, keepdims=True) for c in centres) / width
    scale = lax.rsqrt(spread + EPS)
    return ([c * scale for c in centres], scale)


def coarse_body(
    group_ref,
    own_ref,
    coarse_ref,
    cot_ref,
    qkv_ref,
    qkv_bias_ref,
    proj_ref,
    proj_bias_ref,
    bias_ref,
    out_ref,
    parts_out,
    own_out,
    flat_out,
    table_out,
    cot_out,
    stage,
    keys,
    values,
):
    fetch_groups(stage, cot_ref)
    cot = dot(coarse_order(), stage[...])
    cot_out[...] = cot
    bias = vector(qkv_bias_ref)
    wide = [slice(i * C_C, (i + 1) * C_C) for i in range(3)]
    queries = rounded(dot(own_ref[...], qkv_ref[:, wide[0]]) + bias[:, wide[0]])
    group = jnp.concatenate([group_ref[g] for g in range(4)], 0)
    keys[...] = rounded(dot(group, qkv_ref[:, wide[1]]) + bias[:, wide[1]])
    values[...] = rounded(dot(group, qkv_ref[:, wide[2]]) + bias[:, wide[2]])
    mixture_grad = rounded(dot_nt(cot, proj_ref[...]))
    rows, mask, _, _, toep, _ = coarse_kind()
    mixtures, query_grads, grads = ([], [], [])
    for zone in range(2):
        here = slice(zone * 40, (zone + 1) * 40)
        at = [slice(g * COARSE + zone * 40, g * COARSE + zone * 40 + 40) for g in range(4)]
        k = jnp.concatenate([keys[there, :] for there in at], 0)
        v = jnp.concatenate([values[there, :] for there in at], 0)
        probs, mixture = attend(queries[here], k, v, rows, mask, bias_ref[zone])
        dq, dk, dv, table = attend_back(
            queries[here], k, v, rows, mask, probs, mixture_grad[here], toep, 144
        )
        table_out[zone * 144 : (zone + 1) * 144, :] = table
        mixtures.append(mixture)
        query_grads.append(dq)
        grads.append((dk, dv))
    key_grad, value_grad = (
        rounded(
            jnp.concatenate(
                [grads[zone][i][g * 40 : (g + 1) * 40] for g in range(4) for zone in range(2)], 0
            )
        )
        for i in range(2)
    )
    query_grad = jnp.concatenate(query_grads, 0)
    part = dot_nt(key_grad, qkv_ref[:, wide[1]]) + dot_nt(value_grad, qkv_ref[:, wide[2]])
    for g in range(4):
        parts_out[g] = part[g * COARSE : (g + 1) * COARSE].astype(BF16)
    own_out[...] = dot_nt(query_grad, qkv_ref[:, wide[0]])
    for i, (norm, grad) in enumerate(
        ((own_ref[...], query_grad), (group, key_grad), (group, value_grad))
    ):
        weight = dot_tn(norm, grad)
        sums = column_sum(grad)
        for c in range(3):
            lanes = slice(c * 128, (c + 1) * 128)
            flat_out[pl.ds(3 * i + c, C_C, stride=9), :] = weight[:, lanes]
            flat_out[3456 + 3 * i + c : 3457 + 3 * i + c, :] = sums[:, lanes]
    mixture = jnp.concatenate(mixtures, 0)
    flat_store(flat_out, 3465, dot_tn(mixture, cot))
    flat_store(flat_out, 4617, column_sum(cot))
    attn = rounded(dot(mixture, proj_ref[...]) + vector(proj_bias_ref))
    stage[...] = dot(coarse_order(True), coarse_ref[...] + attn)
    store_groups(out_ref, stage)


def flat_store(flat, start, matrix):
    height, width = matrix.shape
    step = width // 128
    for c in range(step):
        lanes = slice(c * 128, (c + 1) * 128)
        if height == 1:
            flat[start + c : start + c + 1, :] = matrix[:, lanes]
        else:
            flat[pl.ds(start + c, height, stride=step), :] = matrix[:, lanes]


def keep_square(square, matrix):
    height = matrix.shape[0]
    square[0, 0:height, :] = matrix[:, 0:128]
    square[1, 0:height, 0:64] = matrix[:, 128:192]


def every_other(square, start):
    take = pl.ds(start, 96, stride=2)
    return jnp.concatenate([square[0, take, :], square[1, take, :][:, 0:64]], 1)


def block_store(flat, start, blocks):
    for c, block in enumerate(blocks):
        if block.shape[0] == 1:
            flat[start + c : start + c + 1, :] = block
        else:
            flat[pl.ds(start + c, block.shape[0], stride=len(blocks)), :] = block


def fine_back_body(
    starts,
    rows,
    part_ref,
    own_part_ref,
    cot_ref,
    coarse_ref,
    merged_ref,
    fine_ref,
    hat_ref,
    normed_ref,
    mix_ref,
    q_ref,
    k_ref,
    v_ref,
    probs_a,
    probs_b,
    probs_c,
    qkv_ref,
    cgain_ref,
    merge_gain_ref,
    merge_ref,
    proj_ref,
    flat_c,
    table_q,
    fog_out,
    own_out,
    par_out,
    upo_out,
    upp_out,
    dno_out,
    dnp_out,
    pieces_out,
    tables_out,
    kgrad,
    vgrad,
    flat,
    tables,
    square,
):
    norm_grad = part_ref[...] + own_part_ref[...]
    hat, scale = norm_parts(coarse_ref[...])
    flat_store(flat, 3477, column_sum(norm_grad * hat))
    flat_store(flat, 3480, column_sum(norm_grad))
    coarse_grad = rounded(cot_ref[...] + norm_back(hat, scale, norm_grad, vector(cgain_ref)))
    quartet = dot(quartet_order(), fine_ref[...])
    hats, scale = quartet_norm([quartet[p * COARSE : (p + 1) * COARSE] for p in range(4)])
    inners, gains, shifts = ([], [], [])
    merge_gain = vector(merge_gain_ref)
    for p in range(4):
        at = slice(p * C_F, (p + 1) * C_F)
        flat_store(flat, 1173 + 3 * p * C_F, dot_tn(merged_ref[p], coarse_grad))
        grad = dot_nt(coarse_grad, merge_ref[at, :])
        gains.append(column_sum(grad * hats[p]))
        shifts.append(column_sum(grad))
        inners.append(grad * merge_gain[:, at])
    block_store(flat, 1161, lane_blocks(gains))
    block_store(flat, 1167, lane_blocks(shifts))
    width = 4.0 * C_F
    first = sum(jnp.sum(inner, -1, keepdims=True) for inner in inners) / width
    second = sum(jnp.sum(i * h, -1, keepdims=True) for i, h in zip(inners, hats)) / width
    grads = jnp.concatenate([scale * (i - first - h * second) for i, h in zip(inners, hats)], 0)
    high = rounded(grads)
    unmerge = quartet_order(True)
    attn_grad = dot(unmerge, high)
    fog_out[...] = attn_grad + dot(unmerge, grads - high)
    mixture_grad = rounded(dot_nt(attn_grad, proj_ref[...]))
    weight = dot_tn(mix_ref[...], attn_grad)
    corner = weight[0:1]
    keep_square(square, jnp.concatenate([weight, column_sum(attn_grad)], 0))
    block_store(flat, 873, lane_blocks([every_other(square, 1), every_other(square, 2)]))
    kinds = fine_kinds()
    places = {"a": (PART_A, probs_a), "b": (PART_B, probs_b), "c": (PART_C, probs_c)}
    query_grads = {}
    for zone in range(2):
        for name, (start, count), pieces in fine_windows(zone):
            rows_at, mask, _, _, toep, block = kinds[name]
            table_at, probs_ref = places[name]
            dq, dk, dv, table = attend_back(
                q_ref[start : start + count, :],
                gathered(k_ref, pieces),
                gathered(v_ref, pieces),
                rows_at,
                mask,
                probs_ref[zone],
                mixture_grad[start : start + count],
                toep,
                block,
            )
            query_grads[name, zone] = dq
            for c in range(3):
                at = table_at + (2 * c + zone) * block
                tables[at : at + block, :] = table[:, c * 128 : (c + 1) * 128]
            at = 0
            for source, begin, size in pieces:
                to = slice(SOURCES[source] + begin, SOURCES[source] + begin + size)
                kgrad[to, :] = rounded(dk[at : at + size])
                vgrad[to, :] = rounded(dv[at : at + size])
                at += size
    query_grad = jnp.concatenate([query_grads[name, zone] for name in "cab" for zone in range(2)], 0)
    part = dot_nt(kgrad[...], qkv_ref[:, C_F : 2 * C_F]) + dot_nt(vgrad[...], qkv_ref[:, 2 * C_F :])
    own = part[0:FINE] + dot_nt(query_grad, qkv_ref[:, 0:C_F])
    own_out[...] = own
    par_out[...] = part[FINE : 2 * FINE].astype(BF16)
    for place, out in enumerate((upo_out, upp_out, dno_out, dnp_out)):
        at = SOURCES[2 + place]
        out[...] = packed_side(part[at : at + SIDE]).astype(BF16)
    hat_grad = column_sum(own * hat_ref[0:FINE, :])
    hat_grad += column_sum(part[FINE:] * hat_ref[FINE:, :])
    block_store(
        flat, 0, lane_blocks([hat_grad, column_sum(own) + column_sum(part[FINE:])])
    )
    evens, odds, sums = ([], [], [])
    for norm, grad in (
        (normed_ref[0:FINE, :], query_grad),
        (normed_ref[...], kgrad[...]),
        (normed_ref[...], vgrad[...]),
    ):
        keep_square(square, dot_tn(norm, grad))
        evens.append(every_other(square, 0))
        odds.append(every_other(square, 1))
        sums.append(column_sum(grad))
    block_store(flat, 3, lane_blocks(evens + odds))
    block_store(flat, 867, lane_blocks(sums + [corner]))
    tables[240:PART_A, :] = jnp.zeros((PART_A - 240, 128), F32)
    tables[PART_END:, :] = jnp.zeros((TABLE_ROWS - PART_END, 128), F32)
    for c in range(3):
        at = PART_Q + 288 * c
        tables[at : at + 288, :] = table_q[:, c * 128 : (c + 1) * 128]
    split = 3483
    trows = TABLE_ROWS // len(starts)
    for place, start in starts:
        end = start + rows
        if start < split:
            size = min(end, split) - start
            value = flat[start : start + size, :]
            if end > split:
                value = jnp.concatenate([value, flat_c[0 : end - split, :]], 0)
        else:
            size = min(end, 8103) - start
            value = flat_c[start - split : start - split + size, :]
            if size < rows:
                value = jnp.concatenate([value, jnp.zeros((rows - size, 128), F32)], 0)
        chunk = pieces_out.shape[2]
        for y in range(pieces_out.shape[0]):
            pieces_out[y, place] = value[y * chunk : (y + 1) * chunk].astype(BF16)
        tables_out[place] = tables[place * trows : (place + 1) * trows, :].astype(BF16)


def final_body(
    x_ref,
    gain_ref,
    fog_ref,
    own_ref,
    par_ref,
    low_ref,
    high_ref,
    t_ref,
    token_out,
    fine_out,
    coarse_out,
    stage,
    grad,
):
    grad[...] = own_ref[...] + par_ref[...].astype(F32)
    grad[LOW : LOW + SIDE, :] += unpacked_side(low_ref[...].astype(F32))
    grad[TOP : TOP + SIDE, :] += unpacked_side(high_ref[...].astype(F32))
    hat, scale = norm_parts(x_ref[...].astype(F32))
    total = fog_ref[...] + norm_back(hat, scale, rounded(grad[...]), vector(gain_ref))
    stage[...] = dot(fine_order(True), total)
    store_groups(token_out, stage)

    def part(start, height):
        return jnp.concatenate(
            [t_ref[start + c * height : start + (c + 1) * height, :] for c in range(3)], 1
        )

    def natural(kind, block):
        total = None
        for zk in range(2):
            term = dot(table_rows(kind, zk, True), dot_nt(block, table_lanes(zk)))
            total = term if total is None else total + term
        return total

    fine_out[0:288, :] = natural("a", part(PART_A, 144))
    fine_out[288:576, :] = natural("b", part(PART_B, 80)) + natural("c", part(PART_C, 80))
    coarse_out[...] = natural("q", part(PART_Q, 288))


def mesh_parts(lat, lon):
    cores = 2
    xs = 4 if lon % 8 == 0 else 1
    ys = 4 if lat % 4 == 0 else lat
    return (cores, xs, lon // (cores * xs), ys, lat // ys)


def piece_rows(total, lon, ys):
    longest = -(-(127 + total // lon) // 128)
    unit = 16 * ys
    return -(-longest // unit) * unit


def reduce_body(
    dims,
    norm_factor,
    g_ref,
    gt_ref,
    par_ref,
    upo_ref,
    upp_ref,
    dno_ref,
    dnp_ref,
    p_ref,
    t_ref,
    par_out,
    low_out,
    high_out,
    par_buf,
    up_buf,
    down_buf,
    up_sum,
    down_sum,
    low_buf,
    high_buf,
    core_buf,
    head_buf,
    tail_buf,
    y_buf,
    y_sum,
    x_buf,
    x_sum,
    z_buf,
    h_send,
    h_buf,
    share,
    tab_core,
    tab_x,
    tab_sum,
    tab_own,
    tab_hand,
    tab_z,
    tab_all,
    send_sems,
    recv_sems,
):
    cores, xs, zs, ys, hs = dims
    half = xs * zs
    chunk = g_ref.shape[2]
    trows = gt_ref.shape[1]
    lat, lon = (lax.axis_index("lat"), lax.axis_index("lon"))
    core = lax.rem(lon, cores)
    x = lax.rem(lon // cores, xs)
    z = lon // (cores * xs)
    y = lax.rem(lat, ys)
    h = lat // ys
    lats = ys * hs

    def at(here, d, count):
        return lax.rem(here + d, count)

    def lon_of(core_to, x_to, z_to):
        return (z_to * xs + x_to) * cores + core_to

    other_core = (lat, lon_of(1 - core, x, z))
    x_peers = {d: (lat, lon_of(core, at(x, d, xs), z)) for d in range(1, xs)}
    y_peers = {d: (h * ys + at(y, d, ys), lon) for d in range(1, ys)}
    z_peers = {d: (lat, lon_of(core, x, at(z, d, zs))) for d in range(1, zs)}
    far = (at(h, 1, hs) * ys + y, lon)
    before, after = ((at(lat, lats - 1, lats), lon), (at(lat, 1, lats), lon))
    beside = (lat, partner_of(lon, cores * half))
    peers = [before, after] + ([far] if hs > 1 else [])
    peers += list(z_peers.values())[::-1] + list(y_peers.values()) + list(x_peers.values())
    peers += [beside, other_core]
    meet(peers)
    pending = []

    def send(src, dst, peer):
        sem = len(pending)
        copy = start_copy(src, dst, send_sems.at[sem], recv_sems.at[sem], peer)
        pending.append(copy)
        return copy

    def arrived(copies):
        for copy in copies:
            copy.wait_recv()

    def add_into(target, terms, count):
        def step(i, carry):
            total = terms[0](i).astype(F32)
            for term in terms[1:]:
                total = total + term(i).astype(F32)
            target[i] = total.astype(BF16)
            return carry

        lax.fori_loop(0, count, step, 0)

    away = pl.ds((1 - core) * half, half)
    mine = core * half
    table_core = send(gt_ref.at[away], tab_core, other_core)
    edges = [
        send(upp_ref, up_buf, beside),
        send(dnp_ref, down_buf, beside),
        send(par_ref, par_buf, beside),
    ]
    order = {4: (2, 1, 3, 0), 2: (1, 0), 1: (0,)}[ys]
    crossing = {d: send(g_ref.at[at(y, d, ys), away], core_buf.at[d], other_core) for d in order}
    table_core.wait_recv()
    add_into(tab_core, [lambda i: tab_core[i], lambda i: gt_ref[mine + i]], half)
    table_x = [
        send(tab_core.at[pl.ds(at(x, d, xs) * zs, zs)], tab_x.at[d - 1], x_peers[d])
        for d in range(1, xs)
    ]
    cut = half // 2
    head, tail = (pl.ds(0, cut), pl.ds(cut, half - cut))
    gathered_y = []
    for d in order:
        crossing[d].wait_recv()
        row = at(y, d, ys)
        buf = core_buf.at[d]
        add_into(buf, [lambda i: buf[i], lambda i: g_ref[row, mine + i]], half)
        if ys == 4 and d == 2:
            over_right = send(core_buf.at[2, head], head_buf, y_peers[1])
            over_left = send(core_buf.at[2, tail], tail_buf, y_peers[3])
        if ys == 4 and d == 1:
            gathered_y.append(send(core_buf.at[1, tail], y_buf.at[0, tail], y_peers[1]))
        if ys == 4 and d == 3:
            gathered_y.append(send(core_buf.at[3, head], y_buf.at[1, head], y_peers[3]))
        if ys == 2 and d == 1:
            gathered_y.append(send(core_buf.at[1], y_buf.at[0], y_peers[1]))
    if ys == 4:
        over_right.wait_recv()
        right = core_buf.at[1]
        add_into(right, [lambda i: right[i], lambda i: head_buf[i]], cut)
        gathered_y.append(send(core_buf.at[1, head], y_buf.at[0, head], y_peers[1]))
        over_left.wait_recv()
        left = core_buf.at[3, tail]
        add_into(left, [lambda i: left[i], lambda i: tail_buf[i]], half - cut)
        gathered_y.append(send(core_buf.at[3, tail], y_buf.at[1, tail], y_peers[3]))

    arrived(edges[:2])
    up_sum[...] = (upo_ref[...].astype(F32) + up_buf[...].astype(F32)).astype(BF16)
    down_sum[...] = (dno_ref[...].astype(F32) + down_buf[...].astype(F32)).astype(BF16)
    edges.append(send(up_sum, low_buf, after))
    edges.append(send(down_sum, high_buf, before))
    arrived(table_x)
    base = x * zs
    terms = [lambda i: tab_core[base + i]]
    terms += [lambda i, d=d: tab_x[d - 1, i] for d in range(1, xs)]
    add_into(tab_sum, terms, zs)
    table_z = [
        send(tab_sum.at[at(z, d, zs)], tab_z.at[d - 1], z_peers[d]) for d in range(1, zs)
    ]

    arrived(gathered_y)
    terms = [lambda i: core_buf[0, i]]
    terms += [lambda i, d=d: y_buf[d, i] for d in range({4: 2, 2: 1, 1: 0}[ys])]
    add_into(y_sum, terms, half)
    along_x = [
        send(y_sum.at[pl.ds(at(x, d, xs) * zs, zs)], x_buf.at[d - 1], x_peers[d])
        for d in range(1, xs)
    ]

    arrived(table_z)
    total = tab_sum[z].astype(F32)
    for d in range(1, zs):
        total = total + tab_z[d - 1].astype(F32)
    own = tab_all.at[core, x, z]
    tab_own[...] = (total * norm_factor).astype(BF16)
    tab_all[core, x, z] = tab_own[...]
    first_row = ((core * xs + x) * zs + z) * trows

    def prepared(src, dst, peer):
        sem = len(pending)
        copy = pltpu.make_async_remote_copy(
            src_ref=src,
            dst_ref=dst,
            send_sem=send_sems.at[sem],
            recv_sem=recv_sems.at[sem],
            device_id=peer,
            device_id_type=MESH,
        )
        pending.append(copy)
        return copy

    handed = prepared(tab_own, tab_hand, before)
    pending.pop()
    pending.append(None)
    back_z = [prepared(own, own, z_peers[d]) for d in range(1, zs)]

    @pl.when(first_row < PART_A)
    def _():
        handed.start()

    @pl.when(first_row >= PART_A)
    def _():
        for copy in back_z:
            copy.start()

    arrived(along_x)
    terms = [lambda i: y_sum[base + i]]
    terms += [lambda i, d=d: x_buf[d - 1, i] for d in range(1, xs)]
    add_into(x_sum, terms, zs)
    along_z = [send(x_sum.at[at(z, d, zs)], z_buf.at[d - 1], z_peers[d]) for d in range(1, zs)]

    @pl.when(first_row < PART_A)
    def _():
        handed.wait()
        row = first_row + lax.broadcasted_iota(jnp.int32, (trows, 128), 0)
        tab_all[core, x, z] = jnp.where(
            row < PART_A, tab_hand[...].astype(F32), tab_own[...].astype(F32)
        ).astype(BF16)
        for copy in back_z:
            copy.start()

    arrived(along_z)
    total = x_sum[z].astype(F32)
    for d in range(1, zs):
        total = total + z_buf[d - 1].astype(F32)
    if hs > 1:
        h_send[...] = total.astype(BF16)
        across = send(h_send, h_buf, far)
    arrived(back_z)
    own = tab_all.at[core, x]
    back_x = [send(own, own, x_peers[d]) for d in range(1, xs)]
    if hs > 1:
        across.wait_recv()
        total = h_send[...].astype(F32) + h_buf[...].astype(F32)
    rows = pl.ds(pl.multiple_of(y * chunk, 8), chunk)
    share[rows, :] = total * norm_factor
    back_y = [send(share.at[rows], share.at[rows], y_peers[d]) for d in range(1, ys)]
    arrived(back_x)
    own = tab_all.at[core]
    back_core = send(own, own, other_core)
    arrived(edges[2:])
    par_out[...] = par_buf[...]
    low_out[...] = low_buf[...]
    high_out[...] = high_buf[...]
    arrived(back_y)
    p_ref[...] = share[...]
    back_core.wait_recv()
    t_ref[...] = tab_all[...]
    for copy in pending:
        if copy is not None:
            copy.wait_send()


def reduce_all(pieces, tables, edges, norm_factor, dims):
    cores, xs, zs, ys, hs = dims
    half = xs * zs
    chunk = pieces.shape[2]
    trows = tables.shape[1]
    sem = pltpu.SemaphoreType.DMA((64,))
    vmem = pl.BlockSpec(memory_space=pltpu.VMEM)
    side = (128, 128)
    all_tables = (cores, xs, zs, trows, 128)
    outs = [((ys * chunk, 128), F32), (all_tables, BF16), ((FINE, C_F), BF16)]
    outs += [(side, BF16), (side, BF16)]
    buffers = [
        (FINE, C_F),
        *[side] * 6,
        (ys, half, chunk, 128),
        (half // 2, chunk, 128),
        (half - half // 2, chunk, 128),
        (2, half, chunk, 128),
        (half, chunk, 128),
        (max(xs - 1, 1), zs, chunk, 128),
        (zs, chunk, 128),
        (max(zs - 1, 1), chunk, 128),
        (chunk, 128),
        (chunk, 128),
        None,
        (half, trows, 128),
        (max(xs - 1, 1), zs, trows, 128),
        (zs, trows, 128),
        (trows, 128),
        (trows, 128),
        (max(zs - 1, 1), trows, 128),
        all_tables,
    ]
    scratch = [
        pltpu.VMEM((ys * chunk, 128), F32) if shape is None else pltpu.VMEM(shape, BF16)
        for shape in buffers
    ]
    return pl.pallas_call(
        functools.partial(reduce_body, dims, norm_factor),
        out_shape=tuple(jax.ShapeDtypeStruct(shape, dtype) for shape, dtype in outs),
        in_specs=[vmem] * 7,
        out_specs=(vmem,) * 5,
        scratch_shapes=scratch + [sem, sem],
        compiler_params=pltpu.CompilerParams(
            collective_id=7, has_side_effects=True, vmem_limit_bytes=VMEM_BYTES
        ),
        cost_estimate=lasting(35),
        name="grad_reduce",
    )(pieces, tables, *edges)


def shards(
    tokens,
    fine_gain,
    fine_shift,
    fine_qkv,
    fine_qkv_bias,
    fine_proj,
    fine_proj_bias,
    fine_table,
    merge_gain,
    merge_shift,
    merge_weight,
    coarse_gain,
    coarse_shift,
    coarse_qkv,
    coarse_qkv_bias,
    coarse_proj,
    coarse_proj_bias,
    coarse_table,
    cotangent,
):
    lat_count, lon_count = (lax.axis_size("lat"), lax.axis_size("lon"))
    lat, lon = (lax.axis_index("lat"), lax.axis_index("lon"))
    norm_factor = 1.0 / math.sqrt(tokens.size // C_F * lat_count * lon_count / 4)
    fine_rows = fine_table.reshape(576, 138)
    coarse_rows = coarse_table.reshape(576, 138)
    cells = tokens[0].transpose(1, 2, 0, 3)
    cot_cells = cotangent[0].transpose(1, 2, 0, 3)

    group = min(8, lon_count)
    side = ((128, 128), BF16)
    own = ((FINE, C_F), BF16)
    table_part = ((group, PART_A // group, 128), BF16)
    x, low, high, table_send = call(
        prepare_body,
        [own, side, side, table_part],
        (cells, fine_rows),
        [pltpu.VMEM((288, C_F), F32)],
        "prepare",
        2,
    )
    halo = [own, side, side, side, side, table_part]
    bias_a, bias_b = (((2, 432, 144), F32), ((2, 240, 160), F32))
    par, upo, upp, dno, dnp, bias_a, bias_b, bias_c, bias_q = exchange_call(
        halo_body,
        halo[:5] + [bias_a, bias_b, bias_b, ((2, 432, 160), F32)],
        (x, low, high, table_send, fine_rows, coarse_rows),
        [pltpu.VMEM(*s) for s in halo],
        (6, max(group - 1, 1)),
        1,
        "halo",
        12,
    )
    (
        hat,
        normed,
        q,
        k,
        v,
        probs_a,
        probs_b,
        probs_c,
        mixture,
        fine_out,
        merged,
        coarse,
        cnorm,
    ) = call(
        fine_forward_body,
        [
            ((ALL_ROWS, C_F), F32),
            ((ALL_ROWS, C_F), BF16),
            ((FINE, C_F), F32),
            ((ALL_ROWS, C_F), F32),
            ((ALL_ROWS, C_F), F32),
            ((2, 432, 144), F32),
            ((2, 240, 160), F32),
            ((2, 240, 160), F32),
            own,
            own,
            ((4, COARSE, C_F), BF16),
            ((COARSE, C_C), F32),
            ((COARSE, C_C), BF16),
        ],
        (
            x,
            par,
            upo,
            upp,
            dno,
            dnp,
            fine_gain,
            fine_shift,
            fine_qkv,
            fine_qkv_bias,
            fine_proj,
            fine_proj_bias,
            merge_gain,
            merge_shift,
            merge_weight,
            coarse_gain,
            coarse_shift,
            bias_a,
            bias_b,
            bias_c,
        ),
        (),
        "fine_forward",
        10,
    )
    gathered_to = [((4, COARSE, C_C), BF16)]
    (gathered_norm,) = exchange_call(
        group_body, gathered_to, (cnorm,), [pltpu.VMEM(*gathered_to[0])], (3,), 2, "coarse_gather", 5
    )
    coarse_out, parts, own_part, flat_c, table_q, cot = call(
        coarse_body,
        [
            ((6, 3, 4, C_C), BF16),
            ((4, COARSE, C_C), BF16),
            ((COARSE, C_C), F32),
            ((4620, 128), F32),
            ((288, 384), F32),
            ((COARSE, C_C), F32),
        ],
        (
            gathered_norm,
            cnorm,
            coarse,
            cot_cells,
            coarse_qkv,
            coarse_qkv_bias,
            coarse_proj,
            coarse_proj_bias,
            bias_q,
        ),
        [
            pltpu.VMEM((72, C_C), F32),
            pltpu.VMEM((4 * COARSE, C_C), F32),
            pltpu.VMEM((4 * COARSE, C_C), F32),
        ],
        "coarse_attention",
        7,
    )
    (norm_part,) = exchange_call(
        ungroup_body,
        [((COARSE, C_C), F32)],
        (parts,),
        [pltpu.VMEM((3, COARSE, C_C), BF16)],
        (3,),
        3,
        "coarse_scatter",
        5,
    )
    dims = mesh_parts(lat_count, lon_count)
    cores, xs, zs, ys, hs = dims
    segment = PARAMS // lon_count
    rows = piece_rows(PARAMS, lon_count, ys)
    starts = []
    for index in range(lon_count):
        core, x_at, z_at = (index % cores, index // cores % xs, index // (cores * xs))
        starts.append(((core * xs + x_at) * zs + z_at, index * segment // 128))
    trows = TABLE_ROWS // lon_count
    fine_out_grad, own_grad, *edges, pieces, table_pieces = call(
        functools.partial(fine_back_body, starts, rows),
        [
            ((FINE, C_F), F32),
            ((FINE, C_F), F32),
            own,
            side,
            side,
            side,
            side,
            ((ys, lon_count, rows // ys, 128), BF16),
            ((lon_count, trows, 128), BF16),
        ],
        (
            norm_part,
            own_part,
            cot,
            coarse,
            merged,
            fine_out,
            hat,
            normed,
            mixture,
            q,
            k,
            v,
            probs_a,
            probs_b,
            probs_c,
            fine_qkv,
            coarse_gain,
            merge_gain,
            merge_weight,
            fine_proj,
            flat_c,
            table_q,
        ),
        [
            pltpu.VMEM((ALL_ROWS, C_F), F32),
            pltpu.VMEM((ALL_ROWS, C_F), F32),
            pltpu.VMEM((3488, 128), F32),
            pltpu.VMEM((TABLE_ROWS, 128), F32),
            pltpu.VMEM((2, 200, 128), F32),
        ],
        "fine_backward",
        9,
    )
    owned, table_sum, par_back, low_back, high_back = reduce_all(
        pieces, table_pieces, edges, norm_factor, dims
    )
    shift = lax.rem(lon * segment, 128)
    param_grads = lax.dynamic_slice(owned.reshape(-1), (shift,), (segment,))
    token_grad, fine_total, coarse_total = call(
        final_body,
        [((12, 6, 4, C_F), BF16), ((576, 138), F32), ((576, 138), F32)],
        (
            x,
            fine_gain,
            fine_out_grad,
            own_grad,
            par_back,
            low_back,
            high_back,
            table_sum.reshape(TABLE_ROWS, 128),
        ),
        [pltpu.VMEM((288, C_F), F32), pltpu.VMEM((FINE, C_F), F32)],
        "final",
        2,
    )
    return (
        coarse_out.transpose(2, 0, 1, 3)[None],
        token_grad.transpose(2, 0, 1, 3)[None],
        param_grads,
        fine_total.reshape(2, -1),
        coarse_total.reshape(2, -1),
    )


def solution(mesh):
    tiles = P(None, None, "lat", "lon", None)
    whole = P()
    rows = P("lat", None)
    return jax.shard_map(
        shards,
        mesh=mesh,
        in_specs=(tiles,) + (whole,) * 6 + (rows,) + (whole,) * 9 + (rows, tiles),
        out_specs=(tiles, tiles, P("lon"), rows, rows),
        check_vma=False,
    )
```

```python
import functools
import math

import jax
import jax.numpy as jnp
from jax import lax
from jax.experimental import pallas as pl
from jax.experimental.pallas import tpu as pltpu
from jax.sharding import PartitionSpec as P

HEAD = 32
HEADS_F = 6
HEADS_C = 12
C_F = 192
C_C = 384
SPAN = 23
EPS = 1e-05
NEGATIVE = -1e30
MESH = pl.DeviceIdType.MESH
F32 = jnp.float32
BF16 = jnp.bfloat16
MIB = 1024 * 1024
VMEM_BYTES = 28 * MIB

LOW, MID, TOP = (0, 80, 224)
PARAMS = 1037184
TABLE_ROWS = 2048
FINE = 304
SIDE = 80
COARSE = 80
PART_C, PART_A, PART_B, PART_Q, PART_END = (0, 256, 688, 928, 1792)


def whole(x, n):
    return jnp.floor((x + 0.5) * (1.0 / n))


def rest(x, n):
    return x - n * whole(x, n)


def down_rows(n):
    return lax.broadcasted_iota(jnp.int32, (n, 1), 0).astype(F32)


def along_lanes(n):
    return lax.broadcasted_iota(jnp.int32, (1, n), 1).astype(F32)


def index_and_other(n, m, flip):
    return (along_lanes(n), down_rows(m)) if flip else (down_rows(n), along_lanes(m))


def match(a, b):
    return jnp.where(a == b, 1.0, 0.0).astype(BF16)


def fine_row(zone, zq, row, col):
    low = LOW + zone * 40 + (zq * 3 + row) * 6 + col
    mid = MID + zone * 72 + (zq * 6 + row - 3) * 6 + col
    top = TOP + zone * 40 + (zq * 3 + row - 9) * 6 + col
    return jnp.where(row < 3, low, jnp.where(row < 9, mid, top))


def fine_order(flip=False):
    at, cells = index_and_other(FINE, 288, flip)
    low, top = (at < MID, at >= TOP)
    edge = jnp.where(top, at - TOP, at)
    mid = at - MID
    in_edge = low | top
    part = rest(edge, 40)
    zone = jnp.where(in_edge, whole(edge, 40), whole(mid, 72))
    zq = jnp.where(in_edge, whole(part, 18), whole(rest(mid, 72), 36))
    row = jnp.where(
        in_edge,
        whole(rest(part, 18), 6) + jnp.where(top, 9.0, 0.0),
        3 + whole(rest(mid, 36), 6),
    )
    col = jnp.where(in_edge, rest(part, 6), rest(mid, 6))
    code = (row * 6 + col) * 4 + rest(2 * zone + zq + 1, 4)
    return match(jnp.where(in_edge & (part >= 36), -1.0, code), cells)


def coarse_place(at):
    part = rest(at, 40)
    return (whole(at, 40), whole(part, 18), whole(rest(part, 18), 3), rest(part, 3), part < 36)


def coarse_order(flip=False):
    at, cells = index_and_other(COARSE, 72, flip)
    zone, zq, row, col, valid = coarse_place(at)
    code = (row * 3 + col) * 4 + 2 * zone + zq
    return match(jnp.where(valid, code, -1.0), cells)


def quartet_order(flip=False):
    at, tokens = index_and_other(4 * COARSE, FINE, flip)
    p = whole(at, COARSE)
    zone, zq, row, col, valid = coarse_place(rest(at, COARSE))
    rolled = rest(2 * zone + zq + 3, 4)
    source = fine_row(
        whole(rolled, 2), rest(rolled, 2), 2 * row + rest(p, 2), 2 * col + whole(p, 2)
    )
    return match(jnp.where(valid, source, -1.0), tokens)


def head_rows(heads, lats, cols, tokens, block):
    def parts(at):
        part = rest(at, block)
        zq = whole(rest(part, 2 * lats), lats)
        code = (zq * lats + rest(part, lats)) * cols + whole(at, block)
        valid = part < heads * 2 * lats
        return (jnp.where(valid, whole(part, 2 * lats), -1.0), zq, jnp.where(valid, code, -1.0))

    rows = block * cols
    h, zq, code = parts(down_rows(rows))
    mask = match(h, whole(along_lanes(heads * HEAD), HEAD)).astype(F32)
    back = match(parts(along_lanes(rows))[2], down_rows(tokens))
    return ((match(code, along_lanes(tokens)), back), mask, zq)


def pair_keys(size, half):
    u = along_lanes(size)
    if size == 144:
        source, part = (whole(u, 72), rest(u, 72))
        zk, ak, valid = (whole(part, 36), whole(rest(part, 36), 6), part >= 0)
    else:
        slot, part = (whole(u, 40), rest(u, 40))
        source = rest(slot, 2)
        zk = whole(part, 18)
        ak = 3 * whole(slot, 2) + whole(rest(part, 18), 6)
        valid = part < 36
    return (zk, ak, rest(part, 6) + 6 * jnp.abs(half - source), valid)


def group_keys():
    u = along_lanes(160)
    part = rest(u, 40)
    zk, ak = (whole(part, 18), whole(rest(part, 18), 3))
    return (zk, ak, rest(part, 3) + 3 * whole(u, 40), part < 36)


def toeplitz(keys, cols, shift):
    zk, ak, col, valid = keys
    at = down_rows(384)
    tail = at >= 256
    level = jnp.where(tail, whole(at - 256, 64), whole(at, 128))
    entry = jnp.where(tail, 128 + rest(at, 64), rest(at, 128))
    code = (level * 6 + whole(entry, SPAN)) * 64 + rest(entry, SPAN)
    code = jnp.where(entry < 138, code, -1.0)
    key_code = jnp.where(valid, (zk * 6 + ak) * 64 - col + shift + 11, -100.0)
    return [match(code, key_code + oq) for oq in range(cols)]


def table_lanes(zk):
    entry = down_rows(138)
    return match(
        jnp.where(entry < 128, zk * 128 + entry, 256 + zk * 64 + entry - 128), along_lanes(384)
    )


def table_rows(kind, zk, flip=False):
    if kind == "q":
        at, source = index_and_other(288, 576, flip)
        part = rest(at, 144)
        aq = rest(part, 6)
        lead = (whole(aq, 3) * 2 + whole(at, 144)) * HEADS_C + whole(part, 12)
        zq = whole(rest(part, 12), 6)
        return match(((lead * 2 + zq) * 2 + zk) * 3 + rest(aq, 3), source)
    if kind == "a":
        count, block, lats, first = (144, 72, 6, 0)
    else:
        count, block, lats, first = (80, 40, 3, 3 if kind == "c" else 0)
    at, source = index_and_other(count, 288, flip)
    part = rest(at, block)
    lead = whole(at, block) * HEADS_F + whole(part, 2 * lats)
    zq = whole(rest(part, 2 * lats), lats)
    code = ((lead * 2 + zq) * 2 + zk) * 6 + rest(part, lats) + first
    return match(jnp.where(part < 12 * lats, code, -1.0), source)


def dot(a, b):
    return jnp.dot(a.astype(BF16), b.astype(BF16), preferred_element_type=F32)


def dot_nt(a, b):
    return lax.dot_general(
        a.astype(BF16), b.astype(BF16), (((1,), (1,)), ((), ())), preferred_element_type=F32
    )


def dot_tn(a, b):
    return lax.dot_general(
        a.astype(BF16), b.astype(BF16), (((0,), (0,)), ((), ())), preferred_element_type=F32
    )


def rounded(value):
    return value.astype(BF16).astype(F32)


def norm_parts(volume):
    centre = volume - jnp.mean(volume, -1, keepdims=True)
    spread = jnp.mean(centre * centre, -1, keepdims=True)
    scale = lax.rsqrt(spread + EPS)
    return (centre * scale, scale)


def norm_back(hat, scale, grad, gain):
    inner = grad * gain
    return scale * (
        inner
        - jnp.mean(inner, -1, keepdims=True)
        - hat * jnp.mean(inner * hat, -1, keepdims=True)
    )


def column_sum(value):
    return jnp.sum(value, 0, keepdims=True)


def attend(queries, keys, values, rows, mask, bias):
    spread_out, back = rows
    packed = dot(spread_out, queries) * mask
    scores = dot_nt(packed, keys) * HEAD ** (-0.5) + bias
    weights = jnp.exp(scores - jnp.max(scores, -1, keepdims=True))
    probs = weights / jnp.sum(weights, -1, keepdims=True)
    mixture = dot(probs, values) * mask
    return (probs, dot(back, mixture))


def attend_back(queries, keys, values, rows, mask, probs, mixture_grad, toep, block):
    factor = HEAD ** (-0.5)
    spread_out, back = rows
    packed = dot(spread_out, queries) * mask
    grad = dot(spread_out, mixture_grad) * mask
    value_grad = dot_tn(probs, grad)
    prob_grad = dot_nt(grad, values)
    score_grad = probs * (prob_grad - jnp.sum(prob_grad * probs, -1, keepdims=True))
    query_grad = dot(back, dot(score_grad, keys) * factor * mask)
    key_grad = dot_tn(score_grad, packed) * factor
    table = None
    for oq, select in enumerate(toep):
        part = dot_nt(score_grad[oq * block : (oq + 1) * block], select)
        table = part if table is None else table + part
    return (query_grad, key_grad, value_grad, table)


def lasting(micros):
    return pl.CostEstimate(flops=int(micros * 2.0e9), bytes_accessed=int(micros * 3.69e6), transcendentals=int(micros * 1e6))


def call(body, outs, args, scratch, name, micros, in_place=(), limit=VMEM_BYTES):
    vmem = pl.BlockSpec(memory_space=pltpu.VMEM)
    away = pl.BlockSpec(memory_space=pltpu.HBM)
    return pl.pallas_call(
        body,
        out_shape=tuple(jax.ShapeDtypeStruct(shape, dtype) for shape, dtype in outs),
        in_specs=[away if at in in_place else vmem for at in range(len(args))],
        out_specs=(vmem,) * len(outs),
        scratch_shapes=list(scratch),
        compiler_params=pltpu.CompilerParams(vmem_limit_bytes=limit),
        cost_estimate=lasting(micros),
        name=name,
    )(*args)


def vector(ref):
    return ref[...].reshape(1, -1)


def query_half():
    return 1 - lax.rem(lax.axis_index("lon"), 2)


def packed_side(value):
    tail = jnp.concatenate([value[0:40, 128:192], value[40:80, 128:192]], 1)
    return jnp.concatenate([value[:, 0:128], tail, jnp.zeros((8, 128), value.dtype)], 0)


def unpacked_side(block):
    tail = jnp.concatenate([block[80:120, 0:64], block[80:120, 64:128]], 0)
    return jnp.concatenate([block[0:80, :], tail], 1)


def lane_blocks(pieces):
    blocks = []
    for a, b in zip(pieces[::2], pieces[1::2]):
        blocks += [a[:, 0:128], jnp.concatenate([a[:, 128:192], b[:, 0:64]], 1), b[:, 64:192]]
    return blocks


def partner_of(lon, count):
    odd = lax.rem(lon, 2)
    return lax.rem(lon + 2 * odd - 1 + count, count)


def ring_positions():
    lat_count, lon_count = (lax.axis_size("lat"), lax.axis_size("lon"))
    lat, lon = (lax.axis_index("lat"), lax.axis_index("lon"))
    up = lax.rem(lat + 1, lat_count)
    down = lax.rem(lat + lat_count - 1, lat_count)
    return (lat, lon, up, down, partner_of(lon, lon_count))


def greet(peers):
    barrier = pltpu.get_barrier_semaphore()
    for peer in peers:
        pl.semaphore_signal(barrier, inc=1, device_id=peer, device_id_type=MESH)


def await_greetings(peers):
    pl.semaphore_wait(pltpu.get_barrier_semaphore(), len(peers))


def meet(peers):
    greet(peers)
    await_greetings(peers)


def start_copy(src, dst, send_sem, recv_sem, peer):
    copy = pltpu.make_async_remote_copy(
        src_ref=src,
        dst_ref=dst,
        send_sem=send_sem,
        recv_sem=recv_sem,
        device_id=peer,
        device_id_type=MESH,
    )
    copy.start()
    return copy


def exchange(sends, send_sems, recv_sems):
    copies = []
    for at, (src, dst, peer) in enumerate(sends):
        copies.append(start_copy(src, dst, send_sems.at[at], recv_sems.at[at], peer))
    for copy in copies:
        copy.wait_recv()
    for copy in copies:
        copy.wait_send()


def remote_call(body, outs, args, scratch, collective_id, name, micros):
    vmem = pl.BlockSpec(memory_space=pltpu.VMEM)
    return pl.pallas_call(
        body,
        out_shape=tuple(jax.ShapeDtypeStruct(shape, dtype) for shape, dtype in outs),
        in_specs=[vmem] * len(args),
        out_specs=(vmem,) * len(outs),
        scratch_shapes=scratch,
        compiler_params=pltpu.CompilerParams(
            collective_id=collective_id, has_side_effects=True, vmem_limit_bytes=VMEM_BYTES
        ),
        cost_estimate=lasting(micros),
        name=name,
    )(*args)


def semaphores(*counts):
    return [pltpu.SemaphoreType.DMA((count,)) for count in counts for _ in range(2)]


def halo_body(x_ref, low_ref, high_ref, tab_ref, tf_ref, tc_ref, *refs):
    outs, biases, bufs, (ss, rs, ts, tr) = (refs[:5], refs[5:9], refs[9:15], refs[15:])
    par, upo, upp, dno, dnp, tab = bufs
    lat, lon, up, down, partner = ring_positions()
    size = tab.shape[0]
    rank = lax.rem(lon, size)
    others = [lax.rem(rank + d, size) for d in range(1, size)]
    near = [(lat, lon - rank + other) for other in others]
    beside = (lat, partner)
    meet([(up, lon), (down, lon), beside] + near)
    low_copy = start_copy(low_ref, upo, ss.at[1], rs.at[1], (down, lon))
    high_copy = start_copy(high_ref, dno, ss.at[2], rs.at[2], (up, lon))
    table_copy = start_copy(tab_ref.at[rank], tab.at[rank], ss.at[3], rs.at[3], (up, lon))
    x_copy = start_copy(x_ref, par, ss.at[0], rs.at[0], beside)
    copies = [x_copy, low_copy, high_copy, table_copy]
    kinds = fine_kinds()
    store_bias("a", spread("a", tf_ref[0:288, :]), kinds["a"], biases[0])
    store_bias("b", spread("b", tf_ref[288:576, :]), kinds["b"], biases[1])
    store_bias("q", spread("q", tc_ref[...]), coarse_kind(), biases[3])
    low_copy.wait_recv()
    relays = [start_copy(upo, upp, ss.at[4], rs.at[4], beside)]
    high_copy.wait_recv()
    relays.append(start_copy(dno, dnp, ss.at[5], rs.at[5], beside))
    table_copy.wait_recv()
    for d, peer in enumerate(near):
        relays.append(start_copy(tab.at[rank], tab.at[rank], ts.at[d], tr.at[d], peer))
    x_copy.wait_recv()
    for copy in relays:
        copy.wait_recv()
    table = jnp.concatenate([tab[place].astype(F32) for place in range(size)], 0)
    table = jnp.concatenate([table[c * 80 : (c + 1) * 80] for c in range(3)], 1)
    store_bias("c", table, kinds["c"], biases[2])
    for copy in copies + relays:
        copy.wait_send()
    for out, buf in zip(outs, bufs):
        out[...] = buf[...]


def group_peers():
    lat, lon = (lax.axis_index("lat"), lax.axis_index("lon"))
    place = lax.rem(lon, 4)
    others = [lax.rem(place + d, 4) for d in range(1, 4)]
    return (place, others, [(lat, lon - place + other) for other in others])


def forward_gather_body(*refs):
    inner, (out_ref, buf, ss, rs) = (refs[:-4], refs[-4:])
    place, _, peers = group_peers()
    greet(peers)
    fine_forward_body(*inner)
    buf[place] = inner[-1][...]
    await_greetings(peers)
    exchange([(buf.at[place], buf.at[place], peer) for peer in peers], ss, rs)
    out_ref[...] = buf[...]


def coarse_scatter_body(*refs):
    inputs, (out_ref, norm_out, own_out, flat_out, table_out, cot_out) = (refs[:9], refs[9:15])
    stage, keys, values, parts, buf, ss, rs = refs[15:]
    place, others, peers = group_peers()
    greet(peers)
    coarse_body(
        *inputs, out_ref, parts, own_out, flat_out, table_out, cot_out, stage, keys, values
    )
    await_greetings(peers)
    exchange([(parts.at[other], buf.at[d], peers[d]) for d, other in enumerate(others)], ss, rs)
    total = parts[place].astype(F32)
    for d in range(3):
        total = total + buf[d].astype(F32)
    norm_out[...] = total


def spread(kind, table):
    total = None
    for zk in range(2):
        part = dot(dot(table_rows(kind, zk), table), table_lanes(zk))
        total = part if total is None else total + part
    return total


def bias_rows(table, toep, zone, block):
    rows = table[zone * block : (zone + 1) * block]
    return jnp.concatenate([dot(rows, select) for select in toep], 0)


def banned(keys, zq, zone):
    ban = jnp.where(keys[3], 0.0, NEGATIVE)
    if zone == 1:
        ban = ban + jnp.where(zq == keys[0], 0.0, NEGATIVE)
    return ban


def fetch_groups(stage, ref):
    rows, cols = ref.shape[:2]
    for row in range(rows):
        for col in range(cols):
            at = (row * cols + col) * 4
            stage[at : at + 4, :] = ref[row, col].astype(F32)


def store_groups(ref, stage):
    rows, cols = ref.shape[:2]
    for row in range(rows):
        for col in range(cols):
            at = (row * cols + col) * 4
            ref[row, col] = stage[at : at + 4, :].astype(BF16)


def prepare_body(x_ref, tf_ref, own_out, low_out, high_out, tab_out, stage):
    fetch_groups(stage, x_ref)
    tokens = dot(fine_order(), stage[...])
    own_out[...] = tokens.astype(BF16)
    low_out[...] = packed_side(tokens[LOW : LOW + SIDE]).astype(BF16)
    high_out[...] = packed_side(tokens[TOP : TOP + SIDE]).astype(BF16)
    table = spread("c", tf_ref[288:576, :])
    pieces = [table[:, c * 128 : (c + 1) * 128] for c in range(3)]
    block = jnp.concatenate(pieces + [jnp.zeros((16, 128), F32)], 0).astype(BF16)
    size = tab_out.shape[1]
    for place in range(tab_out.shape[0]):
        tab_out[place] = block[place * size : (place + 1) * size, :]


def fine_kinds():
    half = query_half().astype(F32)
    rows_a, mask_a, zq_a = head_rows(HEADS_F, 6, 6, 72, 72)
    rows_b, mask_b, zq_b = head_rows(HEADS_F, 3, 6, 40, 40)
    keys_a, keys_b = (pair_keys(144, half), pair_keys(160, half))
    toep_a, toep_b = (toeplitz(keys_a, 6, 6 * half), toeplitz(keys_b, 6, 6 * half))
    mid = (rows_a, mask_a, zq_a, keys_a, toep_a, 72)
    edge = (rows_b, mask_b, zq_b, keys_b, toep_b, 40)
    return {"a": mid, "b": edge, "c": edge}


def store_bias(name, table, kind, out):
    _, _, zq, keys, toep, block = kind
    lat = lax.axis_index("lat")
    late = along_lanes(160) >= 80
    edge = {
        "a": 0.0,
        "b": jnp.where(late & (lat == lax.axis_size("lat") - 1), NEGATIVE, 0.0),
        "c": jnp.where(jnp.logical_not(late) & (lat == 0), NEGATIVE, 0.0),
        "q": 0.0,
    }[name]
    for zone in range(2):
        terms = bias_rows(table, toep, zone, block)
        out[zone] = terms + banned(keys, zq, 0 if name == "q" else zone) + edge


def coarse_kind():
    rows, mask, zq = head_rows(HEADS_C, 6, 3, 40, 144)
    keys = group_keys()
    toep = toeplitz(keys, 3, 3 * lax.rem(lax.axis_index("lon"), 4).astype(F32))
    return (rows, mask, zq, keys, toep, 144)


def fine_windows(zone):
    edge = zone * 40
    return (
        ("a", (MID + zone * 72, 72), [(0, MID + zone * 72, 72), (1, MID + zone * 72, 72)]),
        ("b", (TOP + edge, 40), [(0, TOP + edge, 40), (1, TOP + edge, 40), (2, edge, 40), (3, edge, 40)]),
        ("c", (LOW + edge, 40), [(4, edge, 40), (5, edge, 40), (0, LOW + edge, 40), (1, LOW + edge, 40)]),
    )


SOURCES = (0, FINE, 2 * FINE, 2 * FINE + SIDE, 2 * FINE + 2 * SIDE, 2 * FINE + 3 * SIDE)
ALL_ROWS = 2 * FINE + 4 * SIDE


def gathered(ref, pieces):
    return jnp.concatenate(
        [ref[SOURCES[source] + start : SOURCES[source] + start + count, :] for source, start, count in pieces],
        0,
    )


def fine_forward_body(
    own_ref,
    par_ref,
    upo_ref,
    upp_ref,
    dno_ref,
    dnp_ref,
    gain_ref,
    shift_ref,
    qkv_ref,
    qkv_bias_ref,
    proj_ref,
    proj_bias_ref,
    merge_gain_ref,
    merge_shift_ref,
    merge_ref,
    coarse_gain_ref,
    coarse_shift_ref,
    bias_a,
    bias_b,
    bias_c,
    hat_out,
    normed,
    q_out,
    k_out,
    v_out,
    probs_a,
    probs_b,
    probs_c,
    mix_out,
    fine_out,
    merged_out,
    coarse_out,
    cnorm_out,
):
    gain, shift = (vector(gain_ref), vector(shift_ref))
    own = own_ref[...].astype(F32)
    for place, tokens in enumerate(
        [own, par_ref[...].astype(F32)]
        + [unpacked_side(ref[...].astype(F32)) for ref in (upo_ref, upp_ref, dno_ref, dnp_ref)]
    ):
        hat, _ = norm_parts(tokens)
        at = slice(SOURCES[place], SOURCES[place] + tokens.shape[0])
        hat_out[at, :] = hat
        normed[at, :] = (hat * gain + shift).astype(BF16)
    bias = vector(qkv_bias_ref)
    q_out[...] = rounded(dot(normed[0:FINE, :], qkv_ref[:, 0:C_F]) + bias[:, 0:C_F])
    k_out[...] = rounded(dot(normed[...], qkv_ref[:, C_F : 2 * C_F]) + bias[:, C_F : 2 * C_F])
    v_out[...] = rounded(dot(normed[...], qkv_ref[:, 2 * C_F :]) + bias[:, 2 * C_F :])
    kinds = fine_kinds()
    probs_refs = {"a": (bias_a, probs_a), "b": (bias_b, probs_b), "c": (bias_c, probs_c)}
    mixtures = {}
    for zone in range(2):
        for name, (start, count), pieces in fine_windows(zone):
            rows, mask = kinds[name][:2]
            bias_ref, probs_ref = probs_refs[name]
            probs, mixture = attend(
                q_out[start : start + count, :],
                gathered(k_out, pieces),
                gathered(v_out, pieces),
                rows,
                mask,
                bias_ref[zone],
            )
            probs_ref[zone] = probs
            mixtures[name, zone] = mixture
    mixture = jnp.concatenate([mixtures[name, zone] for name in "cab" for zone in range(2)], 0)
    mix_out[...] = mixture.astype(BF16)
    attn = rounded(dot(mixture, proj_ref[...]) + vector(proj_bias_ref))
    fine = rounded(own + attn)
    fine_out[...] = fine.astype(BF16)
    quartet = dot(quartet_order(), fine)
    parts = [quartet[p * COARSE : (p + 1) * COARSE] for p in range(4)]
    hats, _ = quartet_norm(parts)
    coarse = None
    gain, shift = (vector(merge_gain_ref), vector(merge_shift_ref))
    for p in range(4):
        at = slice(p * C_F, (p + 1) * C_F)
        value = (hats[p] * gain[:, at] + shift[:, at]).astype(BF16)
        merged_out[p] = value
        part = dot(value, merge_ref[p * C_F : (p + 1) * C_F, :])
        coarse = part if coarse is None else coarse + part
    coarse = rounded(coarse)
    coarse_out[...] = coarse
    hat, _ = norm_parts(coarse)
    cnorm_out[...] = (hat * vector(coarse_gain_ref) + vector(coarse_shift_ref)).astype(BF16)


def quartet_norm(parts):
    width = 4.0 * C_F
    mean = sum(jnp.sum(part, -1, keepdims=True) for part in parts) / width
    centres = [part - mean for part in parts]
    spread = sum(jnp.sum(c * c, -1, keepdims=True) for c in centres) / width
    scale = lax.rsqrt(spread + EPS)
    return ([c * scale for c in centres], scale)


def coarse_body(
    group_ref,
    own_ref,
    coarse_ref,
    cot_ref,
    qkv_ref,
    qkv_bias_ref,
    proj_ref,
    proj_bias_ref,
    bias_ref,
    out_ref,
    parts_out,
    own_out,
    flat_out,
    table_out,
    cot_out,
    stage,
    keys,
    values,
):
    fetch_groups(stage, cot_ref)
    cot = dot(coarse_order(), stage[...])
    cot_out[...] = cot
    bias = vector(qkv_bias_ref)
    wide = [slice(i * C_C, (i + 1) * C_C) for i in range(3)]
    queries = rounded(dot(own_ref[...], qkv_ref[:, wide[0]]) + bias[:, wide[0]])
    group = jnp.concatenate([group_ref[g] for g in range(4)], 0)
    keys[...] = rounded(dot(group, qkv_ref[:, wide[1]]) + bias[:, wide[1]])
    values[...] = rounded(dot(group, qkv_ref[:, wide[2]]) + bias[:, wide[2]])
    mixture_grad = rounded(dot_nt(cot, proj_ref[...]))
    rows, mask, _, _, toep, _ = coarse_kind()
    mixtures, query_grads, grads = ([], [], [])
    for zone in range(2):
        here = slice(zone * 40, (zone + 1) * 40)
        at = [slice(g * COARSE + zone * 40, g * COARSE + zone * 40 + 40) for g in range(4)]
        k = jnp.concatenate([keys[there, :] for there in at], 0)
        v = jnp.concatenate([values[there, :] for there in at], 0)
        probs, mixture = attend(queries[here], k, v, rows, mask, bias_ref[zone])
        dq, dk, dv, table = attend_back(
            queries[here], k, v, rows, mask, probs, mixture_grad[here], toep, 144
        )
        table_out[zone * 144 : (zone + 1) * 144, :] = table
        mixtures.append(mixture)
        query_grads.append(dq)
        grads.append((dk, dv))
    key_grad, value_grad = (
        rounded(
            jnp.concatenate(
                [grads[zone][i][g * 40 : (g + 1) * 40] for g in range(4) for zone in range(2)], 0
            )
        )
        for i in range(2)
    )
    query_grad = jnp.concatenate(query_grads, 0)
    part = dot_nt(key_grad, qkv_ref[:, wide[1]]) + dot_nt(value_grad, qkv_ref[:, wide[2]])
    for g in range(4):
        parts_out[g] = part[g * COARSE : (g + 1) * COARSE].astype(BF16)
    own_out[...] = dot_nt(query_grad, qkv_ref[:, wide[0]])
    for i, (norm, grad) in enumerate(
        ((own_ref[...], query_grad), (group, key_grad), (group, value_grad))
    ):
        weight = dot_tn(norm, grad)
        sums = column_sum(grad)
        for c in range(3):
            lanes = slice(c * 128, (c + 1) * 128)
            flat_out[pl.ds(3 * i + c, C_C, stride=9), :] = weight[:, lanes]
            flat_out[3456 + 3 * i + c : 3457 + 3 * i + c, :] = sums[:, lanes]
    mixture = jnp.concatenate(mixtures, 0)
    flat_store(flat_out, 3465, dot_tn(mixture, cot))
    flat_store(flat_out, 4617, column_sum(cot))
    attn = rounded(dot(mixture, proj_ref[...]) + vector(proj_bias_ref))
    stage[...] = dot(coarse_order(True), coarse_ref[...] + attn)
    store_groups(out_ref, stage)


def flat_store(flat, start, matrix):
    height, width = matrix.shape
    step = width // 128
    for c in range(step):
        lanes = slice(c * 128, (c + 1) * 128)
        if height == 1:
            flat[start + c : start + c + 1, :] = matrix[:, lanes]
        else:
            flat[pl.ds(start + c, height, stride=step), :] = matrix[:, lanes]


def keep_square(square, matrix):
    height = matrix.shape[0]
    square[0, 0:height, :] = matrix[:, 0:128]
    square[1, 0:height, 0:64] = matrix[:, 128:192]


def every_other(square, start):
    take = pl.ds(start, 96, stride=2)
    return jnp.concatenate([square[0, take, :], square[1, take, :][:, 0:64]], 1)


def block_store(flat, start, blocks):
    for c, block in enumerate(blocks):
        if block.shape[0] == 1:
            flat[start + c : start + c + 1, :] = block
        else:
            flat[pl.ds(start + c, block.shape[0], stride=len(blocks)), :] = block


def fine_back_body(
    starts,
    rows,
    part_ref,
    own_part_ref,
    cot_ref,
    coarse_ref,
    merged_ref,
    fine_ref,
    hat_ref,
    normed_ref,
    mix_ref,
    q_ref,
    k_ref,
    v_ref,
    probs_a,
    probs_b,
    probs_c,
    qkv_ref,
    cgain_ref,
    merge_gain_ref,
    merge_ref,
    proj_ref,
    flat_c,
    table_q,
    fog_out,
    own_out,
    par_out,
    upo_out,
    upp_out,
    dno_out,
    dnp_out,
    pieces_out,
    tables_out,
    kgrad,
    vgrad,
    flat,
    tables,
    square,
):
    norm_grad = part_ref[...] + own_part_ref[...]
    hat, scale = norm_parts(coarse_ref[...])
    flat_store(flat, 3477, column_sum(norm_grad * hat))
    flat_store(flat, 3480, column_sum(norm_grad))
    coarse_grad = rounded(cot_ref[...] + norm_back(hat, scale, norm_grad, vector(cgain_ref)))
    quartet = dot(quartet_order(), fine_ref[...])
    hats, scale = quartet_norm([quartet[p * COARSE : (p + 1) * COARSE] for p in range(4)])
    inners, gains, shifts = ([], [], [])
    merge_gain = vector(merge_gain_ref)
    for p in range(4):
        at = slice(p * C_F, (p + 1) * C_F)
        flat_store(flat, 1173 + 3 * p * C_F, dot_tn(merged_ref[p], coarse_grad))
        grad = dot_nt(coarse_grad, merge_ref[at, :])
        gains.append(column_sum(grad * hats[p]))
        shifts.append(column_sum(grad))
        inners.append(grad * merge_gain[:, at])
    block_store(flat, 1161, lane_blocks(gains))
    block_store(flat, 1167, lane_blocks(shifts))
    width = 4.0 * C_F
    first = sum(jnp.sum(inner, -1, keepdims=True) for inner in inners) / width
    second = sum(jnp.sum(i * h, -1, keepdims=True) for i, h in zip(inners, hats)) / width
    grads = jnp.concatenate([scale * (i - first - h * second) for i, h in zip(inners, hats)], 0)
    high = rounded(grads)
    unmerge = quartet_order(True)
    attn_grad = dot(unmerge, high)
    fog_out[...] = attn_grad + dot(unmerge, grads - high)
    mixture_grad = rounded(dot_nt(attn_grad, proj_ref[...]))
    weight = dot_tn(mix_ref[...], attn_grad)
    corner = weight[0:1]
    keep_square(square, jnp.concatenate([weight, column_sum(attn_grad)], 0))
    block_store(flat, 873, lane_blocks([every_other(square, 1), every_other(square, 2)]))
    kinds = fine_kinds()
    places = {"a": (PART_A, probs_a), "b": (PART_B, probs_b), "c": (PART_C, probs_c)}
    query_grads = {}
    for zone in range(2):
        for name, (start, count), pieces in fine_windows(zone):
            rows_at, mask, _, _, toep, block = kinds[name]
            table_at, probs_ref = places[name]
            dq, dk, dv, table = attend_back(
                q_ref[start : start + count, :],
                gathered(k_ref, pieces),
                gathered(v_ref, pieces),
                rows_at,
                mask,
                probs_ref[zone],
                mixture_grad[start : start + count],
                toep,
                block,
            )
            query_grads[name, zone] = dq
            for c in range(3):
                at = table_at + (2 * c + zone) * block
                tables[at : at + block, :] = table[:, c * 128 : (c + 1) * 128]
            at = 0
            for source, begin, size in pieces:
                to = slice(SOURCES[source] + begin, SOURCES[source] + begin + size)
                kgrad[to, :] = rounded(dk[at : at + size])
                vgrad[to, :] = rounded(dv[at : at + size])
                at += size
    query_grad = jnp.concatenate([query_grads[name, zone] for name in "cab" for zone in range(2)], 0)
    part = dot_nt(kgrad[...], qkv_ref[:, C_F : 2 * C_F]) + dot_nt(vgrad[...], qkv_ref[:, 2 * C_F :])
    own = part[0:FINE] + dot_nt(query_grad, qkv_ref[:, 0:C_F])
    own_out[...] = own
    par_out[...] = part[FINE : 2 * FINE].astype(BF16)
    for place, out in enumerate((upo_out, upp_out, dno_out, dnp_out)):
        at = SOURCES[2 + place]
        out[...] = packed_side(part[at : at + SIDE]).astype(BF16)
    hat_grad = column_sum(own * hat_ref[0:FINE, :])
    hat_grad += column_sum(part[FINE:] * hat_ref[FINE:, :])
    block_store(
        flat, 0, lane_blocks([hat_grad, column_sum(own) + column_sum(part[FINE:])])
    )
    evens, odds, sums = ([], [], [])
    for norm, grad in (
        (normed_ref[0:FINE, :], query_grad),
        (normed_ref[...], kgrad[...]),
        (normed_ref[...], vgrad[...]),
    ):
        keep_square(square, dot_tn(norm, grad))
        evens.append(every_other(square, 0))
        odds.append(every_other(square, 1))
        sums.append(column_sum(grad))
    block_store(flat, 3, lane_blocks(evens + odds))
    block_store(flat, 867, lane_blocks(sums + [corner]))
    tables[240:PART_A, :] = jnp.zeros((PART_A - 240, 128), F32)
    tables[PART_END:, :] = jnp.zeros((TABLE_ROWS - PART_END, 128), F32)
    for c in range(3):
        at = PART_Q + 288 * c
        tables[at : at + 288, :] = table_q[:, c * 128 : (c + 1) * 128]
    split = 3483
    trows = TABLE_ROWS // len(starts)
    for place, start in starts:
        end = start + rows
        if start < split:
            size = min(end, split) - start
            value = flat[start : start + size, :]
            if end > split:
                value = jnp.concatenate([value, flat_c[0 : end - split, :]], 0)
        else:
            size = min(end, 8103) - start
            value = flat_c[start - split : start - split + size, :]
            if size < rows:
                value = jnp.concatenate([value, jnp.zeros((rows - size, 128), F32)], 0)
        chunk = pieces_out.shape[2]
        for y in range(pieces_out.shape[0]):
            pieces_out[y, place] = value[y * chunk : (y + 1) * chunk].astype(BF16)
        tables_out[place] = tables[place * trows : (place + 1) * trows, :].astype(BF16)


def final_body(
    x_ref,
    gain_ref,
    fog_ref,
    own_ref,
    par_ref,
    low_ref,
    high_ref,
    t_ref,
    token_out,
    fine_out,
    coarse_out,
    stage,
    grad,
):
    grad[...] = own_ref[...] + par_ref[...].astype(F32)
    grad[LOW : LOW + SIDE, :] += unpacked_side(low_ref[...].astype(F32))
    grad[TOP : TOP + SIDE, :] += unpacked_side(high_ref[...].astype(F32))
    hat, scale = norm_parts(x_ref[...].astype(F32))
    total = fog_ref[...] + norm_back(hat, scale, rounded(grad[...]), vector(gain_ref))
    stage[...] = dot(fine_order(True), total)
    store_groups(token_out, stage)

    def part(start, height):
        return jnp.concatenate(
            [t_ref[start + c * height : start + (c + 1) * height, :] for c in range(3)], 1
        )

    def natural(kind, block):
        total = None
        for zk in range(2):
            term = dot(table_rows(kind, zk, True), dot_nt(block, table_lanes(zk)))
            total = term if total is None else total + term
        return total

    fine_out[0:288, :] = natural("a", part(PART_A, 144))
    fine_out[288:576, :] = natural("b", part(PART_B, 80)) + natural("c", part(PART_C, 80))
    coarse_out[...] = natural("q", part(PART_Q, 288))


def mesh_parts(lat, lon):
    cores = 2
    xs = 4 if lon % 8 == 0 else 1
    ys = 4 if lat % 4 == 0 else lat
    return (cores, xs, lon // (cores * xs), ys, lat // ys)


def piece_rows(total, lon, ys):
    longest = -(-(127 + total // lon) // 128)
    unit = 16 * ys
    return -(-longest // unit) * unit


def reduce_body(
    dims,
    norm_factor,
    compute,
    g_ref,
    gt_ref,
    par_ref,
    upo_ref,
    upp_ref,
    dno_ref,
    dnp_ref,
    p_ref,
    t_ref,
    par_out,
    low_out,
    high_out,
    par_buf,
    up_buf,
    down_buf,
    up_sum,
    down_sum,
    low_buf,
    high_buf,
    core_buf,
    head_buf,
    tail_buf,
    y_buf,
    y_sum,
    x_buf,
    x_sum,
    z_buf,
    h_send,
    h_buf,
    share,
    tab_core,
    tab_x,
    tab_sum,
    tab_own,
    tab_hand,
    tab_z,
    tab_all,
    send_sems,
    recv_sems,
):
    cores, xs, zs, ys, hs = dims
    half = xs * zs
    chunk = g_ref.shape[2]
    trows = gt_ref.shape[1]
    lat, lon = (lax.axis_index("lat"), lax.axis_index("lon"))
    core = lax.rem(lon, cores)
    x = lax.rem(lon // cores, xs)
    z = lon // (cores * xs)
    y = lax.rem(lat, ys)
    h = lat // ys
    lats = ys * hs

    def at(here, d, count):
        return lax.rem(here + d, count)

    def lon_of(core_to, x_to, z_to):
        return (z_to * xs + x_to) * cores + core_to

    other_core = (lat, lon_of(1 - core, x, z))
    x_peers = {d: (lat, lon_of(core, at(x, d, xs), z)) for d in range(1, xs)}
    y_peers = {d: (h * ys + at(y, d, ys), lon) for d in range(1, ys)}
    z_peers = {d: (lat, lon_of(core, x, at(z, d, zs))) for d in range(1, zs)}
    far = (at(h, 1, hs) * ys + y, lon)
    before, after = ((at(lat, lats - 1, lats), lon), (at(lat, 1, lats), lon))
    beside = (lat, partner_of(lon, cores * half))
    peers = [before, after] + ([far] if hs > 1 else [])
    peers += list(z_peers.values())[::-1] + list(y_peers.values()) + list(x_peers.values())
    peers += [beside, other_core]
    greet(peers)
    compute()
    await_greetings(peers)
    pending = []

    def send(src, dst, peer):
        sem = len(pending)
        copy = start_copy(src, dst, send_sems.at[sem], recv_sems.at[sem], peer)
        pending.append(copy)
        return copy

    def arrived(copies):
        for copy in copies:
            copy.wait_recv()

    def add_into(target, terms, count):
        def step(i, carry):
            total = terms[0](i).astype(F32)
            for term in terms[1:]:
                total = total + term(i).astype(F32)
            target[i] = total.astype(BF16)
            return carry

        lax.fori_loop(0, count, step, 0)

    away = pl.ds((1 - core) * half, half)
    mine = core * half
    table_core = send(gt_ref.at[away], tab_core, other_core)
    edges = [
        send(upp_ref, up_buf, beside),
        send(dnp_ref, down_buf, beside),
        send(par_ref, par_buf, beside),
    ]
    order = {4: (2, 1, 3, 0), 2: (1, 0), 1: (0,)}[ys]
    crossing = {d: send(g_ref.at[at(y, d, ys), away], core_buf.at[d], other_core) for d in order}
    table_core.wait_recv()
    add_into(tab_core, [lambda i: tab_core[i], lambda i: gt_ref[mine + i]], half)
    table_x = [
        send(tab_core.at[pl.ds(at(x, d, xs) * zs, zs)], tab_x.at[d - 1], x_peers[d])
        for d in range(1, xs)
    ]
    cut = half // 2
    head, tail = (pl.ds(0, cut), pl.ds(cut, half - cut))
    gathered_y = []
    for d in order:
        crossing[d].wait_recv()
        row = at(y, d, ys)
        buf = core_buf.at[d]
        add_into(buf, [lambda i: buf[i], lambda i: g_ref[row, mine + i]], half)
        if ys == 4 and d == 2:
            over_right = send(core_buf.at[2, head], head_buf, y_peers[1])
            over_left = send(core_buf.at[2, tail], tail_buf, y_peers[3])
        if ys == 4 and d == 1:
            gathered_y.append(send(core_buf.at[1, tail], y_buf.at[0, tail], y_peers[1]))
        if ys == 4 and d == 3:
            gathered_y.append(send(core_buf.at[3, head], y_buf.at[1, head], y_peers[3]))
        if ys == 2 and d == 1:
            gathered_y.append(send(core_buf.at[1], y_buf.at[0], y_peers[1]))
    if ys == 4:
        over_right.wait_recv()
        right = core_buf.at[1]
        add_into(right, [lambda i: right[i], lambda i: head_buf[i]], cut)
        gathered_y.append(send(core_buf.at[1, head], y_buf.at[0, head], y_peers[1]))
        over_left.wait_recv()
        left = core_buf.at[3, tail]
        add_into(left, [lambda i: left[i], lambda i: tail_buf[i]], half - cut)
        gathered_y.append(send(core_buf.at[3, tail], y_buf.at[1, tail], y_peers[3]))

    arrived(edges[:2])
    up_sum[...] = (upo_ref[...].astype(F32) + up_buf[...].astype(F32)).astype(BF16)
    down_sum[...] = (dno_ref[...].astype(F32) + down_buf[...].astype(F32)).astype(BF16)
    edges.append(send(up_sum, low_buf, after))
    edges.append(send(down_sum, high_buf, before))
    arrived(table_x)
    base = x * zs
    terms = [lambda i: tab_core[base + i]]
    terms += [lambda i, d=d: tab_x[d - 1, i] for d in range(1, xs)]
    add_into(tab_sum, terms, zs)
    table_z = [
        send(tab_sum.at[at(z, d, zs)], tab_z.at[d - 1], z_peers[d]) for d in range(1, zs)
    ]

    arrived(gathered_y)
    terms = [lambda i: core_buf[0, i]]
    terms += [lambda i, d=d: y_buf[d, i] for d in range({4: 2, 2: 1, 1: 0}[ys])]
    add_into(y_sum, terms, half)
    along_x = [
        send(y_sum.at[pl.ds(at(x, d, xs) * zs, zs)], x_buf.at[d - 1], x_peers[d])
        for d in range(1, xs)
    ]

    arrived(table_z)
    total = tab_sum[z].astype(F32)
    for d in range(1, zs):
        total = total + tab_z[d - 1].astype(F32)
    own = tab_all.at[core, x, z]
    tab_own[...] = (total * norm_factor).astype(BF16)
    tab_all[core, x, z] = tab_own[...]
    first_row = ((core * xs + x) * zs + z) * trows

    def prepared(src, dst, peer):
        sem = len(pending)
        copy = pltpu.make_async_remote_copy(
            src_ref=src,
            dst_ref=dst,
            send_sem=send_sems.at[sem],
            recv_sem=recv_sems.at[sem],
            device_id=peer,
            device_id_type=MESH,
        )
        pending.append(copy)
        return copy

    handed = prepared(tab_own, tab_hand, before)
    pending.pop()
    pending.append(None)
    back_z = [prepared(own, own, z_peers[d]) for d in range(1, zs)]

    @pl.when(first_row < PART_A)
    def _():
        handed.start()

    @pl.when(first_row >= PART_A)
    def _():
        for copy in back_z:
            copy.start()

    arrived(along_x)
    terms = [lambda i: y_sum[base + i]]
    terms += [lambda i, d=d: x_buf[d - 1, i] for d in range(1, xs)]
    add_into(x_sum, terms, zs)
    along_z = [send(x_sum.at[at(z, d, zs)], z_buf.at[d - 1], z_peers[d]) for d in range(1, zs)]

    @pl.when(first_row < PART_A)
    def _():
        handed.wait()
        row = first_row + lax.broadcasted_iota(jnp.int32, (trows, 128), 0)
        tab_all[core, x, z] = jnp.where(
            row < PART_A, tab_hand[...].astype(F32), tab_own[...].astype(F32)
        ).astype(BF16)
        for copy in back_z:
            copy.start()

    arrived(along_z)
    total = x_sum[z].astype(F32)
    for d in range(1, zs):
        total = total + z_buf[d - 1].astype(F32)
    if hs > 1:
        h_send[...] = total.astype(BF16)
        across = send(h_send, h_buf, far)
    arrived(back_z)
    own = tab_all.at[core, x]
    back_x = [send(own, own, x_peers[d]) for d in range(1, xs)]
    if hs > 1:
        across.wait_recv()
        total = h_send[...].astype(F32) + h_buf[...].astype(F32)
    rows = pl.ds(pl.multiple_of(y * chunk, 8), chunk)
    share[rows, :] = total * norm_factor
    back_y = [send(share.at[rows], share.at[rows], y_peers[d]) for d in range(1, ys)]
    arrived(back_x)
    own = tab_all.at[core]
    back_core = send(own, own, other_core)
    arrived(edges[2:])
    par_out[...] = par_buf[...]
    low_out[...] = low_buf[...]
    high_out[...] = high_buf[...]
    arrived(back_y)
    p_ref[...] = share[...]
    back_core.wait_recv()
    t_ref[...] = tab_all[...]
    for copy in pending:
        if copy is not None:
            copy.wait_send()


def backward_reduce_body(dims, norm_factor, starts, rows, count, *refs):
    inputs, refs = (refs[:count], refs[count:])
    fog_out, own_out, *outs = refs[:7]
    refs = refs[7:]
    inner, refs = (refs[:5], refs[5:])
    edges, pieces, tables = (refs[:5], refs[5], refs[6])

    def compute():
        fine_back_body(
            starts, rows, *inputs, fog_out, own_out, *edges, pieces, tables, *inner
        )

    reduce_body(dims, norm_factor, compute, pieces, tables, *edges, *outs, *refs[7:])


def backward_reduce(args, starts, rows, trows, norm_factor, dims):
    cores, xs, zs, ys, hs = dims
    half = xs * zs
    chunk = rows // ys
    sem = pltpu.SemaphoreType.DMA((64,))
    side = (128, 128)
    all_tables = (cores, xs, zs, trows, 128)
    outs = [((FINE, C_F), F32), ((FINE, C_F), F32)]
    outs += [((ys * chunk, 128), F32), (all_tables, BF16), ((FINE, C_F), BF16)]
    outs += [(side, BF16), (side, BF16)]
    wide = [(ALL_ROWS, C_F), (ALL_ROWS, C_F), (3488, 128), (TABLE_ROWS, 128), (2, 200, 128)]
    buffers = [
        (FINE, C_F),
        *[side] * 4,
        (ys, len(starts), chunk, 128),
        (len(starts), trows, 128),
        (FINE, C_F),
        *[side] * 6,
        (ys, half, chunk, 128),
        (half // 2, chunk, 128),
        (half - half // 2, chunk, 128),
        (2, half, chunk, 128),
        (half, chunk, 128),
        (max(xs - 1, 1), zs, chunk, 128),
        (zs, chunk, 128),
        (max(zs - 1, 1), chunk, 128),
        (chunk, 128),
        (chunk, 128),
        None,
        (half, trows, 128),
        (max(xs - 1, 1), zs, trows, 128),
        (zs, trows, 128),
        (trows, 128),
        (trows, 128),
        (max(zs - 1, 1), trows, 128),
        all_tables,
    ]
    scratch = [pltpu.VMEM(shape, F32) for shape in wide]
    scratch += [
        pltpu.VMEM((ys * chunk, 128), F32) if shape is None else pltpu.VMEM(shape, BF16)
        for shape in buffers
    ]
    body = functools.partial(
        backward_reduce_body, dims, norm_factor, starts, rows, len(args)
    )
    return remote_call(body, outs, args, scratch + [sem, sem], 7, "fine_backward_reduce", 40)


def shards(
    tokens,
    fine_gain,
    fine_shift,
    fine_qkv,
    fine_qkv_bias,
    fine_proj,
    fine_proj_bias,
    fine_table,
    merge_gain,
    merge_shift,
    merge_weight,
    coarse_gain,
    coarse_shift,
    coarse_qkv,
    coarse_qkv_bias,
    coarse_proj,
    coarse_proj_bias,
    coarse_table,
    cotangent,
):
    lat_count, lon_count = (lax.axis_size("lat"), lax.axis_size("lon"))
    lat, lon = (lax.axis_index("lat"), lax.axis_index("lon"))
    norm_factor = 1.0 / math.sqrt(tokens.size // C_F * lat_count * lon_count / 4)
    fine_rows = fine_table.reshape(576, 138)
    coarse_rows = coarse_table.reshape(576, 138)
    cells = tokens[0].transpose(1, 2, 0, 3)
    cot_cells = cotangent[0].transpose(1, 2, 0, 3)

    group = min(8, lon_count)
    side = ((128, 128), BF16)
    own = ((FINE, C_F), BF16)
    table_part = ((group, PART_A // group, 128), BF16)
    x, low, high, table_send = call(
        prepare_body,
        [own, side, side, table_part],
        (cells, fine_rows),
        [pltpu.VMEM((288, C_F), F32)],
        "prepare",
        2,
    )
    halo = [own, side, side, side, side, table_part]
    bias_a, bias_b = (((2, 432, 144), F32), ((2, 240, 160), F32))
    par, upo, upp, dno, dnp, bias_a, bias_b, bias_c, bias_q = remote_call(
        halo_body,
        halo[:5] + [bias_a, bias_b, bias_b, ((2, 432, 160), F32)],
        (x, low, high, table_send, fine_rows, coarse_rows),
        [pltpu.VMEM(*s) for s in halo] + semaphores(6, max(group - 1, 1)),
        1,
        "halo",
        12,
    )
    (
        hat,
        normed,
        q,
        k,
        v,
        probs_a,
        probs_b,
        probs_c,
        mixture,
        fine_out,
        merged,
        coarse,
        cnorm,
        gathered_norm,
    ) = remote_call(
        forward_gather_body,
        [
            ((ALL_ROWS, C_F), F32),
            ((ALL_ROWS, C_F), BF16),
            ((FINE, C_F), F32),
            ((ALL_ROWS, C_F), F32),
            ((ALL_ROWS, C_F), F32),
            ((2, 432, 144), F32),
            ((2, 240, 160), F32),
            ((2, 240, 160), F32),
            own,
            own,
            ((4, COARSE, C_F), BF16),
            ((COARSE, C_C), F32),
            ((COARSE, C_C), BF16),
            ((4, COARSE, C_C), BF16),
        ],
        (
            x,
            par,
            upo,
            upp,
            dno,
            dnp,
            fine_gain,
            fine_shift,
            fine_qkv,
            fine_qkv_bias,
            fine_proj,
            fine_proj_bias,
            merge_gain,
            merge_shift,
            merge_weight,
            coarse_gain,
            coarse_shift,
            bias_a,
            bias_b,
            bias_c,
        ),
        [pltpu.VMEM((4, COARSE, C_C), BF16)] + semaphores(3),
        2,
        "fine_forward_gather",
        11,
    )
    coarse_out, norm_part, own_part, flat_c, table_q, cot = remote_call(
        coarse_scatter_body,
        [
            ((6, 3, 4, C_C), BF16),
            ((COARSE, C_C), F32),
            ((COARSE, C_C), F32),
            ((4620, 128), F32),
            ((288, 384), F32),
            ((COARSE, C_C), F32),
        ],
        (
            gathered_norm,
            cnorm,
            coarse,
            cot_cells,
            coarse_qkv,
            coarse_qkv_bias,
            coarse_proj,
            coarse_proj_bias,
            bias_q,
        ),
        [
            pltpu.VMEM((72, C_C), F32),
            pltpu.VMEM((4 * COARSE, C_C), F32),
            pltpu.VMEM((4 * COARSE, C_C), F32),
            pltpu.VMEM((4, COARSE, C_C), BF16),
            pltpu.VMEM((3, COARSE, C_C), BF16),
            *semaphores(3),
        ],
        3,
        "coarse_attention_scatter",
        12,
    )
    dims = mesh_parts(lat_count, lon_count)
    cores, xs, zs, ys, hs = dims
    segment = PARAMS // lon_count
    rows = piece_rows(PARAMS, lon_count, ys)
    starts = []
    for index in range(lon_count):
        core, x_at, z_at = (index % cores, index // cores % xs, index // (cores * xs))
        starts.append(((core * xs + x_at) * zs + z_at, index * segment // 128))
    fine_out_grad, own_grad, owned, table_sum, par_back, low_back, high_back = backward_reduce(
        (
            norm_part,
            own_part,
            cot,
            coarse,
            merged,
            fine_out,
            hat,
            normed,
            mixture,
            q,
            k,
            v,
            probs_a,
            probs_b,
            probs_c,
            fine_qkv,
            coarse_gain,
            merge_gain,
            merge_weight,
            fine_proj,
            flat_c,
            table_q,
        ),
        starts,
        rows,
        TABLE_ROWS // lon_count,
        norm_factor,
        dims,
    )
    shift = lax.rem(lon * segment, 128)
    param_grads = lax.dynamic_slice(owned.reshape(-1), (shift,), (segment,))
    token_grad, fine_total, coarse_total = call(
        final_body,
        [((12, 6, 4, C_F), BF16), ((576, 138), F32), ((576, 138), F32)],
        (
            x,
            fine_gain,
            fine_out_grad,
            own_grad,
            par_back,
            low_back,
            high_back,
            table_sum.reshape(TABLE_ROWS, 128),
        ),
        [pltpu.VMEM((288, C_F), F32), pltpu.VMEM((FINE, C_F), F32)],
        "final",
        2,
    )
    return (
        coarse_out.transpose(2, 0, 1, 3)[None],
        token_grad.transpose(2, 0, 1, 3)[None],
        param_grads,
        fine_total.reshape(2, -1),
        coarse_total.reshape(2, -1),
    )


def solution(mesh):
    tiles = P(None, None, "lat", "lon", None)
    whole = P()
    rows = P("lat", None)
    return jax.shard_map(
        shards,
        mesh=mesh,
        in_specs=(tiles,) + (whole,) * 6 + (rows,) + (whole,) * 9 + (rows, tiles),
        out_specs=(tiles, tiles, P("lon"), rows, rows),
        check_vma=False,
    )
```

```python
import functools
import math

import jax
import jax.numpy as jnp
from jax import lax
from jax.experimental import pallas as pl
from jax.experimental.pallas import tpu as pltpu
from jax.sharding import PartitionSpec as P

HEAD = 32
HEADS_F = 6
HEADS_C = 12
C_F = 192
C_C = 384
SPAN = 23
EPS = 1e-05
NEGATIVE = -1e30
MESH = pl.DeviceIdType.MESH
F32 = jnp.float32
BF16 = jnp.bfloat16
MIB = 1024 * 1024
VMEM_BYTES = 28 * MIB

LOW, MID, TOP = (0, 80, 224)
PARAMS = 1037184
TABLE_ROWS = 2048
FINE = 304
SIDE = 80
COARSE = 80
PART_C, PART_A, PART_B, PART_Q, PART_END = (0, 256, 688, 928, 1792)


def whole(x, n):
    return jnp.floor((x + 0.5) * (1.0 / n))


def rest(x, n):
    return x - n * whole(x, n)


def down_rows(n):
    return lax.broadcasted_iota(jnp.int32, (n, 1), 0).astype(F32)


def along_lanes(n):
    return lax.broadcasted_iota(jnp.int32, (1, n), 1).astype(F32)


def index_and_other(n, m, flip):
    return (along_lanes(n), down_rows(m)) if flip else (down_rows(n), along_lanes(m))


def match(a, b):
    return jnp.where(a == b, 1.0, 0.0).astype(BF16)


def fine_row(zone, zq, row, col):
    low = LOW + zone * 40 + (zq * 3 + row) * 6 + col
    mid = MID + zone * 72 + (zq * 6 + row - 3) * 6 + col
    top = TOP + zone * 40 + (zq * 3 + row - 9) * 6 + col
    return jnp.where(row < 3, low, jnp.where(row < 9, mid, top))


def fine_order(flip=False):
    at, cells = index_and_other(FINE, 288, flip)
    low, top = (at < MID, at >= TOP)
    edge = jnp.where(top, at - TOP, at)
    mid = at - MID
    in_edge = low | top
    part = rest(edge, 40)
    zone = jnp.where(in_edge, whole(edge, 40), whole(mid, 72))
    zq = jnp.where(in_edge, whole(part, 18), whole(rest(mid, 72), 36))
    row = jnp.where(
        in_edge,
        whole(rest(part, 18), 6) + jnp.where(top, 9.0, 0.0),
        3 + whole(rest(mid, 36), 6),
    )
    col = jnp.where(in_edge, rest(part, 6), rest(mid, 6))
    code = (row * 6 + col) * 4 + rest(2 * zone + zq + 1, 4)
    return match(jnp.where(in_edge & (part >= 36), -1.0, code), cells)


def coarse_place(at):
    part = rest(at, 40)
    return (whole(at, 40), whole(part, 18), whole(rest(part, 18), 3), rest(part, 3), part < 36)


def coarse_order(flip=False):
    at, cells = index_and_other(COARSE, 72, flip)
    zone, zq, row, col, valid = coarse_place(at)
    code = (row * 3 + col) * 4 + 2 * zone + zq
    return match(jnp.where(valid, code, -1.0), cells)


def quartet_order(flip=False):
    at, tokens = index_and_other(4 * COARSE, FINE, flip)
    p = whole(at, COARSE)
    zone, zq, row, col, valid = coarse_place(rest(at, COARSE))
    rolled = rest(2 * zone + zq + 3, 4)
    source = fine_row(
        whole(rolled, 2), rest(rolled, 2), 2 * row + rest(p, 2), 2 * col + whole(p, 2)
    )
    return match(jnp.where(valid, source, -1.0), tokens)


def head_rows(heads, lats, cols, tokens, block):
    def parts(at):
        part = rest(at, block)
        zq = whole(rest(part, 2 * lats), lats)
        code = (zq * lats + rest(part, lats)) * cols + whole(at, block)
        valid = part < heads * 2 * lats
        return (jnp.where(valid, whole(part, 2 * lats), -1.0), zq, jnp.where(valid, code, -1.0))

    rows = block * cols
    h, zq, code = parts(down_rows(rows))
    mask = match(h, whole(along_lanes(heads * HEAD), HEAD)).astype(F32)
    back = match(parts(along_lanes(rows))[2], down_rows(tokens))
    return ((match(code, along_lanes(tokens)), back), mask, zq)


def pair_keys(size, half):
    u = along_lanes(size)
    if size == 144:
        source, part = (whole(u, 72), rest(u, 72))
        zk, ak, valid = (whole(part, 36), whole(rest(part, 36), 6), part >= 0)
    else:
        slot, part = (whole(u, 40), rest(u, 40))
        source = rest(slot, 2)
        zk = whole(part, 18)
        ak = 3 * whole(slot, 2) + whole(rest(part, 18), 6)
        valid = part < 36
    return (zk, ak, rest(part, 6) + 6 * jnp.abs(half - source), valid)


def group_keys():
    u = along_lanes(160)
    part = rest(u, 40)
    zk, ak = (whole(part, 18), whole(rest(part, 18), 3))
    return (zk, ak, rest(part, 3) + 3 * whole(u, 40), part < 36)


def toeplitz(keys, cols, shift):
    zk, ak, col, valid = keys
    at = down_rows(384)
    tail = at >= 256
    level = jnp.where(tail, whole(at - 256, 64), whole(at, 128))
    entry = jnp.where(tail, 128 + rest(at, 64), rest(at, 128))
    code = (level * 6 + whole(entry, SPAN)) * 64 + rest(entry, SPAN)
    code = jnp.where(entry < 138, code, -1.0)
    key_code = jnp.where(valid, (zk * 6 + ak) * 64 - col + shift + 11, -100.0)
    return [match(code, key_code + oq) for oq in range(cols)]


def table_lanes(zk):
    entry = down_rows(138)
    return match(
        jnp.where(entry < 128, zk * 128 + entry, 256 + zk * 64 + entry - 128), along_lanes(384)
    )


def table_rows(kind, zk, flip=False):
    if kind == "q":
        at, source = index_and_other(288, 576, flip)
        part = rest(at, 144)
        aq = rest(part, 6)
        lead = (whole(aq, 3) * 2 + whole(at, 144)) * HEADS_C + whole(part, 12)
        zq = whole(rest(part, 12), 6)
        return match(((lead * 2 + zq) * 2 + zk) * 3 + rest(aq, 3), source)
    if kind == "a":
        count, block, lats, first = (144, 72, 6, 0)
    else:
        count, block, lats, first = (80, 40, 3, 3 if kind == "c" else 0)
    at, source = index_and_other(count, 288, flip)
    part = rest(at, block)
    lead = whole(at, block) * HEADS_F + whole(part, 2 * lats)
    zq = whole(rest(part, 2 * lats), lats)
    code = ((lead * 2 + zq) * 2 + zk) * 6 + rest(part, lats) + first
    return match(jnp.where(part < 12 * lats, code, -1.0), source)


def dot(a, b):
    return jnp.dot(a.astype(BF16), b.astype(BF16), preferred_element_type=F32)


def dot_nt(a, b):
    return lax.dot_general(
        a.astype(BF16), b.astype(BF16), (((1,), (1,)), ((), ())), preferred_element_type=F32
    )


def dot_tn(a, b):
    return lax.dot_general(
        a.astype(BF16), b.astype(BF16), (((0,), (0,)), ((), ())), preferred_element_type=F32
    )


def rounded(value):
    return value.astype(BF16).astype(F32)


def norm_parts(volume):
    centre = volume - jnp.mean(volume, -1, keepdims=True)
    spread = jnp.mean(centre * centre, -1, keepdims=True)
    scale = lax.rsqrt(spread + EPS)
    return (centre * scale, scale)


def norm_back(hat, scale, grad, gain):
    inner = grad * gain
    return scale * (
        inner
        - jnp.mean(inner, -1, keepdims=True)
        - hat * jnp.mean(inner * hat, -1, keepdims=True)
    )


def column_sum(value):
    return jnp.sum(value, 0, keepdims=True)


def attend(queries, keys, values, rows, mask, bias):
    spread_out, back = rows
    packed = dot(spread_out, queries) * mask
    scores = dot_nt(packed, keys) * HEAD ** (-0.5) + bias
    weights = jnp.exp(scores - jnp.max(scores, -1, keepdims=True))
    probs = weights / jnp.sum(weights, -1, keepdims=True)
    mixture = dot(probs, values) * mask
    return (probs, dot(back, mixture))


def attend_back(queries, keys, values, rows, mask, probs, mixture_grad, toep, block):
    factor = HEAD ** (-0.5)
    spread_out, back = rows
    packed = dot(spread_out, queries) * mask
    grad = dot(spread_out, mixture_grad) * mask
    value_grad = dot_tn(probs, grad)
    prob_grad = dot_nt(grad, values)
    score_grad = probs * (prob_grad - jnp.sum(prob_grad * probs, -1, keepdims=True))
    query_grad = dot(back, dot(score_grad, keys) * factor * mask)
    key_grad = dot_tn(score_grad, packed) * factor
    table = None
    for oq, select in enumerate(toep):
        part = dot_nt(score_grad[oq * block : (oq + 1) * block], select)
        table = part if table is None else table + part
    return (query_grad, key_grad, value_grad, table)


def lasting(micros):
    return pl.CostEstimate(flops=int(micros * 2.0e9), bytes_accessed=int(micros * 3.69e6), transcendentals=int(micros * 1e6))


def call(body, outs, args, scratch, name, micros, in_place=(), limit=VMEM_BYTES):
    vmem = pl.BlockSpec(memory_space=pltpu.VMEM)
    away = pl.BlockSpec(memory_space=pltpu.HBM)
    return pl.pallas_call(
        body,
        out_shape=tuple(jax.ShapeDtypeStruct(shape, dtype) for shape, dtype in outs),
        in_specs=[away if at in in_place else vmem for at in range(len(args))],
        out_specs=(vmem,) * len(outs),
        scratch_shapes=list(scratch),
        compiler_params=pltpu.CompilerParams(vmem_limit_bytes=limit),
        cost_estimate=lasting(micros),
        name=name,
    )(*args)


def vector(ref):
    return ref[...].reshape(1, -1)


def query_half():
    return 1 - lax.rem(lax.axis_index("lon"), 2)


def packed_side(value):
    tail = jnp.concatenate([value[0:40, 128:192], value[40:80, 128:192]], 1)
    return jnp.concatenate([value[:, 0:128], tail, jnp.zeros((8, 128), value.dtype)], 0)


def unpacked_side(block):
    tail = jnp.concatenate([block[80:120, 0:64], block[80:120, 64:128]], 0)
    return jnp.concatenate([block[0:80, :], tail], 1)


def lane_blocks(pieces):
    blocks = []
    for a, b in zip(pieces[::2], pieces[1::2]):
        blocks += [a[:, 0:128], jnp.concatenate([a[:, 128:192], b[:, 0:64]], 1), b[:, 64:192]]
    return blocks


def partner_of(lon, count):
    odd = lax.rem(lon, 2)
    return lax.rem(lon + 2 * odd - 1 + count, count)


def ring_positions():
    lat_count, lon_count = (lax.axis_size("lat"), lax.axis_size("lon"))
    lat, lon = (lax.axis_index("lat"), lax.axis_index("lon"))
    up = lax.rem(lat + 1, lat_count)
    down = lax.rem(lat + lat_count - 1, lat_count)
    return (lat, lon, up, down, partner_of(lon, lon_count))


def greet(peers):
    barrier = pltpu.get_barrier_semaphore()
    for peer in peers:
        pl.semaphore_signal(barrier, inc=1, device_id=peer, device_id_type=MESH)


def await_greetings(peers):
    pl.semaphore_wait(pltpu.get_barrier_semaphore(), len(peers))


def meet(peers):
    greet(peers)
    await_greetings(peers)


def start_copy(src, dst, send_sem, recv_sem, peer):
    copy = pltpu.make_async_remote_copy(
        src_ref=src,
        dst_ref=dst,
        send_sem=send_sem,
        recv_sem=recv_sem,
        device_id=peer,
        device_id_type=MESH,
    )
    copy.start()
    return copy


def exchange(sends, send_sems, recv_sems):
    copies = []
    for at, (src, dst, peer) in enumerate(sends):
        copies.append(start_copy(src, dst, send_sems.at[at], recv_sems.at[at], peer))
    for copy in copies:
        copy.wait_recv()
    for copy in copies:
        copy.wait_send()


def remote_call(body, outs, args, scratch, collective_id, name, micros):
    vmem = pl.BlockSpec(memory_space=pltpu.VMEM)
    return pl.pallas_call(
        body,
        out_shape=tuple(jax.ShapeDtypeStruct(shape, dtype) for shape, dtype in outs),
        in_specs=[vmem] * len(args),
        out_specs=(vmem,) * len(outs),
        scratch_shapes=scratch,
        compiler_params=pltpu.CompilerParams(
            collective_id=collective_id, has_side_effects=True, vmem_limit_bytes=VMEM_BYTES
        ),
        cost_estimate=lasting(micros),
        name=name,
    )(*args)


def semaphores(*counts):
    return [pltpu.SemaphoreType.DMA((count,)) for count in counts for _ in range(2)]


def halo_body(cells_ref, tf_ref, tc_ref, x_out, *refs):
    outs, biases, bufs = (refs[:5], refs[5:9], refs[9:15])
    x_ref, low_ref, high_ref, tab_ref, stage, ss, rs, ts, tr = refs[15:]
    par, upo, upp, dno, dnp, tab = bufs
    lat, lon, up, down, partner = ring_positions()
    size = tab.shape[0]
    rank = lax.rem(lon, size)
    others = [lax.rem(rank + d, size) for d in range(1, size)]
    near = [(lat, lon - rank + other) for other in others]
    beside = (lat, partner)
    peers = [(up, lon), (down, lon), beside] + near
    greet(peers)
    prepare_body(cells_ref, tf_ref, x_ref, low_ref, high_ref, tab_ref, stage)
    x_out[...] = x_ref[...]
    await_greetings(peers)
    low_copy = start_copy(low_ref, upo, ss.at[1], rs.at[1], (down, lon))
    high_copy = start_copy(high_ref, dno, ss.at[2], rs.at[2], (up, lon))
    table_copy = start_copy(tab_ref.at[rank], tab.at[rank], ss.at[3], rs.at[3], (up, lon))
    x_copy = start_copy(x_ref, par, ss.at[0], rs.at[0], beside)
    copies = [x_copy, low_copy, high_copy, table_copy]
    kinds = fine_kinds()
    store_bias("a", spread("a", tf_ref[0:288, :]), kinds["a"], biases[0])
    store_bias("b", spread("b", tf_ref[288:576, :]), kinds["b"], biases[1])
    store_bias("q", spread("q", tc_ref[...]), coarse_kind(), biases[3])
    low_copy.wait_recv()
    relays = [start_copy(upo, upp, ss.at[4], rs.at[4], beside)]
    high_copy.wait_recv()
    relays.append(start_copy(dno, dnp, ss.at[5], rs.at[5], beside))
    table_copy.wait_recv()
    for d, peer in enumerate(near):
        relays.append(start_copy(tab.at[rank], tab.at[rank], ts.at[d], tr.at[d], peer))
    x_copy.wait_recv()
    for copy in relays:
        copy.wait_recv()
    table = jnp.concatenate([tab[place].astype(F32) for place in range(size)], 0)
    table = jnp.concatenate([table[c * 80 : (c + 1) * 80] for c in range(3)], 1)
    store_bias("c", table, kinds["c"], biases[2])
    for copy in copies + relays:
        copy.wait_send()
    for out, buf in zip(outs, bufs):
        out[...] = buf[...]


def group_peers():
    lat, lon = (lax.axis_index("lat"), lax.axis_index("lon"))
    place = lax.rem(lon, 4)
    others = [lax.rem(place + d, 4) for d in range(1, 4)]
    return (place, others, [(lat, lon - place + other) for other in others])


def forward_gather_body(*refs):
    inner, (out_ref, buf, ss, rs) = (refs[:-4], refs[-4:])
    place, _, peers = group_peers()
    greet(peers)
    fine_forward_body(*inner)
    buf[place] = inner[-1][...]
    await_greetings(peers)
    exchange([(buf.at[place], buf.at[place], peer) for peer in peers], ss, rs)
    out_ref[...] = buf[...]


def coarse_scatter_body(*refs):
    inputs, (out_ref, norm_out, own_out, flat_out, table_out, cot_out) = (refs[:9], refs[9:15])
    stage, keys, values, parts, buf, ss, rs = refs[15:]
    place, others, peers = group_peers()
    greet(peers)
    coarse_body(
        *inputs, out_ref, parts, own_out, flat_out, table_out, cot_out, stage, keys, values
    )
    await_greetings(peers)
    exchange([(parts.at[other], buf.at[d], peers[d]) for d, other in enumerate(others)], ss, rs)
    total = parts[place].astype(F32)
    for d in range(3):
        total = total + buf[d].astype(F32)
    norm_out[...] = total


def spread(kind, table):
    total = None
    for zk in range(2):
        part = dot(dot(table_rows(kind, zk), table), table_lanes(zk))
        total = part if total is None else total + part
    return total


def bias_rows(table, toep, zone, block):
    rows = table[zone * block : (zone + 1) * block]
    return jnp.concatenate([dot(rows, select) for select in toep], 0)


def banned(keys, zq, zone):
    ban = jnp.where(keys[3], 0.0, NEGATIVE)
    if zone == 1:
        ban = ban + jnp.where(zq == keys[0], 0.0, NEGATIVE)
    return ban


def fetch_groups(stage, ref):
    rows, cols = ref.shape[:2]
    for row in range(rows):
        for col in range(cols):
            at = (row * cols + col) * 4
            stage[at : at + 4, :] = ref[row, col].astype(F32)


def store_groups(ref, stage):
    rows, cols = ref.shape[:2]
    for row in range(rows):
        for col in range(cols):
            at = (row * cols + col) * 4
            ref[row, col] = stage[at : at + 4, :].astype(BF16)


def prepare_body(x_ref, tf_ref, own_out, low_out, high_out, tab_out, stage):
    fetch_groups(stage, x_ref)
    tokens = dot(fine_order(), stage[...])
    own_out[...] = tokens.astype(BF16)
    low_out[...] = packed_side(tokens[LOW : LOW + SIDE]).astype(BF16)
    high_out[...] = packed_side(tokens[TOP : TOP + SIDE]).astype(BF16)
    table = spread("c", tf_ref[288:576, :])
    pieces = [table[:, c * 128 : (c + 1) * 128] for c in range(3)]
    block = jnp.concatenate(pieces + [jnp.zeros((16, 128), F32)], 0).astype(BF16)
    size = tab_out.shape[1]
    for place in range(tab_out.shape[0]):
        tab_out[place] = block[place * size : (place + 1) * size, :]


def fine_kinds():
    half = query_half().astype(F32)
    rows_a, mask_a, zq_a = head_rows(HEADS_F, 6, 6, 72, 72)
    rows_b, mask_b, zq_b = head_rows(HEADS_F, 3, 6, 40, 40)
    keys_a, keys_b = (pair_keys(144, half), pair_keys(160, half))
    toep_a, toep_b = (toeplitz(keys_a, 6, 6 * half), toeplitz(keys_b, 6, 6 * half))
    mid = (rows_a, mask_a, zq_a, keys_a, toep_a, 72)
    edge = (rows_b, mask_b, zq_b, keys_b, toep_b, 40)
    return {"a": mid, "b": edge, "c": edge}


def store_bias(name, table, kind, out):
    _, _, zq, keys, toep, block = kind
    lat = lax.axis_index("lat")
    late = along_lanes(160) >= 80
    edge = {
        "a": 0.0,
        "b": jnp.where(late & (lat == lax.axis_size("lat") - 1), NEGATIVE, 0.0),
        "c": jnp.where(jnp.logical_not(late) & (lat == 0), NEGATIVE, 0.0),
        "q": 0.0,
    }[name]
    for zone in range(2):
        terms = bias_rows(table, toep, zone, block)
        out[zone] = terms + banned(keys, zq, 0 if name == "q" else zone) + edge


def coarse_kind():
    rows, mask, zq = head_rows(HEADS_C, 6, 3, 40, 144)
    keys = group_keys()
    toep = toeplitz(keys, 3, 3 * lax.rem(lax.axis_index("lon"), 4).astype(F32))
    return (rows, mask, zq, keys, toep, 144)


def fine_windows(zone):
    edge = zone * 40
    return (
        ("a", (MID + zone * 72, 72), [(0, MID + zone * 72, 72), (1, MID + zone * 72, 72)]),
        ("b", (TOP + edge, 40), [(0, TOP + edge, 40), (1, TOP + edge, 40), (2, edge, 40), (3, edge, 40)]),
        ("c", (LOW + edge, 40), [(4, edge, 40), (5, edge, 40), (0, LOW + edge, 40), (1, LOW + edge, 40)]),
    )


SOURCES = (0, FINE, 2 * FINE, 2 * FINE + SIDE, 2 * FINE + 2 * SIDE, 2 * FINE + 3 * SIDE)
ALL_ROWS = 2 * FINE + 4 * SIDE


def gathered(ref, pieces):
    return jnp.concatenate(
        [ref[SOURCES[source] + start : SOURCES[source] + start + count, :] for source, start, count in pieces],
        0,
    )


def fine_forward_body(
    own_ref,
    par_ref,
    upo_ref,
    upp_ref,
    dno_ref,
    dnp_ref,
    gain_ref,
    shift_ref,
    qkv_ref,
    qkv_bias_ref,
    proj_ref,
    proj_bias_ref,
    merge_gain_ref,
    merge_shift_ref,
    merge_ref,
    coarse_gain_ref,
    coarse_shift_ref,
    bias_a,
    bias_b,
    bias_c,
    hat_out,
    normed,
    q_out,
    k_out,
    v_out,
    probs_a,
    probs_b,
    probs_c,
    mix_out,
    fine_out,
    merged_out,
    coarse_out,
    cnorm_out,
):
    gain, shift = (vector(gain_ref), vector(shift_ref))
    own = own_ref[...].astype(F32)
    for place, tokens in enumerate(
        [own, par_ref[...].astype(F32)]
        + [unpacked_side(ref[...].astype(F32)) for ref in (upo_ref, upp_ref, dno_ref, dnp_ref)]
    ):
        hat, _ = norm_parts(tokens)
        at = slice(SOURCES[place], SOURCES[place] + tokens.shape[0])
        hat_out[at, :] = hat
        normed[at, :] = (hat * gain + shift).astype(BF16)
    bias = vector(qkv_bias_ref)
    q_out[...] = rounded(dot(normed[0:FINE, :], qkv_ref[:, 0:C_F]) + bias[:, 0:C_F])
    k_out[...] = rounded(dot(normed[...], qkv_ref[:, C_F : 2 * C_F]) + bias[:, C_F : 2 * C_F])
    v_out[...] = rounded(dot(normed[...], qkv_ref[:, 2 * C_F :]) + bias[:, 2 * C_F :])
    kinds = fine_kinds()
    probs_refs = {"a": (bias_a, probs_a), "b": (bias_b, probs_b), "c": (bias_c, probs_c)}
    mixtures = {}
    for zone in range(2):
        for name, (start, count), pieces in fine_windows(zone):
            rows, mask = kinds[name][:2]
            bias_ref, probs_ref = probs_refs[name]
            probs, mixture = attend(
                q_out[start : start + count, :],
                gathered(k_out, pieces),
                gathered(v_out, pieces),
                rows,
                mask,
                bias_ref[zone],
            )
            probs_ref[zone] = probs
            mixtures[name, zone] = mixture
    mixture = jnp.concatenate([mixtures[name, zone] for name in "cab" for zone in range(2)], 0)
    mix_out[...] = mixture.astype(BF16)
    attn = rounded(dot(mixture, proj_ref[...]) + vector(proj_bias_ref))
    fine = rounded(own + attn)
    fine_out[...] = fine.astype(BF16)
    quartet = dot(quartet_order(), fine)
    parts = [quartet[p * COARSE : (p + 1) * COARSE] for p in range(4)]
    hats, _ = quartet_norm(parts)
    coarse = None
    gain, shift = (vector(merge_gain_ref), vector(merge_shift_ref))
    for p in range(4):
        at = slice(p * C_F, (p + 1) * C_F)
        value = (hats[p] * gain[:, at] + shift[:, at]).astype(BF16)
        merged_out[p] = value
        part = dot(value, merge_ref[p * C_F : (p + 1) * C_F, :])
        coarse = part if coarse is None else coarse + part
    coarse = rounded(coarse)
    coarse_out[...] = coarse
    hat, _ = norm_parts(coarse)
    cnorm_out[...] = (hat * vector(coarse_gain_ref) + vector(coarse_shift_ref)).astype(BF16)


def quartet_norm(parts):
    width = 4.0 * C_F
    mean = sum(jnp.sum(part, -1, keepdims=True) for part in parts) / width
    centres = [part - mean for part in parts]
    spread = sum(jnp.sum(c * c, -1, keepdims=True) for c in centres) / width
    scale = lax.rsqrt(spread + EPS)
    return ([c * scale for c in centres], scale)


def coarse_body(
    group_ref,
    own_ref,
    coarse_ref,
    cot_ref,
    qkv_ref,
    qkv_bias_ref,
    proj_ref,
    proj_bias_ref,
    bias_ref,
    out_ref,
    parts_out,
    own_out,
    flat_out,
    table_out,
    cot_out,
    stage,
    keys,
    values,
):
    fetch_groups(stage, cot_ref)
    cot = dot(coarse_order(), stage[...])
    cot_out[...] = cot
    bias = vector(qkv_bias_ref)
    wide = [slice(i * C_C, (i + 1) * C_C) for i in range(3)]
    queries = rounded(dot(own_ref[...], qkv_ref[:, wide[0]]) + bias[:, wide[0]])
    group = jnp.concatenate([group_ref[g] for g in range(4)], 0)
    keys[...] = rounded(dot(group, qkv_ref[:, wide[1]]) + bias[:, wide[1]])
    values[...] = rounded(dot(group, qkv_ref[:, wide[2]]) + bias[:, wide[2]])
    mixture_grad = rounded(dot_nt(cot, proj_ref[...]))
    rows, mask, _, _, toep, _ = coarse_kind()
    mixtures, query_grads, grads = ([], [], [])
    for zone in range(2):
        here = slice(zone * 40, (zone + 1) * 40)
        at = [slice(g * COARSE + zone * 40, g * COARSE + zone * 40 + 40) for g in range(4)]
        k = jnp.concatenate([keys[there, :] for there in at], 0)
        v = jnp.concatenate([values[there, :] for there in at], 0)
        probs, mixture = attend(queries[here], k, v, rows, mask, bias_ref[zone])
        dq, dk, dv, table = attend_back(
            queries[here], k, v, rows, mask, probs, mixture_grad[here], toep, 144
        )
        table_out[zone * 144 : (zone + 1) * 144, :] = table
        mixtures.append(mixture)
        query_grads.append(dq)
        grads.append((dk, dv))
    key_grad, value_grad = (
        rounded(
            jnp.concatenate(
                [grads[zone][i][g * 40 : (g + 1) * 40] for g in range(4) for zone in range(2)], 0
            )
        )
        for i in range(2)
    )
    query_grad = jnp.concatenate(query_grads, 0)
    part = dot_nt(key_grad, qkv_ref[:, wide[1]]) + dot_nt(value_grad, qkv_ref[:, wide[2]])
    for g in range(4):
        parts_out[g] = part[g * COARSE : (g + 1) * COARSE].astype(BF16)
    own_out[...] = dot_nt(query_grad, qkv_ref[:, wide[0]])
    for i, (norm, grad) in enumerate(
        ((own_ref[...], query_grad), (group, key_grad), (group, value_grad))
    ):
        weight = dot_tn(norm, grad)
        sums = column_sum(grad)
        for c in range(3):
            lanes = slice(c * 128, (c + 1) * 128)
            flat_out[pl.ds(3 * i + c, C_C, stride=9), :] = weight[:, lanes]
            flat_out[3456 + 3 * i + c : 3457 + 3 * i + c, :] = sums[:, lanes]
    mixture = jnp.concatenate(mixtures, 0)
    flat_store(flat_out, 3465, dot_tn(mixture, cot))
    flat_store(flat_out, 4617, column_sum(cot))
    attn = rounded(dot(mixture, proj_ref[...]) + vector(proj_bias_ref))
    stage[...] = dot(coarse_order(True), coarse_ref[...] + attn)
    store_groups(out_ref, stage)


def flat_store(flat, start, matrix):
    height, width = matrix.shape
    step = width // 128
    for c in range(step):
        lanes = slice(c * 128, (c + 1) * 128)
        if height == 1:
            flat[start + c : start + c + 1, :] = matrix[:, lanes]
        else:
            flat[pl.ds(start + c, height, stride=step), :] = matrix[:, lanes]


def keep_square(square, matrix):
    height = matrix.shape[0]
    square[0, 0:height, :] = matrix[:, 0:128]
    square[1, 0:height, 0:64] = matrix[:, 128:192]


def every_other(square, start):
    take = pl.ds(start, 96, stride=2)
    return jnp.concatenate([square[0, take, :], square[1, take, :][:, 0:64]], 1)


def block_store(flat, start, blocks):
    for c, block in enumerate(blocks):
        if block.shape[0] == 1:
            flat[start + c : start + c + 1, :] = block
        else:
            flat[pl.ds(start + c, block.shape[0], stride=len(blocks)), :] = block


def fine_back_body(
    starts,
    rows,
    part_ref,
    own_part_ref,
    cot_ref,
    coarse_ref,
    merged_ref,
    fine_ref,
    hat_ref,
    normed_ref,
    mix_ref,
    q_ref,
    k_ref,
    v_ref,
    probs_a,
    probs_b,
    probs_c,
    qkv_ref,
    cgain_ref,
    merge_gain_ref,
    merge_ref,
    proj_ref,
    flat_c,
    table_q,
    fog_out,
    own_out,
    par_out,
    upo_out,
    upp_out,
    dno_out,
    dnp_out,
    pieces_out,
    tables_out,
    kgrad,
    vgrad,
    flat,
    tables,
    square,
):
    norm_grad = part_ref[...] + own_part_ref[...]
    hat, scale = norm_parts(coarse_ref[...])
    flat_store(flat, 3477, column_sum(norm_grad * hat))
    flat_store(flat, 3480, column_sum(norm_grad))
    coarse_grad = rounded(cot_ref[...] + norm_back(hat, scale, norm_grad, vector(cgain_ref)))
    quartet = dot(quartet_order(), fine_ref[...])
    hats, scale = quartet_norm([quartet[p * COARSE : (p + 1) * COARSE] for p in range(4)])
    inners, gains, shifts = ([], [], [])
    merge_gain = vector(merge_gain_ref)
    for p in range(4):
        at = slice(p * C_F, (p + 1) * C_F)
        flat_store(flat, 1173 + 3 * p * C_F, dot_tn(merged_ref[p], coarse_grad))
        grad = dot_nt(coarse_grad, merge_ref[at, :])
        gains.append(column_sum(grad * hats[p]))
        shifts.append(column_sum(grad))
        inners.append(grad * merge_gain[:, at])
    block_store(flat, 1161, lane_blocks(gains))
    block_store(flat, 1167, lane_blocks(shifts))
    width = 4.0 * C_F
    first = sum(jnp.sum(inner, -1, keepdims=True) for inner in inners) / width
    second = sum(jnp.sum(i * h, -1, keepdims=True) for i, h in zip(inners, hats)) / width
    grads = jnp.concatenate([scale * (i - first - h * second) for i, h in zip(inners, hats)], 0)
    high = rounded(grads)
    unmerge = quartet_order(True)
    attn_grad = dot(unmerge, high)
    fog_out[...] = attn_grad + dot(unmerge, grads - high)
    mixture_grad = rounded(dot_nt(attn_grad, proj_ref[...]))
    weight = dot_tn(mix_ref[...], attn_grad)
    corner = weight[0:1]
    keep_square(square, jnp.concatenate([weight, column_sum(attn_grad)], 0))
    block_store(flat, 873, lane_blocks([every_other(square, 1), every_other(square, 2)]))
    kinds = fine_kinds()
    places = {"a": (PART_A, probs_a), "b": (PART_B, probs_b), "c": (PART_C, probs_c)}
    query_grads = {}
    for zone in range(2):
        for name, (start, count), pieces in fine_windows(zone):
            rows_at, mask, _, _, toep, block = kinds[name]
            table_at, probs_ref = places[name]
            dq, dk, dv, table = attend_back(
                q_ref[start : start + count, :],
                gathered(k_ref, pieces),
                gathered(v_ref, pieces),
                rows_at,
                mask,
                probs_ref[zone],
                mixture_grad[start : start + count],
                toep,
                block,
            )
            query_grads[name, zone] = dq
            for c in range(3):
                at = table_at + (2 * c + zone) * block
                tables[at : at + block, :] = table[:, c * 128 : (c + 1) * 128]
            at = 0
            for source, begin, size in pieces:
                to = slice(SOURCES[source] + begin, SOURCES[source] + begin + size)
                kgrad[to, :] = rounded(dk[at : at + size])
                vgrad[to, :] = rounded(dv[at : at + size])
                at += size
    query_grad = jnp.concatenate([query_grads[name, zone] for name in "cab" for zone in range(2)], 0)
    part = dot_nt(kgrad[...], qkv_ref[:, C_F : 2 * C_F]) + dot_nt(vgrad[...], qkv_ref[:, 2 * C_F :])
    own = part[0:FINE] + dot_nt(query_grad, qkv_ref[:, 0:C_F])
    own_out[...] = own
    par_out[...] = part[FINE : 2 * FINE].astype(BF16)
    for place, out in enumerate((upo_out, upp_out, dno_out, dnp_out)):
        at = SOURCES[2 + place]
        out[...] = packed_side(part[at : at + SIDE]).astype(BF16)
    hat_grad = column_sum(own * hat_ref[0:FINE, :])
    hat_grad += column_sum(part[FINE:] * hat_ref[FINE:, :])
    block_store(
        flat, 0, lane_blocks([hat_grad, column_sum(own) + column_sum(part[FINE:])])
    )
    evens, odds, sums = ([], [], [])
    for norm, grad in (
        (normed_ref[0:FINE, :], query_grad),
        (normed_ref[...], kgrad[...]),
        (normed_ref[...], vgrad[...]),
    ):
        keep_square(square, dot_tn(norm, grad))
        evens.append(every_other(square, 0))
        odds.append(every_other(square, 1))
        sums.append(column_sum(grad))
    block_store(flat, 3, lane_blocks(evens + odds))
    block_store(flat, 867, lane_blocks(sums + [corner]))
    tables[240:PART_A, :] = jnp.zeros((PART_A - 240, 128), F32)
    tables[PART_END:, :] = jnp.zeros((TABLE_ROWS - PART_END, 128), F32)
    for c in range(3):
        at = PART_Q + 288 * c
        tables[at : at + 288, :] = table_q[:, c * 128 : (c + 1) * 128]
    split = 3483
    trows = TABLE_ROWS // len(starts)
    for place, start in starts:
        end = start + rows
        if start < split:
            size = min(end, split) - start
            value = flat[start : start + size, :]
            if end > split:
                value = jnp.concatenate([value, flat_c[0 : end - split, :]], 0)
        else:
            size = min(end, 8103) - start
            value = flat_c[start - split : start - split + size, :]
            if size < rows:
                value = jnp.concatenate([value, jnp.zeros((rows - size, 128), F32)], 0)
        chunk = pieces_out.shape[2]
        for y in range(pieces_out.shape[0]):
            pieces_out[y, place] = value[y * chunk : (y + 1) * chunk].astype(BF16)
        tables_out[place] = tables[place * trows : (place + 1) * trows, :].astype(BF16)


def final_body(
    x_ref,
    gain_ref,
    fog_ref,
    own_ref,
    par_ref,
    low_ref,
    high_ref,
    t_ref,
    token_out,
    fine_out,
    coarse_out,
    stage,
    grad,
):
    grad[...] = own_ref[...] + par_ref[...].astype(F32)
    grad[LOW : LOW + SIDE, :] += unpacked_side(low_ref[...].astype(F32))
    grad[TOP : TOP + SIDE, :] += unpacked_side(high_ref[...].astype(F32))
    hat, scale = norm_parts(x_ref[...].astype(F32))
    total = fog_ref[...] + norm_back(hat, scale, rounded(grad[...]), vector(gain_ref))
    stage[...] = dot(fine_order(True), total)
    store_groups(token_out, stage)

    def part(start, height):
        return jnp.concatenate(
            [t_ref[start + c * height : start + (c + 1) * height, :] for c in range(3)], 1
        )

    def natural(kind, block):
        total = None
        for zk in range(2):
            term = dot(table_rows(kind, zk, True), dot_nt(block, table_lanes(zk)))
            total = term if total is None else total + term
        return total

    fine_out[0:288, :] = natural("a", part(PART_A, 144))
    fine_out[288:576, :] = natural("b", part(PART_B, 80)) + natural("c", part(PART_C, 80))
    coarse_out[...] = natural("q", part(PART_Q, 288))


def mesh_parts(lat, lon):
    cores = 2
    xs = 4 if lon % 8 == 0 else 1
    ys = 4 if lat % 4 == 0 else lat
    return (cores, xs, lon // (cores * xs), ys, lat // ys)


def piece_rows(total, lon, ys):
    longest = -(-(127 + total // lon) // 128)
    unit = 16 * ys
    return -(-longest // unit) * unit


def reduce_body(
    dims,
    norm_factor,
    compute,
    g_ref,
    gt_ref,
    par_ref,
    upo_ref,
    upp_ref,
    dno_ref,
    dnp_ref,
    p_ref,
    t_ref,
    par_out,
    low_out,
    high_out,
    par_buf,
    up_buf,
    down_buf,
    up_sum,
    down_sum,
    low_buf,
    high_buf,
    core_buf,
    head_buf,
    tail_buf,
    y_buf,
    y_sum,
    x_buf,
    x_sum,
    z_buf,
    h_send,
    h_buf,
    share,
    tab_core,
    tab_x,
    tab_sum,
    tab_own,
    tab_hand,
    tab_z,
    tab_all,
    send_sems,
    recv_sems,
):
    cores, xs, zs, ys, hs = dims
    half = xs * zs
    chunk = g_ref.shape[2]
    trows = gt_ref.shape[1]
    lat, lon = (lax.axis_index("lat"), lax.axis_index("lon"))
    core = lax.rem(lon, cores)
    x = lax.rem(lon // cores, xs)
    z = lon // (cores * xs)
    y = lax.rem(lat, ys)
    h = lat // ys
    lats = ys * hs

    def at(here, d, count):
        return lax.rem(here + d, count)

    def lon_of(core_to, x_to, z_to):
        return (z_to * xs + x_to) * cores + core_to

    other_core = (lat, lon_of(1 - core, x, z))
    x_peers = {d: (lat, lon_of(core, at(x, d, xs), z)) for d in range(1, xs)}
    y_peers = {d: (h * ys + at(y, d, ys), lon) for d in range(1, ys)}
    z_peers = {d: (lat, lon_of(core, x, at(z, d, zs))) for d in range(1, zs)}
    far = (at(h, 1, hs) * ys + y, lon)
    before, after = ((at(lat, lats - 1, lats), lon), (at(lat, 1, lats), lon))
    beside = (lat, partner_of(lon, cores * half))
    peers = [before, after] + ([far] if hs > 1 else [])
    peers += list(z_peers.values())[::-1] + list(y_peers.values()) + list(x_peers.values())
    peers += [beside, other_core]
    greet(peers)
    compute()
    await_greetings(peers)
    pending = []

    def send(src, dst, peer):
        sem = len(pending)
        copy = start_copy(src, dst, send_sems.at[sem], recv_sems.at[sem], peer)
        pending.append(copy)
        return copy

    def arrived(copies):
        for copy in copies:
            copy.wait_recv()

    def add_into(target, terms, count):
        def step(i, carry):
            total = terms[0](i).astype(F32)
            for term in terms[1:]:
                total = total + term(i).astype(F32)
            target[i] = total.astype(BF16)
            return carry

        lax.fori_loop(0, count, step, 0)

    away = pl.ds((1 - core) * half, half)
    mine = core * half
    table_core = send(gt_ref.at[away], tab_core, other_core)
    edges = [
        send(upp_ref, up_buf, beside),
        send(dnp_ref, down_buf, beside),
        send(par_ref, par_buf, beside),
    ]
    order = {4: (2, 1, 3, 0), 2: (1, 0), 1: (0,)}[ys]
    crossing = {d: send(g_ref.at[at(y, d, ys), away], core_buf.at[d], other_core) for d in order}
    table_core.wait_recv()
    add_into(tab_core, [lambda i: tab_core[i], lambda i: gt_ref[mine + i]], half)
    table_x = [
        send(tab_core.at[pl.ds(at(x, d, xs) * zs, zs)], tab_x.at[d - 1], x_peers[d])
        for d in range(1, xs)
    ]
    cut = half // 2
    head, tail = (pl.ds(0, cut), pl.ds(cut, half - cut))
    gathered_y = []
    for d in order:
        crossing[d].wait_recv()
        row = at(y, d, ys)
        buf = core_buf.at[d]
        add_into(buf, [lambda i: buf[i], lambda i: g_ref[row, mine + i]], half)
        if ys == 4 and d == 2:
            over_right = send(core_buf.at[2, head], head_buf, y_peers[1])
            over_left = send(core_buf.at[2, tail], tail_buf, y_peers[3])
        if ys == 4 and d == 1:
            gathered_y.append(send(core_buf.at[1, tail], y_buf.at[0, tail], y_peers[1]))
        if ys == 4 and d == 3:
            gathered_y.append(send(core_buf.at[3, head], y_buf.at[1, head], y_peers[3]))
        if ys == 2 and d == 1:
            gathered_y.append(send(core_buf.at[1], y_buf.at[0], y_peers[1]))
    if ys == 4:
        over_right.wait_recv()
        right = core_buf.at[1]
        add_into(right, [lambda i: right[i], lambda i: head_buf[i]], cut)
        gathered_y.append(send(core_buf.at[1, head], y_buf.at[0, head], y_peers[1]))
        over_left.wait_recv()
        left = core_buf.at[3, tail]
        add_into(left, [lambda i: left[i], lambda i: tail_buf[i]], half - cut)
        gathered_y.append(send(core_buf.at[3, tail], y_buf.at[1, tail], y_peers[3]))

    arrived(edges[:2])
    up_sum[...] = (upo_ref[...].astype(F32) + up_buf[...].astype(F32)).astype(BF16)
    down_sum[...] = (dno_ref[...].astype(F32) + down_buf[...].astype(F32)).astype(BF16)
    edges.append(send(up_sum, low_buf, after))
    edges.append(send(down_sum, high_buf, before))
    arrived(table_x)
    base = x * zs
    terms = [lambda i: tab_core[base + i]]
    terms += [lambda i, d=d: tab_x[d - 1, i] for d in range(1, xs)]
    add_into(tab_sum, terms, zs)
    table_z = [
        send(tab_sum.at[at(z, d, zs)], tab_z.at[d - 1], z_peers[d]) for d in range(1, zs)
    ]

    arrived(gathered_y)
    terms = [lambda i: core_buf[0, i]]
    terms += [lambda i, d=d: y_buf[d, i] for d in range({4: 2, 2: 1, 1: 0}[ys])]
    add_into(y_sum, terms, half)
    along_x = [
        send(y_sum.at[pl.ds(at(x, d, xs) * zs, zs)], x_buf.at[d - 1], x_peers[d])
        for d in range(1, xs)
    ]

    arrived(table_z)
    total = tab_sum[z].astype(F32)
    for d in range(1, zs):
        total = total + tab_z[d - 1].astype(F32)
    own = tab_all.at[core, x, z]
    tab_own[...] = (total * norm_factor).astype(BF16)
    tab_all[core, x, z] = tab_own[...]
    first_row = ((core * xs + x) * zs + z) * trows

    def prepared(src, dst, peer):
        sem = len(pending)
        copy = pltpu.make_async_remote_copy(
            src_ref=src,
            dst_ref=dst,
            send_sem=send_sems.at[sem],
            recv_sem=recv_sems.at[sem],
            device_id=peer,
            device_id_type=MESH,
        )
        pending.append(copy)
        return copy

    handed = prepared(tab_own, tab_hand, before)
    pending.pop()
    pending.append(None)
    back_z = [prepared(own, own, z_peers[d]) for d in range(1, zs)]

    @pl.when(first_row < PART_A)
    def _():
        handed.start()

    @pl.when(first_row >= PART_A)
    def _():
        for copy in back_z:
            copy.start()

    arrived(along_x)
    terms = [lambda i: y_sum[base + i]]
    terms += [lambda i, d=d: x_buf[d - 1, i] for d in range(1, xs)]
    add_into(x_sum, terms, zs)
    along_z = [send(x_sum.at[at(z, d, zs)], z_buf.at[d - 1], z_peers[d]) for d in range(1, zs)]

    @pl.when(first_row < PART_A)
    def _():
        handed.wait()
        row = first_row + lax.broadcasted_iota(jnp.int32, (trows, 128), 0)
        tab_all[core, x, z] = jnp.where(
            row < PART_A, tab_hand[...].astype(F32), tab_own[...].astype(F32)
        ).astype(BF16)
        for copy in back_z:
            copy.start()

    arrived(along_z)
    total = x_sum[z].astype(F32)
    for d in range(1, zs):
        total = total + z_buf[d - 1].astype(F32)
    if hs > 1:
        h_send[...] = total.astype(BF16)
        across = send(h_send, h_buf, far)
    arrived(back_z)
    own = tab_all.at[core, x]
    back_x = [send(own, own, x_peers[d]) for d in range(1, xs)]
    if hs > 1:
        across.wait_recv()
        total = h_send[...].astype(F32) + h_buf[...].astype(F32)
    rows = pl.ds(pl.multiple_of(y * chunk, 8), chunk)
    share[rows, :] = total * norm_factor
    back_y = [send(share.at[rows], share.at[rows], y_peers[d]) for d in range(1, ys)]
    arrived(back_x)
    own = tab_all.at[core]
    back_core = send(own, own, other_core)
    arrived(edges[2:])
    par_out[...] = par_buf[...]
    low_out[...] = low_buf[...]
    high_out[...] = high_buf[...]
    arrived(back_y)
    p_ref[...] = share[...]
    back_core.wait_recv()
    t_ref[...] = tab_all[...]
    for copy in pending:
        if copy is not None:
            copy.wait_send()


def backward_reduce_body(dims, norm_factor, starts, rows, count, *refs):
    inputs, refs = (refs[:count], refs[count:])
    fog_out, own_out, *outs = refs[:7]
    refs = refs[7:]
    inner, refs = (refs[:5], refs[5:])
    edges, pieces, tables = (refs[:5], refs[5], refs[6])

    def compute():
        fine_back_body(
            starts, rows, *inputs, fog_out, own_out, *edges, pieces, tables, *inner
        )

    reduce_body(dims, norm_factor, compute, pieces, tables, *edges, *outs, *refs[7:])


def backward_reduce(args, starts, rows, trows, norm_factor, dims):
    cores, xs, zs, ys, hs = dims
    half = xs * zs
    chunk = rows // ys
    sem = pltpu.SemaphoreType.DMA((64,))
    side = (128, 128)
    all_tables = (cores, xs, zs, trows, 128)
    outs = [((FINE, C_F), F32), ((FINE, C_F), F32)]
    outs += [((ys * chunk, 128), F32), (all_tables, BF16), ((FINE, C_F), BF16)]
    outs += [(side, BF16), (side, BF16)]
    wide = [(ALL_ROWS, C_F), (ALL_ROWS, C_F), (3488, 128), (TABLE_ROWS, 128), (2, 200, 128)]
    buffers = [
        (FINE, C_F),
        *[side] * 4,
        (ys, len(starts), chunk, 128),
        (len(starts), trows, 128),
        (FINE, C_F),
        *[side] * 6,
        (ys, half, chunk, 128),
        (half // 2, chunk, 128),
        (half - half // 2, chunk, 128),
        (2, half, chunk, 128),
        (half, chunk, 128),
        (max(xs - 1, 1), zs, chunk, 128),
        (zs, chunk, 128),
        (max(zs - 1, 1), chunk, 128),
        (chunk, 128),
        (chunk, 128),
        None,
        (half, trows, 128),
        (max(xs - 1, 1), zs, trows, 128),
        (zs, trows, 128),
        (trows, 128),
        (trows, 128),
        (max(zs - 1, 1), trows, 128),
        all_tables,
    ]
    scratch = [pltpu.VMEM(shape, F32) for shape in wide]
    scratch += [
        pltpu.VMEM((ys * chunk, 128), F32) if shape is None else pltpu.VMEM(shape, BF16)
        for shape in buffers
    ]
    body = functools.partial(
        backward_reduce_body, dims, norm_factor, starts, rows, len(args)
    )
    return remote_call(body, outs, args, scratch + [sem, sem], 7, "fine_backward_reduce", 40)


def shards(
    tokens,
    fine_gain,
    fine_shift,
    fine_qkv,
    fine_qkv_bias,
    fine_proj,
    fine_proj_bias,
    fine_table,
    merge_gain,
    merge_shift,
    merge_weight,
    coarse_gain,
    coarse_shift,
    coarse_qkv,
    coarse_qkv_bias,
    coarse_proj,
    coarse_proj_bias,
    coarse_table,
    cotangent,
):
    lat_count, lon_count = (lax.axis_size("lat"), lax.axis_size("lon"))
    lat, lon = (lax.axis_index("lat"), lax.axis_index("lon"))
    norm_factor = 1.0 / math.sqrt(tokens.size // C_F * lat_count * lon_count / 4)
    fine_rows = fine_table.reshape(576, 138)
    coarse_rows = coarse_table.reshape(576, 138)
    cells = tokens[0].transpose(1, 2, 0, 3)
    cot_cells = cotangent[0].transpose(1, 2, 0, 3)

    group = min(8, lon_count)
    side = ((128, 128), BF16)
    own = ((FINE, C_F), BF16)
    table_part = ((group, PART_A // group, 128), BF16)
    halo = [own, side, side, side, side, table_part]
    bias_a, bias_b = (((2, 432, 144), F32), ((2, 240, 160), F32))
    x, par, upo, upp, dno, dnp, bias_a, bias_b, bias_c, bias_q = remote_call(
        halo_body,
        [own] + halo[:5] + [bias_a, bias_b, bias_b, ((2, 432, 160), F32)],
        (cells, fine_rows, coarse_rows),
        [pltpu.VMEM(*s) for s in halo + [own, side, side, table_part, ((288, C_F), F32)]]
        + semaphores(6, max(group - 1, 1)),
        1,
        "halo",
        12,
    )
    (
        hat,
        normed,
        q,
        k,
        v,
        probs_a,
        probs_b,
        probs_c,
        mixture,
        fine_out,
        merged,
        coarse,
        cnorm,
        gathered_norm,
    ) = remote_call(
        forward_gather_body,
        [
            ((ALL_ROWS, C_F), F32),
            ((ALL_ROWS, C_F), BF16),
            ((FINE, C_F), F32),
            ((ALL_ROWS, C_F), F32),
            ((ALL_ROWS, C_F), F32),
            ((2, 432, 144), F32),
            ((2, 240, 160), F32),
            ((2, 240, 160), F32),
            own,
            own,
            ((4, COARSE, C_F), BF16),
            ((COARSE, C_C), F32),
            ((COARSE, C_C), BF16),
            ((4, COARSE, C_C), BF16),
        ],
        (
            x,
            par,
            upo,
            upp,
            dno,
            dnp,
            fine_gain,
            fine_shift,
            fine_qkv,
            fine_qkv_bias,
            fine_proj,
            fine_proj_bias,
            merge_gain,
            merge_shift,
            merge_weight,
            coarse_gain,
            coarse_shift,
            bias_a,
            bias_b,
            bias_c,
        ),
        [pltpu.VMEM((4, COARSE, C_C), BF16)] + semaphores(3),
        2,
        "fine_forward_gather",
        11,
    )
    coarse_out, norm_part, own_part, flat_c, table_q, cot = remote_call(
        coarse_scatter_body,
        [
            ((6, 3, 4, C_C), BF16),
            ((COARSE, C_C), F32),
            ((COARSE, C_C), F32),
            ((4620, 128), F32),
            ((288, 384), F32),
            ((COARSE, C_C), F32),
        ],
        (
            gathered_norm,
            cnorm,
            coarse,
            cot_cells,
            coarse_qkv,
            coarse_qkv_bias,
            coarse_proj,
            coarse_proj_bias,
            bias_q,
        ),
        [
            pltpu.VMEM((72, C_C), F32),
            pltpu.VMEM((4 * COARSE, C_C), F32),
            pltpu.VMEM((4 * COARSE, C_C), F32),
            pltpu.VMEM((4, COARSE, C_C), BF16),
            pltpu.VMEM((3, COARSE, C_C), BF16),
            *semaphores(3),
        ],
        3,
        "coarse_attention_scatter",
        12,
    )
    dims = mesh_parts(lat_count, lon_count)
    cores, xs, zs, ys, hs = dims
    segment = PARAMS // lon_count
    rows = piece_rows(PARAMS, lon_count, ys)
    starts = []
    for index in range(lon_count):
        core, x_at, z_at = (index % cores, index // cores % xs, index // (cores * xs))
        starts.append(((core * xs + x_at) * zs + z_at, index * segment // 128))
    fine_out_grad, own_grad, owned, table_sum, par_back, low_back, high_back = backward_reduce(
        (
            norm_part,
            own_part,
            cot,
            coarse,
            merged,
            fine_out,
            hat,
            normed,
            mixture,
            q,
            k,
            v,
            probs_a,
            probs_b,
            probs_c,
            fine_qkv,
            coarse_gain,
            merge_gain,
            merge_weight,
            fine_proj,
            flat_c,
            table_q,
        ),
        starts,
        rows,
        TABLE_ROWS // lon_count,
        norm_factor,
        dims,
    )
    shift = lax.rem(lon * segment, 128)
    param_grads = lax.dynamic_slice(owned.reshape(-1), (shift,), (segment,))
    token_grad, fine_total, coarse_total = call(
        final_body,
        [((12, 6, 4, C_F), BF16), ((576, 138), F32), ((576, 138), F32)],
        (
            x,
            fine_gain,
            fine_out_grad,
            own_grad,
            par_back,
            low_back,
            high_back,
            table_sum.reshape(TABLE_ROWS, 128),
        ),
        [pltpu.VMEM((288, C_F), F32), pltpu.VMEM((FINE, C_F), F32)],
        "final",
        2,
    )
    return (
        coarse_out.transpose(2, 0, 1, 3)[None],
        token_grad.transpose(2, 0, 1, 3)[None],
        param_grads,
        fine_total.reshape(2, -1),
        coarse_total.reshape(2, -1),
    )


def solution(mesh):
    tiles = P(None, None, "lat", "lon", None)
    whole = P()
    rows = P("lat", None)
    return jax.shard_map(
        shards,
        mesh=mesh,
        in_specs=(tiles,) + (whole,) * 6 + (rows,) + (whole,) * 9 + (rows, tiles),
        out_specs=(tiles, tiles, P("lon"), rows, rows),
        check_vma=False,
    )
```
